32 devices in a mesh: stream: 4 (over y, core), dp: 8 (over z, x).
Axes of the slice: x: 2, y: 2, z: 4, core: 2. Of those that a mesh axis runs over, the one named last changes fastest.
Arguments:
- enc_input: bfloat16 [4096, 1024], P(('stream', 'dp')), may hold values from -6 to 6
- pred_input: bfloat16 [2, 4096, 1024], P(None, ('stream', 'dp')), may hold values from -6 to 6
- cotangent: bfloat16 [3, 4096, 1024], P(None, ('stream', 'dp')), may hold values from -6 to 6
- bucket_len: int32 [8], P('dp'), may hold values from 256 to 512, as said below
- pad_len: int32 [8, 2], P('dp'), may hold values from 0 to 63, as said below
- rel_table: int32 [512], replicated, may hold values from 0 to 31
- enc_qkv: bfloat16 [3, 1024, 1024], P(None, 'dp'), may hold values from -0.1875 to 0.1875
- enc_out: bfloat16 [1024, 1024], P('dp'), may hold values from -3 to 3
- enc_ffn_in: bfloat16 [1024, 4096], P('dp'), may hold values from -0.1875 to 0.1875
- enc_ffn_out: bfloat16 [4096, 1024], P('dp'), may hold values from -0.09375 to 0.09375
- enc_ffn_bias: bfloat16 [4096], P('dp'), may hold values from -3 to 3
- enc_bias: bfloat16 [4, 1024], P(None, 'dp'), may hold values from -2 to 2
- enc_gain: bfloat16 [2, 1024], P(None, 'dp'), may hold values from 0.5 to 1.5
- enc_shift: bfloat16 [2, 1024], P(None, 'dp'), may hold values from -2 to 2
- dec_qkv: bfloat16 [3, 1024, 1024], P(None, 'dp'), may hold values from -0.1875 to 0.1875
- dec_out: bfloat16 [1024, 1024], P('dp'), may hold values from -3 to 3
- dec_rel: bfloat16 [1024, 512], P('dp'), may hold values from -0.1875 to 0.1875
- dec_rel_bias: bfloat16 [512], P('dp'), may hold values from -3 to 3
- dec_ffn_in: bfloat16 [1024, 4096], P('dp'), may hold values from -0.1875 to 0.1875
- dec_ffn_out: bfloat16 [4096, 1024], P('dp'), may hold values from -0.09375 to 0.09375
- dec_ffn_bias: bfloat16 [4096], P('dp'), may hold values from -3 to 3
- dec_bias: bfloat16 [4, 1024], P(None, 'dp'), may hold values from -2 to 2
- dec_gain: bfloat16 [2, 1024], P(None, 'dp'), may hold values from 0.5 to 1.5
- dec_shift: bfloat16 [2, 1024], P(None, 'dp'), may hold values from -2 to 2
Outputs:
- dec_output: float32 [3, 4096, 1024], P(None, ('stream', 'dp'))
- enc_input_grad: float32 [4096, 1024], P(('stream', 'dp'))
- pred_input_grad: float32 [2, 4096, 1024], P(None, ('stream', 'dp'))
- enc_qkv_grad: float32 [3, 1024, 1024], P(None, 'dp')
- enc_out_grad: float32 [1024, 1024], P('dp')
- enc_ffn_in_grad: float32 [1024, 4096], P('dp')
- enc_ffn_out_grad: float32 [4096, 1024], P('dp')
- enc_ffn_bias_grad: float32 [4096], P('dp')
- enc_bias_grad: float32 [4, 1024], P(None, 'dp')
- enc_gain_grad: float32 [2, 1024], P(None, 'dp')
- enc_shift_grad: float32 [2, 1024], P(None, 'dp')
- dec_qkv_grad: float32 [3, 1024, 1024], P(None, 'dp')
- dec_out_grad: float32 [1024, 1024], P('dp')
- dec_rel_grad: float32 [1024, 512], P('dp')
- dec_rel_bias_grad: float32 [512], P('dp')
- dec_ffn_in_grad: float32 [1024, 4096], P('dp')
- dec_ffn_out_grad: float32 [4096, 1024], P('dp')
- dec_ffn_bias_grad: float32 [4096], P('dp')
- dec_bias_grad: float32 [4, 1024], P(None, 'dp')
- dec_gain_grad: float32 [2, 1024], P(None, 'dp')
- dec_shift_grad: float32 [2, 1024], P(None, 'dp')
The draws below stay inside these ranges and needn't reach their ends.
Inputs may be any that keep to these rules, and one draw needn't show every extreme that they name: bucket_len[g] is 512 or 256, each in some group; data group g holds 512 // bucket_len[g] sequences of that length. pad_len[g, q] is below bucket_len[g] // 8; entries with q >= 512 // bucket_len[g] are unused.
All inputs are finite; a program needn't handle non-finite values.
Results may differ from the reference program's by a relative error of at most 0.03.
Values may be sent and summed in bfloat16 or wider, within the bound.
No kernel may reach another device: no remote copies, remote signals or barrier semaphores. Data moves between devices by JAX's collectives and lax.ppermute only.
A program may use at most 320 MiB of HBM per device.

```python
import jax
import jax.numpy as jnp
from jax import lax

D = 1024
H = 16
FF = 4096
NB = 32
HD = 64
TOK_DEV = 128
SLOTS = 2
LMAX = 512
TOKENS = 4096
N_STREAM = 4
N_DP = 8


def bucket_shifts(key):
    shifts = jax.random.randint(jax.random.fold_in(key, 11), (N_DP,), 0, 2)
    order = jax.random.permutation(jax.random.fold_in(key, 12), N_DP)
    shifts = shifts.at[order[0]].set(0).at[order[1]].set(1)
    return (shifts, order)


def lengths_of(shifts):
    return jnp.where(shifts == 0, LMAX, LMAX // 2).astype(jnp.int32)


def draw_bucket_len(key, part):
    shifts, _ = bucket_shifts(key)
    return lengths_of(shifts)


def draw_pad_len(key, part):
    shifts, order = bucket_shifts(key)
    key = jax.random.fold_in(key, 2)
    limits = lengths_of(shifts) // 8
    raw = jax.random.randint(key, (N_DP, SLOTS), 0, 1 << 20)
    pads = raw % limits[:, None]
    pads = pads.at[order[0], 0].set(LMAX // 8 - 1).at[order[1], 0].set(0)
    return pads.astype(jnp.int32)


def plant(entries, stream_key, least, high):
    longest = entries.shape.index(max(entries.shape))
    spots = []
    for shift in (0, 1):
        where = [jax.random.randint(jax.random.fold_in(stream_key, axis), (), 0, length) for axis, length in enumerate(entries.shape)]
        where[longest] = (where[longest] + shift) % entries.shape[longest]
        spots.append(tuple(where))
    return entries.at[spots[0]].set(least).at[spots[1]].set(high)


def steps_of(rng, shape, shards, smallest, largest):
    def one(dim, shards_of):
        steps = jax.random.uniform(jax.random.fold_in(jax.random.fold_in(rng, 6), dim), (shards_of,), jnp.float32, smallest / len(shards), largest / len(shards))
        return jnp.repeat(jnp.exp(steps), shape[dim] // shards_of).reshape((-1,) + (1,) * (len(shape) - dim - 1))

    level = one(*shards[0])
    for cut in shards[1:]:
        level = level * one(*cut)
    return level


def normal_values(rng, shape, scale, limit, shards=(), held_as=jnp.bfloat16):
    values = scale * jax.random.normal(rng, shape, jnp.float32)
    if shards:
        values = values * steps_of(rng, shape, shards, -0.22, 0.18)
    return jnp.clip(values, -limit, limit).astype(held_as)


def setup_inputs(seed: int = 0) -> dict:
    seeds = jax.random.split(jax.random.key(seed), 25)
    return {
        "enc_input": normal_values(seeds[0], (TOKENS, D), 1.0, 6.0, ((0, 32),)),
        "pred_input": normal_values(seeds[1], (2, TOKENS, D), 1.0, 6.0, ((1, 32),)),
        "cotangent": normal_values(seeds[2], (3, TOKENS, D), 1.0, 6.0, ((1, 32),)),
        "bucket_len": draw_bucket_len(jax.random.fold_in(seeds[24], 71), 0),
        "pad_len": draw_pad_len(jax.random.fold_in(seeds[24], 71), 0),
        "rel_table": plant(jax.random.randint(seeds[5], (LMAX,), 0, NB), jax.random.fold_in(seeds[5], 1), 0, NB - 1).astype(jnp.int32),
        "enc_qkv": normal_values(seeds[6], (3, D, D), D ** -0.5, 0.1875, ((1, 8),)),
        "enc_out": normal_values(seeds[7], (D, D), (max(D // 256, 1)) ** -0.5, 3.0, ((0, 8),)),
        "enc_ffn_in": normal_values(seeds[8], (D, FF), D ** -0.5, 0.1875, ((0, 8),)),
        "enc_ffn_out": normal_values(seeds[9], (FF, D), FF ** -0.5, 0.09375, ((0, 8),)),
        "enc_ffn_bias": normal_values(seeds[10], (FF,), 0.5, 3.0, ((0, 8),)),
        "enc_bias": normal_values(seeds[11], (4, D), 0.3, 2.0, ((1, 8),)),
        "enc_gain": jnp.clip(1.0 + 0.1 * jax.random.normal(seeds[12], (2, D), jnp.float32), 0.5, 1.5).astype(jnp.bfloat16),
        "enc_shift": normal_values(seeds[13], (2, D), 0.3, 2.0, ((1, 8),)),
        "dec_qkv": normal_values(seeds[14], (3, D, D), D ** -0.5, 0.1875, ((1, 8),)),
        "dec_out": normal_values(seeds[15], (D, D), (max(D // 256, 1)) ** -0.5, 3.0, ((0, 8),)),
        "dec_rel": normal_values(seeds[16], (D, H * NB), D ** -0.5, 0.1875, ((0, 8),)),
        "dec_rel_bias": normal_values(seeds[17], (H * NB,), 0.5, 3.0, ((0, 8),)),
        "dec_ffn_in": normal_values(seeds[18], (D, FF), D ** -0.5, 0.1875, ((0, 8),)),
        "dec_ffn_out": normal_values(seeds[19], (FF, D), FF ** -0.5, 0.09375, ((0, 8),)),
        "dec_ffn_bias": normal_values(seeds[20], (FF,), 0.5, 3.0, ((0, 8),)),
        "dec_bias": normal_values(seeds[21], (4, D), 0.3, 2.0, ((1, 8),)),
        "dec_gain": jnp.clip(1.0 + 0.1 * jax.random.normal(seeds[22], (2, D), jnp.float32), 0.5, 1.5).astype(jnp.bfloat16),
        "dec_shift": normal_values(seeds[23], (2, D), 0.3, 2.0, ((1, 8),)),
    }


EPSILON = 1e-05
MASKED = -1000000000.0

@jax.custom_vjp
def low(v):
    return lax.optimization_barrier(v.astype(jnp.bfloat16)).astype(jnp.float32)

@jax.custom_vjp
def low_back(v):
    return v

def low_keep(v):
    return (low(v), None)

def low_pass(kept, grad):
    return (grad,)

def back_keep(v):
    return (v, None)

def back_low(kept, grad):
    return (low(grad),)
low.defvjp(low_keep, low_pass)
low_back.defvjp(back_keep, back_low)

def matmul(left, right):
    return jnp.dot(left, right, precision=lax.Precision.HIGHEST)

def normed(values, gain, shift):
    center = values - lax.optimization_barrier(jnp.mean(values, axis=-1, keepdims=True))
    spread = lax.optimization_barrier(jnp.mean(center * center, axis=-1, keepdims=True))
    return center * lax.rsqrt(spread + EPSILON) * gain + shift

def split_heads(values):
    return values.reshape(values.shape[0], H, HD)

def head_scores(queries, key_rows):
    return jnp.einsum('qhd,khd->hqk', split_heads(queries), split_heads(key_rows), precision=lax.Precision.HIGHEST) * HD ** (-0.5)

def layout(bucket, pads):
    quarter = bucket // N_STREAM
    places = jnp.arange(N_STREAM * TOK_DEV, dtype=jnp.int32)
    holder = places // TOK_DEV
    within = places % TOK_DEV
    sequence = within // quarter
    position = holder * quarter + within % quarter
    owned = sequence[:, None] == jnp.arange(SLOTS, dtype=jnp.int32)[None, :]
    padding = lax.optimization_barrier(jnp.sum(jnp.where(owned, pads[None, :], 0), axis=1))
    return (sequence, position, position < bucket - padding)

def feed_forward(hidden, w_in, w_back, b_in, b_back, gain, shift):
    inner = low_back(matmul(low(hidden), w_in) + b_in)
    active = low(jax.nn.gelu(inner, approximate=False))
    branch = low_back(matmul(active, w_back) + b_back)
    return normed(hidden + branch, gain, shift)

def projections(rounded, qkv, biases):
    queries = low(low_back(matmul(rounded, qkv[0]) + biases[0]))
    key_rows = low(low_back(matmul(rounded, qkv[1])))
    val_rows = low(low_back(matmul(rounded, qkv[2]) + biases[1]))
    return (queries, key_rows, val_rows)

def encoder_layer(inputs, weights, sequence, position, valid):
    qkv, w_out, w_in, w_back, b_in, biases, gains, shifts = weights
    queries, key_rows, val_rows = projections(inputs, qkv, biases)
    allowed = (sequence[:, None] == sequence[None, :]) & valid[None, :]
    scores = jnp.where(allowed[None], low_back(head_scores(queries, key_rows)), MASKED)
    probs = jax.nn.softmax(scores, axis=-1)
    context = jnp.einsum('hqk,khd->qhd', low(probs), split_heads(val_rows), precision=lax.Precision.HIGHEST).reshape(inputs.shape)
    attended = low_back(matmul(low(low_back(context)), w_out) + biases[2])
    hidden = normed(inputs + attended, gains[0], shifts[0])
    return feed_forward(hidden, w_in, w_back, b_in, biases[3], gains[1], shifts[1])

def decoder_layer(streams, weights, table, sequence, position, valid):
    qkv, w_out, rel_w, rel_b, w_in, w_back, b_in, biases, gains, shifts = weights
    rows = streams[0].shape[0]
    distance = jnp.clip(position[:, None] - position[None, :], 0, LMAX - 1)
    picked = jnp.broadcast_to(table[distance][:, None, :], (rows, H, rows))
    same = (sequence[:, None] == sequence[None, :]) & valid[None, :]
    earlier = position[None, :] < position[:, None]
    projected = []
    for inputs in streams:
        rounded = low(inputs)
        queries, key_rows, val_rows = projections(rounded, qkv, biases)
        rel_rows = low_back(matmul(rounded, rel_w) + rel_b).reshape(rows, H, NB)
        projected.append((queries, key_rows, val_rows, rel_rows))
    main_keys = projected[0][1]
    main_vals = split_heads(projected[0][2])
    results = []
    for number in range(3):
        queries, key_rows, val_rows, rel_rows = projected[number]
        rel_bias = jnp.transpose(jnp.take_along_axis(rel_rows, picked, axis=2), (1, 0, 2))
        scores = low_back(head_scores(queries, main_keys) + rel_bias)
        if number == 0:
            allowed = same & (earlier | (position[None, :] == position[:, None]))
            probs = jax.nn.softmax(jnp.where(allowed[None], scores, MASKED), axis=-1)
            context = jnp.einsum('hqk,khd->qhd', low(probs), main_vals, precision=lax.Precision.HIGHEST)
        else:
            own_dot = lax.optimization_barrier(jnp.sum(split_heads(queries) * split_heads(key_rows), axis=-1)) * HD ** (-0.5)
            own = low_back(jnp.transpose(own_dot) + jnp.transpose(rel_rows[:, :, table[0]]))
            full = jnp.concatenate([jnp.where((same & earlier)[None], scores, MASKED), own[:, :, None]], axis=2)
            probs = jax.nn.softmax(full, axis=-1)
            context = jnp.einsum('hqk,khd->qhd', low(probs[:, :, :-1]), main_vals, precision=lax.Precision.HIGHEST)
            context = context + jnp.transpose(probs[:, :, -1])[:, :, None] * split_heads(val_rows)
        context = context.reshape(rows, D)
        attended = low_back(matmul(low(low_back(context)), w_out) + biases[2])
        hidden = normed(streams[number] + attended, gains[0], shifts[0])
        results.append(feed_forward(hidden, w_in, w_back, b_in, biases[3], gains[1], shifts[1]))
    return results

def reference(enc_input, pred_input, cotangent, bucket_len, pad_len, rel_table, enc_qkv, enc_out, enc_ffn_in, enc_ffn_out, enc_ffn_bias, enc_bias, enc_gain, enc_shift, dec_qkv, dec_out, dec_rel, dec_rel_bias, dec_ffn_in, dec_ffn_out, dec_ffn_bias, dec_bias, dec_gain, dec_shift):
    single = jnp.float32
    enc_w = tuple((w.astype(single) for w in (enc_qkv, enc_out, enc_ffn_in, enc_ffn_out, enc_ffn_bias, enc_bias, enc_gain, enc_shift)))
    dec_w = tuple((w.astype(single) for w in (dec_qkv, dec_out, dec_rel, dec_rel_bias, dec_ffn_in, dec_ffn_out, dec_ffn_bias, dec_bias, dec_gain, dec_shift)))
    rows = N_STREAM * TOK_DEV
    enc_groups = jnp.transpose(enc_input.astype(single).reshape(N_STREAM, N_DP, TOK_DEV, D), (1, 0, 2, 3)).reshape(N_DP, rows, D)
    pred_groups = jnp.transpose(pred_input.astype(single).reshape(2, N_STREAM, N_DP, TOK_DEV, D), (2, 0, 1, 3, 4)).reshape(N_DP, 2, rows, D)
    cot_groups = jnp.transpose(cotangent.astype(single).reshape(3, N_STREAM, N_DP, TOK_DEV, D), (2, 0, 1, 3, 4)).reshape(N_DP, 3, rows, D)

    def forward(enc_weights, dec_weights, enc_rows_all, pred_rows_all):

        def one_group(carry, items):
            enc_rows, pred_rows, bucket, pads = items
            sequence, position, valid = layout(bucket, pads)
            main = encoder_layer(enc_rows, enc_weights, sequence, position, valid)
            outs = decoder_layer((main, pred_rows[0], pred_rows[1]), dec_weights, rel_table, sequence, position, valid)
            return (carry, jnp.stack(outs))
        _, outs = lax.scan(jax.checkpoint(one_group), jnp.zeros((), jnp.float32), (enc_rows_all, pred_rows_all, bucket_len, pad_len))
        return outs
    outs, pullback = jax.vjp(forward, enc_w, dec_w, enc_groups, pred_groups)
    enc_g, dec_g, enc_in_g, pred_in_g = pullback(cot_groups)
    dec_output = jnp.transpose(outs.reshape(N_DP, 3, N_STREAM, TOK_DEV, D), (1, 2, 0, 3, 4)).reshape(3, TOKENS, D)
    enc_input_grad = jnp.transpose(enc_in_g.reshape(N_DP, N_STREAM, TOK_DEV, D), (1, 0, 2, 3)).reshape(TOKENS, D)
    pred_input_grad = jnp.transpose(pred_in_g.reshape(N_DP, 2, N_STREAM, TOK_DEV, D), (1, 2, 0, 3, 4)).reshape(2, TOKENS, D)
    return (dec_output, enc_input_grad, pred_input_grad, enc_g[0], enc_g[1], enc_g[2], enc_g[3], enc_g[4], enc_g[5], enc_g[6], enc_g[7], dec_g[0], dec_g[1], dec_g[2], dec_g[3], dec_g[4], dec_g[5], dec_g[6], dec_g[7], dec_g[8], dec_g[9])
```

```python
from functools import partial

import jax
import jax.numpy as jnp
from jax import lax
from jax.experimental import pallas as pl
from jax.experimental.pallas import tpu as pltpu
from jax.sharding import PartitionSpec as P

H = 16
NB = 32
HD = 64
EPSILON = 1e-05
MASKED = -1000000000.0
BF = jnp.bfloat16
F32 = jnp.float32
TILE = 128
STREAMS = 4
XOR = (0, 2, 1, 3)
VMEM_LIMIT = 60 * 1024 * 1024


def dot(a, b):
    return jnp.dot(a, b, preferred_element_type=F32)


def dot_nt(a, b):
    return lax.dot_general(a, b, (((1,), (1,)), ((), ())), preferred_element_type=F32)


def dot_tn(a, b):
    return lax.dot_general(a, b, (((0,), (0,)), ((), ())), preferred_element_type=F32)


def swap(values, bit):
    return lax.ppermute(values, "stream", [(i, i ^ bit) for i in range(STREAMS)])


def gather_rows(rows):
    far = swap(rows, 2)
    half = jnp.concatenate([rows, far], axis=0)
    return jnp.concatenate([half, swap(half, 1)], axis=0)


def scatter_rows(partials):
    n = partials.shape[0] // 4
    near = swap(partials[2 * n :].astype(BF), 1)
    keep = partials[: 2 * n].astype(F32) + near.astype(F32)
    far = swap(keep[n:].astype(BF), 2)
    return keep[:n] + far.astype(F32)


def turn_blocks(blocks):
    far = swap(jnp.stack([blocks[1], blocks[3]]), 2)
    near = swap(jnp.stack([blocks[2], far[1]]), 1)
    return [blocks[0], far[0], near[0], near[1]]


def by_absolute(blocks, here):
    stacked = jnp.stack([blocks[XOR.index(j)] for j in range(4)])
    return [lax.dynamic_index_in_dim(stacked, here ^ a, 0, keepdims=False) for a in range(4)]


def ring_order(n):
    return list(range(0, n, 2)) + list(range(n - 1, 0, -2))


def ring_member(place, n):
    place = lax.rem(place + 2 * n, n)
    return jnp.where(place < n // 2, 2 * place, 2 * (n - place) - 1)


def ring_place(g, n):
    return jnp.where(g % 2 == 0, g // 2, n - (g + 1) // 2)


def ring_step(values, n, step):
    order = ring_order(n)
    pairs = [(order[i], order[(i + step) % n]) for i in range(n)]
    return lax.ppermute(values, "dp", pairs)


def ring_pieces(own, n):
    rows = own.shape[0]
    pieces = [(0, 0, own)]
    ahead = back = own
    for k in range(1, n // 2):
        ahead = ring_step(ahead, n, 1)
        back = ring_step(back, n, -1)
        pieces += [(k, 0, ahead), (n - k, 0, back)]
    half = halved(rows)
    top = ring_step(ahead[:half], n, 1)
    bottom = ring_step(back[half:], n, -1)
    pieces += [(n // 2, 0, top), (n // 2, half, bottom)]
    return pieces


def assemble(pieces, index, regions, shapes, n):
    moves = []
    for number, (behind, first, piece) in enumerate(pieces):
        last = first + piece.shape[0]
        for r0, r1, c0, c1, which, to_row, to_col in regions:
            lo, hi = max(r0, first), min(r1, last)
            if lo < hi:
                moves.append((number, behind, lo - first, hi - first, c0, c1, which, to_row + lo - r0, to_col))

    def kernel(index_ref, *refs):
        sources = refs[: len(pieces)]
        outs = refs[len(pieces) :]
        for number, behind, lo, hi, c0, c1, which, row, col in moves:
            g = index_ref[behind]
            outs[which][g, row : row + hi - lo, col : col + c1 - c0] = sources[number][lo:hi, c0:c1]

    vmem = pl.BlockSpec(memory_space=pltpu.VMEM)
    return pl.pallas_call(
        kernel,
        out_shape=[jax.ShapeDtypeStruct((n,) + shape, BF) for shape in shapes],
        in_specs=[pl.BlockSpec(memory_space=pltpu.SMEM)] + [vmem] * len(pieces),
        out_specs=[vmem] * len(shapes),
        compiler_params=pltpu.CompilerParams(vmem_limit_bytes=VMEM_LIMIT),
    )(index, *[piece for _, _, piece in pieces])


def halved(rows):
    return rows // 32 * 16


def ring_sum(arrays, n, place):
    def part(ahead):
        g = ring_member(place + ahead, n)
        return jnp.concatenate(
            [lax.dynamic_index_in_dim(a, g, 0, keepdims=False) for a in arrays], axis=0
        ).astype(F32)

    middle = part(n // 2)
    half = halved(middle.shape[0])
    up = ring_step(middle[:half].astype(BF), n, 1).astype(F32)
    down = ring_step(middle[half:].astype(BF), n, -1).astype(F32)
    for k in range(n // 2 - 1, 0, -1):
        ahead, back = part(k), part(-k)
        if k == n // 2 - 1:
            ahead = jnp.concatenate([ahead[:half] + up, ahead[half:]], axis=0)
            back = jnp.concatenate([back[:half], back[half:] + down], axis=0)
        else:
            ahead, back = ahead + up, back + down
        up = ring_step(ahead.astype(BF), n, 1).astype(F32)
        down = ring_step(back.astype(BF), n, -1).astype(F32)
    return part(0) + up + down


def tile_width(t, causal, total):
    return TILE * (t + 1) if causal else total


def head_mask(e):
    lane = lax.broadcasted_iota(jnp.int32, (1, TILE), 1)
    return ((lane // HD) == e).astype(F32)


def rel_mask(h):
    lane = lax.broadcasted_iota(jnp.int32, (1, TILE), 1)
    return ((lane // NB) == h).astype(F32)


def allowed_keys(t, width, meta, causal, strict):
    bucket = meta[8]
    shape = (TILE, width)
    row = lax.broadcasted_iota(jnp.int32, shape, 0) + t * TILE
    col = lax.broadcasted_iota(jnp.int32, shape, 1)
    pos = col & (bucket - 1)
    first = col < bucket
    limit = bucket - jnp.where(first, meta[9], meta[10])
    allowed = (pos < limit) & ((row < bucket) == first)
    if causal:
        allowed = allowed & ((col < row) if strict else (col <= row))
    return allowed


def load_rows(meta, target, source, c0, c1):
    for chunk in range(8):
        start = pl.multiple_of(meta[chunk], 64)
        target[pl.ds(start, 64), :] = source[chunk * 64 : chunk * 64 + 64, c0:c1]


def store_rows(meta, target, source, c0, c1):
    for chunk in range(8):
        start = pl.multiple_of(meta[chunk], 64)
        target[chunk * 64 : chunk * 64 + 64, c0:c1] = source[pl.ds(start, 64), :].astype(target.dtype)


def rel_bias(rel_rows, h, table):
    high = rel_rows.astype(BF)
    rest = (rel_rows - high.astype(F32)).astype(BF)
    mask = rel_mask(h)
    both = jnp.concatenate(
        [(high.astype(F32) * mask).astype(BF), (rest.astype(F32) * mask).astype(BF)], axis=1
    )
    spread = dot(both, table)
    return pltpu.roll(spread, 0, 1, stride=1, stride_axis=0)


def scores_of(t, h, width, meta, qs, ks, rs, table_ref, causal, strict):
    pair, e = h // 2, h % 2
    lanes = slice(TILE * pair, TILE * (pair + 1))
    rows = slice(TILE * t, TILE * (t + 1))
    query = (qs[rows, lanes].astype(F32) * (head_mask(e) * HD**-0.5)).astype(BF)
    scores = dot_nt(query, ks[0:width, lanes])
    if rs is not None:
        first = sum(TILE * (u + 1) for u in range(t))
        scores = scores + rel_bias(rs[rows, :], h, table_ref[:, first : first + width])
    return query, jnp.where(allowed_keys(t, width, meta, causal, strict), scores, MASKED)


def attention_forward(meta, qkv, main=None, rel=None, tables=None):
    total = qkv.shape[0]
    width_all = qkv.shape[1] // 3
    heads = width_all // HD
    causal = rel is not None
    own = main is not None

    def kernel(meta_ref, *refs):
        refs = list(refs)
        qkv_ref = refs.pop(0)
        main_ref = refs.pop(0) if own else qkv_ref
        rel_ref, table_ref, hot_ref = (refs.pop(0), refs.pop(0), refs.pop(0)) if causal else (None,) * 3
        ctx_ref, lse_ref, qs, ks, vs, cs = refs[:6]
        refs = refs[6:]
        rs = refs.pop(0) if causal else None
        load_rows(meta_ref, qs, qkv_ref, 0, width_all)
        load_rows(meta_ref, ks, main_ref, width_all, 2 * width_all)
        load_rows(meta_ref, vs, main_ref, 2 * width_all, 3 * width_all)
        if causal:
            load_rows(meta_ref, rs, rel_ref, 0, rel.shape[1])
        if own:
            kn, vn = refs
            load_rows(meta_ref, kn, qkv_ref, width_all, 2 * width_all)
            load_rows(meta_ref, vn, qkv_ref, 2 * width_all, 3 * width_all)
        for t in range(total // TILE):
            rows = slice(TILE * t, TILE * (t + 1))
            width = tile_width(t, causal, total)
            lse_lane = lax.broadcasted_iota(jnp.int32, (TILE, TILE), 1)
            lse = jnp.zeros((TILE, TILE), F32)
            for pair in range(heads // 2):
                lanes = slice(TILE * pair, TILE * (pair + 1))
                context = jnp.zeros((TILE, TILE), F32)
                for e in range(2):
                    h = 2 * pair + e
                    query, scores = scores_of(t, h, width, meta_ref, qs, ks, rs, table_ref, causal, own)
                    top = jnp.max(scores, axis=1, keepdims=True)
                    if own:
                        own_score = jnp.sum(
                            query.astype(F32) * kn[rows, lanes].astype(F32), axis=1, keepdims=True
                        ) + jnp.sum(rs[rows, :] * (hot_ref[...] * rel_mask(h)), axis=1, keepdims=True)
                        top = jnp.maximum(top, own_score)
                    expos = jnp.exp(scores - top)
                    sums = jnp.sum(expos, axis=1, keepdims=True)
                    if own:
                        own_expo = jnp.exp(own_score - top)
                        sums = sums + own_expo
                    inverse = 1.0 / sums
                    probs = (expos * inverse).astype(BF)
                    part = dot(probs, vs[0:width, lanes])
                    if own:
                        part = part + (own_expo * inverse) * vn[rows, lanes].astype(F32)
                    context = context + part * head_mask(e)
                    lse = jnp.where(lse_lane == h, top + jnp.log(sums), lse)
                cs[rows, lanes] = context.astype(BF)
            lse_ref[rows, :] = lse
        store_rows(meta_ref, ctx_ref, cs, 0, width_all)

    vmem = pl.BlockSpec(memory_space=pltpu.VMEM)
    args = [qkv]
    scratch = [pltpu.VMEM((total, width_all), BF) for _ in range(4)]
    if own:
        args.append(main)
    if causal:
        args += [rel, tables[0], tables[2]]
        scratch.append(pltpu.VMEM((total, rel.shape[1]), F32))
    if own:
        scratch += [pltpu.VMEM((total, width_all), BF) for _ in range(2)]
    return pl.pallas_call(
        kernel,
        out_shape=(
            jax.ShapeDtypeStruct((total, width_all), BF),
            jax.ShapeDtypeStruct((total, TILE), F32),
        ),
        in_specs=[pl.BlockSpec(memory_space=pltpu.SMEM)] + [vmem] * len(args),
        out_specs=(vmem, vmem),
        scratch_shapes=scratch,
        compiler_params=pltpu.CompilerParams(vmem_limit_bytes=VMEM_LIMIT),
    )(meta, *args)


def attention_backward(meta, qkv, dctx, lse, main=None, rel=None, tables=None):
    total = qkv.shape[0]
    width_all = qkv.shape[1] // 3
    heads = width_all // HD
    causal = rel is not None
    own = main is not None

    def kernel(meta_ref, *refs):
        refs = list(refs)
        qkv_ref, dctx_ref, lse_ref = refs[:3]
        refs = refs[3:]
        main_ref = refs.pop(0) if own else qkv_ref
        rel_ref, table_ref, back_ref, hot_ref, flip_ref = (
            [refs.pop(0) for _ in range(5)] if causal else (None,) * 5
        )
        dq_ref, dk_ref, dv_ref = refs[:3]
        refs = refs[3:]
        drel_ref = refs.pop(0) if causal else None
        dkn_ref, dvn_ref = (refs.pop(0), refs.pop(0)) if own else (None, None)
        qs, ks, vs, gs, dqs, dks, dvs = refs[:7]
        refs = refs[7:]
        rs, drs = (refs.pop(0), refs.pop(0)) if causal else (None, None)
        load_rows(meta_ref, qs, qkv_ref, 0, width_all)
        load_rows(meta_ref, ks, main_ref, width_all, 2 * width_all)
        load_rows(meta_ref, vs, main_ref, 2 * width_all, 3 * width_all)
        load_rows(meta_ref, gs, dctx_ref, 0, width_all)
        if causal:
            load_rows(meta_ref, rs, rel_ref, 0, rel.shape[1])
        if own:
            kn, vn, dkn, dvn = refs
            load_rows(meta_ref, kn, qkv_ref, width_all, 2 * width_all)
            load_rows(meta_ref, vn, qkv_ref, 2 * width_all, 3 * width_all)
        dks[...] = jnp.zeros_like(dks)
        dvs[...] = jnp.zeros_like(dvs)
        for t in range(total // TILE):
            rows = slice(TILE * t, TILE * (t + 1))
            width = tile_width(t, causal, total)
            first = sum(TILE * (u + 1) for u in range(t))
            drel = jnp.zeros((TILE, TILE), F32)
            for pair in range(heads // 2):
                lanes = slice(TILE * pair, TILE * (pair + 1))
                dq = jnp.zeros((TILE, TILE), F32)
                dkey_own = jnp.zeros((TILE, TILE), F32)
                dval_own = jnp.zeros((TILE, TILE), F32)
                for e in range(2):
                    h = 2 * pair + e
                    mask = head_mask(e)
                    query, scores = scores_of(t, h, width, meta_ref, qs, ks, rs, table_ref, causal, own)
                    norm = lse_ref[rows, h : h + 1]
                    probs = jnp.exp(scores - norm)
                    grad = (gs[rows, lanes].astype(F32) * mask).astype(BF)
                    dprobs = dot_nt(grad, vs[0:width, lanes])
                    rowdot = jnp.sum(probs * dprobs, axis=1, keepdims=True)
                    if own:
                        own_score = jnp.sum(
                            query.astype(F32) * kn[rows, lanes].astype(F32), axis=1, keepdims=True
                        ) + jnp.sum(rs[rows, :] * (hot_ref[...] * rel_mask(h)), axis=1, keepdims=True)
                        own_prob = jnp.exp(own_score - norm)
                        own_dprob = jnp.sum(
                            grad.astype(F32) * vn[rows, lanes].astype(F32), axis=1, keepdims=True
                        )
                        rowdot = rowdot + own_prob * own_dprob
                        own_dscore = (own_prob * (own_dprob - rowdot)).astype(BF).astype(F32)
                        dq = dq + own_dscore * kn[rows, lanes].astype(F32) * (mask * HD**-0.5)
                        dkey_own = dkey_own + own_dscore * query.astype(F32)
                        dval_own = dval_own + own_prob * grad.astype(F32)
                        drel = drel + own_dscore * (hot_ref[...] * rel_mask(h))
                    dscores = (probs * (dprobs - rowdot)).astype(BF)
                    dq = dq + dot(dscores, ks[0:width, lanes]) * (mask * HD**-0.5)
                    dks[0:width, lanes] += dot_tn(dscores, query)
                    dvs[0:width, lanes] += dot_tn(probs.astype(BF), grad)
                    if causal:
                        blocks = [
                            dot(dscores[:, TILE * b : TILE * (b + 1)], flip_ref[...])
                            for b in reversed(range(width // TILE))
                        ]
                        mirrored = jnp.concatenate(blocks, axis=1) if len(blocks) > 1 else blocks[0]
                        turned = pltpu.roll(mirrored, 0, 1, stride=1, stride_axis=0).astype(BF)
                        drel = drel + dot(turned, back_ref[first : first + width, :]) * rel_mask(h)
                dqs[rows, lanes] = dq
                if own:
                    dkn[rows, lanes] = dkey_own
                    dvn[rows, lanes] = dval_own
            if causal:
                drs[rows, :] = drel
        store_rows(meta_ref, dq_ref, dqs, 0, width_all)
        store_rows(meta_ref, dk_ref, dks, 0, width_all)
        store_rows(meta_ref, dv_ref, dvs, 0, width_all)
        if causal:
            store_rows(meta_ref, drel_ref, drs, 0, rel.shape[1])
        if own:
            store_rows(meta_ref, dkn_ref, dkn, 0, width_all)
            store_rows(meta_ref, dvn_ref, dvn, 0, width_all)

    vmem = pl.BlockSpec(memory_space=pltpu.VMEM)
    args = [qkv, dctx, lse]
    shape = (total, width_all)
    outs = [jax.ShapeDtypeStruct(shape, BF), jax.ShapeDtypeStruct(shape, F32), jax.ShapeDtypeStruct(shape, F32)]
    scratch = [pltpu.VMEM(shape, BF) for _ in range(4)] + [pltpu.VMEM(shape, F32) for _ in range(3)]
    if own:
        args.append(main)
    if causal:
        args += [rel, tables[0], tables[1], tables[2], tables[3]]
        outs.append(jax.ShapeDtypeStruct((total, rel.shape[1]), BF))
        scratch += [pltpu.VMEM((total, rel.shape[1]), F32) for _ in range(2)]
    if own:
        outs += [jax.ShapeDtypeStruct(shape, BF) for _ in range(2)]
        scratch += [pltpu.VMEM(shape, BF) for _ in range(2)] + [pltpu.VMEM(shape, F32) for _ in range(2)]
    return pl.pallas_call(
        kernel,
        out_shape=outs,
        in_specs=[pl.BlockSpec(memory_space=pltpu.SMEM)] + [vmem] * len(args),
        out_specs=[vmem] * len(outs),
        scratch_shapes=scratch,
        compiler_params=pltpu.CompilerParams(vmem_limit_bytes=VMEM_LIMIT),
    )(meta, *args)


def rel_tables(rel_table, total):
    ahead, back = [], []
    for t in range(total // TILE):
        width = TILE * (t + 1)
        here = rel_table[:width]
        ahead += [jnp.flip(here[: TILE * t + 1]), jnp.flip(here[TILE * t + 1 :])]
        back += [here[width - TILE + 1 :], here[: width - TILE + 1]]
    ahead, back = jnp.concatenate(ahead), jnp.concatenate(back)
    rows = jnp.arange(2 * TILE, dtype=jnp.int32) % NB
    forward = (rows[:, None] == ahead[None, :]).astype(BF)
    backward = (back[:, None] == rows[None, :TILE]).astype(BF)
    hot = (rows[None, :TILE] == rel_table[0]).astype(F32)
    ids = jnp.arange(TILE, dtype=jnp.int32)
    flip = (ids[:, None] + ids[None, :] == TILE - 1).astype(BF)
    return forward, backward, hot, flip


def norm_parts(values):
    center = values - jnp.mean(values, axis=-1, keepdims=True)
    spread = jnp.mean(center * center, axis=-1, keepdims=True)
    inverse = lax.rsqrt(spread + EPSILON)
    return center * inverse, inverse


def norm_back(grad, unit, inverse, gain):
    inner = grad * gain
    mean = jnp.mean(inner, axis=-1, keepdims=True)
    along = jnp.mean(inner * unit, axis=-1, keepdims=True)
    return inverse * (inner - mean - unit * along), jnp.sum(grad * unit, axis=0), jnp.sum(grad, axis=0)


def gelu(inner):
    return jax.nn.gelu(inner, approximate=False)


class Layer:
    pass


def own_columns(matrix, here):
    width = matrix.shape[-1] // STREAMS
    return lax.dynamic_slice_in_dim(matrix, here * width, width, axis=matrix.ndim - 1)


def forward_tail(inputs, context, w):
    attended = scatter_rows(dot(context, w.out)) + w.bias[2]
    unit0, inverse0 = norm_parts(inputs + attended)
    hidden = unit0 * w.gain[0] + w.shift[0]
    hidden_all = gather_rows(hidden.astype(BF))
    inner = dot(hidden_all, w.ffn_in) + w.ffn_bias
    active = gelu(inner).astype(BF)
    branch = scatter_rows(dot(active, w.ffn_out)) + w.bias[3]
    unit1, inverse1 = norm_parts(hidden + branch)
    output = unit1 * w.gain[1] + w.shift[1]
    return output, (unit0, inverse0, hidden_all, inner, active, unit1, inverse1)


def backward_tail(grad, context, kept, w):
    unit0, inverse0, hidden_all, inner, active, unit1, inverse1 = kept
    sum_grad, gain1, shift1 = norm_back(grad, unit1, inverse1, w.gain[1])
    branch_low = sum_grad.astype(BF)
    branch_all = gather_rows(branch_low)
    active_grad = dot_nt(branch_all, w.ffn_out)
    _, pull = jax.vjp(gelu, inner)
    inner_grad = pull(active_grad)[0].astype(BF)
    hidden_grad = sum_grad + scatter_rows(dot_nt(inner_grad, w.ffn_in))
    input_grad, gain0, shift0 = norm_back(hidden_grad, unit0, inverse0, w.gain[0])
    attended_low = input_grad.astype(BF)
    attended_all = gather_rows(attended_low)
    context_grad = dot_nt(attended_all, w.out).astype(BF)
    weight_grads = (
        dot_tn(context, attended_all),
        dot_tn(hidden_all, inner_grad),
        dot_tn(active, branch_all),
    )
    small = (
        jnp.sum(inner_grad.astype(F32), axis=0),
        jnp.sum(attended_low.astype(F32), axis=0),
        jnp.sum(branch_low.astype(F32), axis=0),
        gain0,
        gain1,
        shift0,
        shift1,
    )
    return input_grad, context_grad, weight_grads, small


def per_device(
    enc_input, pred_input, cotangent, bucket_len, pad_len, rel_table,
    enc_qkv, enc_out, enc_ffn_in, enc_ffn_out, enc_ffn_bias, enc_bias, enc_gain, enc_shift,
    dec_qkv, dec_out, dec_rel, dec_rel_bias, dec_ffn_in, dec_ffn_out, dec_ffn_bias, dec_bias, dec_gain, dec_shift,
):
    here = lax.axis_index("stream")
    n = lax.axis_size("dp")
    group = lax.axis_index("dp")
    place = ring_place(group, n)
    rows = enc_input.shape[0]
    total = STREAMS * rows
    dim = enc_input.shape[1]
    share = enc_out.shape[0]
    quarter = dim // STREAMS
    ffn = enc_ffn_in.shape[1]
    ffn_share = enc_ffn_out.shape[0]
    ffn_part = ffn_share // STREAMS
    rel_all = dec_rel.shape[1]
    rel_part = rel_all // STREAMS

    bucket = bucket_len[0]
    starts = []
    for j in XOR:
        holder = here ^ j
        for chunk in range(2):
            starts.append(jnp.where(bucket == total, holder * rows + chunk * 64, chunk * bucket + holder * 64))
    meta = jnp.stack([v.astype(jnp.int32) for v in starts + [bucket, pad_len[0, 0], pad_len[0, 1]]])
    tables = rel_tables(rel_table, total)
    ring_index = jnp.stack([ring_member(place - o, n) for o in range(n)]).astype(jnp.int32)

    def ffn_columns(matrix):
        blocks = matrix.reshape(matrix.shape[0], n, ffn_share)
        part = lax.dynamic_slice_in_dim(blocks, here * ffn_part, ffn_part, axis=2)
        return part.reshape(matrix.shape[0], n * ffn_part)

    def ffn_rows(matrix):
        return lax.dynamic_slice_in_dim(matrix, here * ffn_part, ffn_part, axis=0)

    smalls = [
        a.reshape(-1)
        for a in (
            enc_ffn_bias, enc_bias, enc_gain, enc_shift, dec_ffn_bias, dec_bias, dec_gain, dec_shift, dec_rel_bias
        )
    ]
    small_own = jnp.concatenate(smalls)
    fixed = 4 * share
    small_rows = -(-small_own.shape[0] // quarter)
    small_rows += -small_rows % 16
    small_own = jnp.pad(small_own, (0, small_rows * quarter - small_own.shape[0])).reshape(small_rows, quarter)

    def attention_pack(qkv, out, more):
        return jnp.concatenate(
            [own_columns(qkv, here).reshape(3 * share, quarter), own_columns(out, here)] + more, axis=0
        )

    def ffn_pack(matrix_in, matrix_out):
        return jnp.concatenate([ffn_columns(matrix_in), ffn_rows(matrix_out)], axis=0)

    def attention_regions(extra):
        regions = [(i * share, (i + 1) * share, 0, quarter, 0, 0, i * quarter) for i in range(3)]
        regions.append((fixed - share, fixed, 0, quarter, 1, 0, 0))
        return regions + extra

    shapes = [(share, 3 * quarter), (share, quarter)]
    ffn_shapes = [(share, n * ffn_part), (ffn_part, dim)]
    ffn_regions = [
        (0, share, 0, dim, 0, 0, 0),
        (share, share + ffn_part, 0, dim, 1, 0, 0),
    ]
    pieces = ring_pieces(attention_pack(enc_qkv, enc_out, [small_own]), n)
    enc_wqkv, enc_wout, small_all = assemble(
        pieces,
        ring_index,
        attention_regions([(fixed, fixed + small_rows, 0, quarter, 2, 0, 0)]),
        shapes + [(small_rows, quarter)],
        n,
    )
    pieces = ring_pieces(ffn_pack(enc_ffn_in, enc_ffn_out), n)
    enc_win, enc_wback = assemble(pieces, ring_index, ffn_regions, ffn_shapes, n)
    half = share // 2
    rel_own = own_columns(dec_rel, here)
    rel_pack = jnp.concatenate([rel_own[:half], rel_own[half:]], axis=1)
    pieces = ring_pieces(attention_pack(dec_qkv, dec_out, [rel_pack]), n)
    dec_wqkv, dec_wout, dec_wrel = assemble(
        pieces,
        ring_index,
        attention_regions(
            [
                (fixed, fixed + half, 0, rel_part, 2, 0, 0),
                (fixed, fixed + half, rel_part, 2 * rel_part, 2, half, 0),
            ]
        ),
        shapes + [(share, rel_part)],
        n,
    )
    pieces = ring_pieces(ffn_pack(dec_ffn_in, dec_ffn_out), n)
    dec_win, dec_wback = assemble(pieces, ring_index, ffn_regions, ffn_shapes, n)

    small_all = small_all.reshape(n, -1).astype(F32)
    small_full = []
    offset = 0
    for arr in (enc_ffn_bias, enc_bias, enc_gain, enc_shift, dec_ffn_bias, dec_bias, dec_gain, dec_shift, dec_rel_bias):
        part = small_all[:, offset : offset + arr.size]
        offset += arr.size
        if arr.ndim == 1:
            small_full.append(part.reshape(-1))
        else:
            small_full.append(jnp.transpose(part.reshape((n,) + arr.shape), (1, 0, 2)).reshape(arr.shape[0], -1))

    def turn_out(columns):
        blocks = columns.reshape(dim, quarter)
        sent = [lax.dynamic_slice_in_dim(blocks, (here ^ j) * quarter, quarter, axis=0) for j in XOR]
        return jnp.concatenate(by_absolute(turn_blocks(sent), here), axis=1)

    def turn_out_back(grad):
        sent = [lax.dynamic_slice_in_dim(grad, (here ^ j) * quarter, quarter, axis=1) for j in XOR]
        return jnp.concatenate(by_absolute(turn_blocks(sent), here), axis=0).reshape(n, share, quarter)

    def layer(wqkv, wout, win, wback, bias_in, bias, gain, shift):
        w = Layer()
        w.qkv = wqkv.reshape(dim, 3 * quarter)
        w.out = turn_out(wout)
        w.ffn_in = win.reshape(dim, n * ffn_part)
        w.ffn_out = wback.reshape(n * ffn_part, dim)
        w.ffn_bias = lax.dynamic_slice_in_dim(
            bias_in.reshape(n, STREAMS, ffn_part), here, 1, axis=1
        ).reshape(-1)
        w.bias, w.gain, w.shift = bias, gain, shift
        mine = own_columns(bias, here)
        w.qkv_bias = jnp.concatenate([mine[0], jnp.zeros_like(mine[0]), mine[1]])
        return w

    enc = layer(enc_wqkv, enc_wout, enc_win, enc_wback, *small_full[:4])
    dec = layer(dec_wqkv, dec_wout, dec_win, dec_wback, *small_full[4:8])
    dec.rel = dec_wrel.reshape(dim, rel_part)
    dec.rel_bias = own_columns(small_full[8], here)

    enc_all = gather_rows(enc_input)
    enc_heads = (dot(enc_all, enc.qkv) + enc.qkv_bias).astype(BF)
    enc_context, enc_lse = attention_forward(meta, enc_heads)
    main_rows, enc_kept = forward_tail(enc_input.astype(F32), enc_context, enc)
    stream_inputs = (main_rows, pred_input[0].astype(F32), pred_input[1].astype(F32))
    stream_all = [gather_rows(low) for low in (main_rows.astype(BF), pred_input[0], pred_input[1])]
    heads = [(dot(low, dec.qkv) + dec.qkv_bias).astype(BF) for low in stream_all]
    rels = [dot(low, dec.rel) + dec.rel_bias for low in stream_all]
    contexts, lses, kept, outputs = [], [], [], []
    for i in range(3):
        context, lse = attention_forward(meta, heads[i], None if i == 0 else heads[0], rels[i], tables)
        output, keep = forward_tail(stream_inputs[i], context, dec)
        contexts.append(context)
        lses.append(lse)
        kept.append(keep)
        outputs.append(output)

    residuals, weight_grads, smalls, dheads, drels = [], [], [], [], []
    key_grad = val_grad = 0.0
    query_main = None
    for i in range(3):
        residual, dctx, weights, small = backward_tail(
            cotangent[i].astype(F32), contexts[i], kept[i], dec
        )
        result = attention_backward(
            meta, heads[i], dctx, lses[i], None if i == 0 else heads[0], rels[i], tables
        )
        key_grad = key_grad + result[1]
        val_grad = val_grad + result[2]
        drels.append(result[3])
        if i == 0:
            query_main = result[0]
            dheads.append(None)
        else:
            dheads.append(jnp.concatenate([result[0], result[4], result[5]], axis=1))
        residuals.append(residual)
        weight_grads.append(weights)
        smalls.append(small)
    dheads[0] = jnp.concatenate([query_main, key_grad.astype(BF), val_grad.astype(BF)], axis=1)
    input_grads = [
        residuals[i] + scatter_rows(dot_nt(dheads[i], dec.qkv) + dot_nt(drels[i], dec.rel)) for i in range(3)
    ]
    dec_qkv_part = sum(dot_tn(stream_all[i], dheads[i]) for i in range(3)).astype(BF)
    dec_rel_part = sum(dot_tn(stream_all[i], drels[i]) for i in range(3)).astype(BF)
    dec_out_part, dec_in_part, dec_back_part = [
        sum(weight_grads[i][k] for i in range(3)).astype(BF) for k in range(3)
    ]
    dec_small = [sum(smalls[i][k] for i in range(3)) for k in range(7)]
    head_sum = sum(jnp.sum(dheads[i].astype(F32), axis=0) for i in range(3))
    rel_sum = sum(jnp.sum(drels[i].astype(F32), axis=0) for i in range(3))

    def widen(part, size):
        return lax.dynamic_update_slice(jnp.zeros((size,), F32), part, (here * part.shape[0],))

    def small_pack(small, heads_grad, rel_grad=None):
        wide = jnp.stack([widen(heads_grad[:quarter], dim), widen(heads_grad[2 * quarter :], dim)] + list(small[1:]))
        parts = [
            jnp.transpose(wide.reshape(8, n, share), (1, 0, 2)).reshape(n, 8 * share),
            small[0].reshape(n, ffn_part),
        ]
        if rel_grad is not None:
            parts.append(widen(rel_grad, rel_all).reshape(n, rel_all // n))
        used = sum(p.shape[1] for p in parts)
        rows_used = -(-used // quarter)
        rows_used += -rows_used % 16
        parts.append(jnp.zeros((n, rows_used * quarter - used), F32))
        return jnp.concatenate(parts, axis=1).reshape(n, rows_used, quarter).astype(BF)

    def attention_sum(qkv_grad, out_grad, more):
        arrays = [qkv_grad.reshape(n, share, 3 * quarter)[:, :, i * quarter : (i + 1) * quarter] for i in range(3)]
        return ring_sum(arrays + [turn_out_back(out_grad)] + more, n, place)

    def ffn_sum(in_grad, back_grad):
        return ring_sum([in_grad.reshape(n, share, dim), back_grad.reshape(n, ffn_part, dim)], n, place)

    dec_ffn_sum = ffn_sum(dec_in_part, dec_back_part)
    rel_blocks = dec_rel_part.reshape(n, share, rel_part)
    dec_attention_sum = attention_sum(
        dec_qkv_part,
        dec_out_part,
        [
            jnp.concatenate([rel_blocks[:, :half], rel_blocks[:, half:]], axis=2),
            small_pack(dec_small, head_sum, rel_sum),
        ],
    )

    residual, dctx, enc_weights, enc_small = backward_tail(input_grads[0], enc_context, enc_kept, enc)
    dq, dk, dv = attention_backward(meta, enc_heads, dctx, enc_lse)
    enc_dheads = jnp.concatenate([dq, dk.astype(BF), dv.astype(BF)], axis=1)
    enc_input_grad = residual + scatter_rows(dot_nt(enc_dheads, enc.qkv))
    enc_ffn_sum = ffn_sum(enc_weights[1].astype(BF), enc_weights[2].astype(BF))
    enc_head_sum = jnp.sum(enc_dheads.astype(F32), axis=0)
    enc_attention_sum = attention_sum(
        dot_tn(enc_all, enc_dheads).astype(BF), enc_weights[0].astype(BF), [small_pack(enc_small, enc_head_sum)]
    )

    def spread(total_rows):
        low = total_rows.astype(BF)
        far = swap(low, 2)
        near = swap(jnp.stack([low, far]), 1)
        return by_absolute([low, far, near[0], near[1]], here)

    def attention_out(total_rows, with_rel):
        blocks = spread(total_rows)
        wide = jnp.concatenate([b[:fixed] for b in blocks], axis=1).astype(F32)
        qkv = wide[: 3 * share].reshape(3, share, dim)
        out = wide[3 * share :]
        at = fixed
        results = [qkv, out]
        if with_rel:
            parts = [
                jnp.concatenate([b[at : at + half, :rel_part], b[at : at + half, rel_part:]], axis=0) for b in blocks
            ]
            results.append(jnp.concatenate(parts, axis=1).astype(F32))
            at += half
        tiny = jnp.stack([b[at:] for b in blocks]).astype(F32).reshape(STREAMS, -1)
        inner = tiny[:, 8 * share : 8 * share + ffn_part].reshape(-1)
        summed = jnp.sum(tiny, axis=0)
        wide_sum = summed[: 8 * share].reshape(8, share)
        results += [inner, wide_sum[:4], wide_sum[4:6], wide_sum[6:8]]
        if with_rel:
            first = 8 * share + ffn_part
            results.append(summed[first : first + rel_all // n])
        return results

    def ffn_out(total_rows):
        blocks = spread(total_rows)
        grad_in = jnp.stack([b[:share].reshape(share, n, ffn_part) for b in blocks], axis=2)
        grad_out = jnp.concatenate([b[share:] for b in blocks], axis=0)
        return grad_in.reshape(share, ffn).astype(F32), grad_out.astype(F32)

    dec_in_grad, dec_back_grad = ffn_out(dec_ffn_sum)
    dec_qkv_grad, dec_out_grad, dec_rel_grad, *dec_tiny, dec_rel_bias_grad = attention_out(dec_attention_sum, True)
    enc_in_grad, enc_back_grad = ffn_out(enc_ffn_sum)
    enc_qkv_grad, enc_out_grad, *enc_tiny = attention_out(enc_attention_sum, False)

    return (
        jnp.stack(outputs),
        enc_input_grad,
        jnp.stack([input_grads[1], input_grads[2]]),
        enc_qkv_grad,
        enc_out_grad,
        enc_in_grad,
        enc_back_grad,
        *enc_tiny,
        dec_qkv_grad,
        dec_out_grad,
        dec_rel_grad,
        dec_rel_bias_grad,
        dec_in_grad,
        dec_back_grad,
        *dec_tiny,
    )


def solution(mesh):
    tokens = P(("stream", "dp"), None)
    streams = P(None, ("stream", "dp"), None)
    first, second, cube = P("dp", None), P(None, "dp"), P(None, "dp", None)
    flat = P("dp")
    return jax.shard_map(
        per_device,
        mesh=mesh,
        in_specs=(
            tokens, streams, streams, flat, first, P(),
            cube, first, first, first, flat, second, second, second,
            cube, first, first, flat, first, first, flat, second, second, second,
        ),
        out_specs=(
            streams, tokens, streams,
            cube, first, first, first, flat, second, second, second,
            cube, first, first, flat, first, first, flat, second, second, second,
        ),
        check_vma=False,
    )
```

```python
from functools import partial

import jax
import jax.numpy as jnp
from jax import lax
from jax.experimental import pallas as pl
from jax.experimental.pallas import tpu as pltpu
from jax.sharding import PartitionSpec as P

H = 16
NB = 32
HD = 64
EPSILON = 1e-05
MASKED = -1000000000.0
BF = jnp.bfloat16
F32 = jnp.float32
TILE = 128
STREAMS = 4
XOR = (0, 2, 1, 3)
VMEM_LIMIT = 16 * 1024 * 1024


def dot(a, b):
    return jnp.dot(a, b, preferred_element_type=F32)


def dot_nt(a, b):
    return lax.dot_general(a, b, (((1,), (1,)), ((), ())), preferred_element_type=F32)


def dot_tn(a, b):
    return lax.dot_general(a, b, (((0,), (0,)), ((), ())), preferred_element_type=F32)


def swap(values, bit):
    return lax.ppermute(values, "stream", [(i, i ^ bit) for i in range(STREAMS)])


def gather_halves(rows):
    half = jnp.concatenate([rows, swap(rows, 2)], axis=0)
    return half, swap(half, 1)


def scatter_rows(keep, near):
    n = keep.shape[0] // 2
    near = swap(near, 1)
    far = swap((keep[n:] + near[n:].astype(F32)).astype(BF), 2)
    return keep[:n] + near[:n].astype(F32), far


def scatter_dots(partials):
    n = partials.shape[0] // 2
    return scatter_rows(partials[:n], partials[n:].astype(BF))


def turn_blocks(blocks):
    far = swap(jnp.stack([blocks[1], blocks[3]]), 2)
    near = swap(jnp.stack([blocks[2], far[1]]), 1)
    return [blocks[0], far[0], near[0], near[1]]


def by_absolute(blocks, here):
    stacked = jnp.stack([blocks[XOR.index(j)] for j in range(4)])
    return [lax.dynamic_index_in_dim(stacked, here ^ a, 0, keepdims=False) for a in range(4)]


def ring_order(n):
    return list(range(0, n, 2)) + list(range(n - 1, 0, -2))


def ring_member(place, n):
    place = lax.rem(place + 2 * n, n)
    return jnp.where(place < n // 2, 2 * place, 2 * (n - place) - 1)


def ring_place(g, n):
    return jnp.where(g % 2 == 0, g // 2, n - (g + 1) // 2)


def ring_step(values, n, step):
    order = ring_order(n)
    pairs = [(order[i], order[(i + step) % n]) for i in range(n)]
    return lax.ppermute(values, "dp", pairs)


def ring_pieces(own, n):
    rows = own.shape[0]
    pieces = [(0, 0, own)]
    ahead = back = own
    for k in range(1, n // 2):
        ahead = ring_step(ahead, n, 1)
        back = ring_step(back, n, -1)
        pieces += [(k, 0, ahead), (n - k, 0, back)]
    half = halved(rows)
    top = ring_step(ahead[:half], n, 1)
    bottom = ring_step(back[half:], n, -1)
    pieces += [(n // 2, 0, top), (n // 2, half, bottom)]
    return pieces


def assemble(pieces, index, regions, shapes, n):
    moves = []
    for number, (behind, first, piece) in enumerate(pieces):
        last = first + piece.shape[0]
        for r0, r1, c0, c1, which, to_row, to_col in regions:
            lo, hi = max(r0, first), min(r1, last)
            if lo < hi:
                moves.append((number, behind, lo - first, hi - first, c0, c1, which, to_row + lo - r0, to_col))

    def kernel(index_ref, *refs):
        sources = refs[: len(pieces)]
        outs = refs[len(pieces) :]
        for number, behind, lo, hi, c0, c1, which, row, col in moves:
            g = index_ref[behind]
            outs[which][g, row : row + hi - lo, col : col + c1 - c0] = sources[number][lo:hi, c0:c1]

    vmem = pl.BlockSpec(memory_space=pltpu.VMEM)
    return pl.pallas_call(
        kernel,
        out_shape=[jax.ShapeDtypeStruct((n,) + shape, BF) for shape in shapes],
        in_specs=[pl.BlockSpec(memory_space=pltpu.SMEM)] + [vmem] * len(pieces),
        out_specs=[vmem] * len(shapes),
        compiler_params=pltpu.CompilerParams(vmem_limit_bytes=VMEM_LIMIT),
    )(index, *[piece for _, _, piece in pieces])


def halved(rows):
    return rows // 32 * 16


def ring_sum(arrays, n, place):
    def part(ahead):
        g = ring_member(place + ahead, n)
        return jnp.concatenate(
            [lax.dynamic_index_in_dim(a, g, 0, keepdims=False) for a in arrays], axis=0
        ).astype(F32)

    middle = part(n // 2)
    half = halved(middle.shape[0])
    up = ring_step(middle[:half].astype(BF), n, 1).astype(F32)
    down = ring_step(middle[half:].astype(BF), n, -1).astype(F32)
    for k in range(n // 2 - 1, 0, -1):
        ahead, back = part(k), part(-k)
        if k == n // 2 - 1:
            ahead = jnp.concatenate([ahead[:half] + up, ahead[half:]], axis=0)
            back = jnp.concatenate([back[:half], back[half:] + down], axis=0)
        else:
            ahead, back = ahead + up, back + down
        up = ring_step(ahead.astype(BF), n, 1).astype(F32)
        down = ring_step(back.astype(BF), n, -1).astype(F32)
    return part(0) + up + down


def tile_width(t, causal, total):
    return TILE * (t + 1) if causal else total


def head_mask(e):
    lane = lax.broadcasted_iota(jnp.int32, (1, TILE), 1)
    return ((lane // HD) == e).astype(F32)


def rel_mask(h):
    lane = lax.broadcasted_iota(jnp.int32, (1, TILE), 1)
    return ((lane // NB) == h).astype(F32)


def allowed_keys(t, width, meta, causal, strict):
    bucket = meta[8]
    shape = (TILE, width)
    row = lax.broadcasted_iota(jnp.int32, shape, 0) + t * TILE
    col = lax.broadcasted_iota(jnp.int32, shape, 1)
    pos = col & (bucket - 1)
    first = col < bucket
    limit = bucket - jnp.where(first, meta[9], meta[10])
    allowed = (pos < limit) & ((row < bucket) == first)
    if causal:
        allowed = allowed & ((col < row) if strict else (col <= row))
    return allowed


def load_rows(meta, target, source, c0, c1):
    for chunk in range(8):
        start = pl.multiple_of(meta[chunk], 64)
        target[pl.ds(start, 64), :] = source[chunk * 64 : chunk * 64 + 64, c0:c1]


def store_rows(meta, target, source, c0, c1):
    for chunk in range(8):
        start = pl.multiple_of(meta[chunk], 64)
        target[chunk * 64 : chunk * 64 + 64, c0:c1] = source[pl.ds(start, 64), :].astype(target.dtype)


def rel_bias(rel_rows, h, table):
    high = rel_rows.astype(BF)
    rest = (rel_rows - high.astype(F32)).astype(BF)
    mask = rel_mask(h)
    both = jnp.concatenate(
        [(high.astype(F32) * mask).astype(BF), (rest.astype(F32) * mask).astype(BF)], axis=1
    )
    spread = dot(both, table)
    return pltpu.roll(spread, 0, 1, stride=1, stride_axis=0)


def table_slice(t, width):
    first = sum(TILE * (u + 1) for u in range(t))
    return slice(first, first + width)


def attention_forward(meta, qkv, main=None, rel=None, tables=None):
    total = qkv.shape[0]
    width_all = qkv.shape[1] // 3
    heads = width_all // HD
    causal = rel is not None
    own = main is not None

    def kernel(meta_ref, *refs):
        refs = list(refs)
        qkv_ref = refs.pop(0)
        main_ref = refs.pop(0) if own else qkv_ref
        rel_ref, table_ref, hot_ref = (refs.pop(0), refs.pop(0), refs.pop(0)) if causal else (None,) * 3
        ctx_ref, lse_ref, qs, ks, vs, cs, kt = refs[:7]
        refs = refs[7:]
        rs = refs.pop(0) if causal else None
        load_rows(meta_ref, qs, qkv_ref, 0, width_all)
        load_rows(meta_ref, ks, main_ref, width_all, 2 * width_all)
        load_rows(meta_ref, vs, main_ref, 2 * width_all, 3 * width_all)
        if causal:
            load_rows(meta_ref, rs, rel_ref, 0, rel.shape[1])
        if own:
            kn, vn = refs
            load_rows(meta_ref, kn, qkv_ref, width_all, 2 * width_all)
            load_rows(meta_ref, vn, qkv_ref, 2 * width_all, 3 * width_all)
        kt[...] = ks[...].T
        for t in range(total // TILE):
            rows = slice(TILE * t, TILE * (t + 1))
            width = tile_width(t, causal, total)
            allowed = allowed_keys(t, width, meta_ref, causal, own)
            lse_lane = lax.broadcasted_iota(jnp.int32, (TILE, TILE), 1)
            lse = jnp.zeros((TILE, TILE), F32)
            query = [(qs[rows, HD * h : HD * (h + 1)].astype(F32) * HD**-0.5).astype(BF) for h in range(heads)]
            scores = [dot(query[h], kt[HD * h : HD * (h + 1), 0:width]) for h in range(heads)]
            if causal:
                biases = [rel_bias(rs[rows, :], h, table_ref[:, table_slice(t, width)]) for h in range(heads)]
                scores = [a + b for a, b in zip(scores, biases)]
            scores = [jnp.where(allowed, a, MASKED) for a in scores]
            tops = [jnp.max(a, axis=1, keepdims=True) for a in scores]
            if own:
                own_scores = [
                    jnp.sum(
                        query[h].astype(F32) * kn[rows, HD * h : HD * (h + 1)].astype(F32), axis=1, keepdims=True
                    )
                    + jnp.sum(rs[rows, :] * (hot_ref[...] * rel_mask(h)), axis=1, keepdims=True)
                    for h in range(heads)
                ]
                tops = [jnp.maximum(a, b) for a, b in zip(tops, own_scores)]
            expos = [jnp.exp(a - b) for a, b in zip(scores, tops)]
            sums = [jnp.sum(a, axis=1, keepdims=True) for a in expos]
            if own:
                own_expos = [jnp.exp(a - b) for a, b in zip(own_scores, tops)]
                sums = [a + b for a, b in zip(sums, own_expos)]
            inverses = [1.0 / a for a in sums]
            parts = [
                dot((expos[h] * inverses[h]).astype(BF), vs[0:width, HD * h : HD * (h + 1)]) for h in range(heads)
            ]
            if own:
                parts = [
                    parts[h] + (own_expos[h] * inverses[h]) * vn[rows, HD * h : HD * (h + 1)].astype(F32)
                    for h in range(heads)
                ]
            cs[rows, :] = jnp.concatenate(parts, axis=1).astype(BF)
            for h in range(heads):
                lse = jnp.where(lse_lane == h, tops[h] + jnp.log(sums[h]), lse)
            lse_ref[rows, :] = lse
        store_rows(meta_ref, ctx_ref, cs, 0, width_all)

    vmem = pl.BlockSpec(memory_space=pltpu.VMEM)
    args = [qkv]
    scratch = [pltpu.VMEM((total, width_all), BF) for _ in range(4)] + [pltpu.VMEM((width_all, total), BF)]
    if own:
        args.append(main)
    if causal:
        args += [rel, tables[0], tables[2]]
        scratch.append(pltpu.VMEM((total, rel.shape[1]), F32))
    if own:
        scratch += [pltpu.VMEM((total, width_all), BF) for _ in range(2)]
    return pl.pallas_call(
        kernel,
        out_shape=(
            jax.ShapeDtypeStruct((total, width_all), BF),
            jax.ShapeDtypeStruct((total, TILE), F32),
        ),
        in_specs=[pl.BlockSpec(memory_space=pltpu.SMEM)] + [vmem] * len(args),
        out_specs=(vmem, vmem),
        scratch_shapes=scratch,
        compiler_params=pltpu.CompilerParams(vmem_limit_bytes=VMEM_LIMIT),
    )(meta, *args)


def attention_backward(meta, qkv, dctx, lse, main=None, rel=None, tables=None):
    total = qkv.shape[0]
    width_all = qkv.shape[1] // 3
    heads = width_all // HD
    causal = rel is not None
    own = main is not None

    def kernel(meta_ref, *refs):
        refs = list(refs)
        qkv_ref, dctx_ref, lse_ref = refs[:3]
        refs = refs[3:]
        main_ref = refs.pop(0) if own else qkv_ref
        rel_ref, table_ref, back_ref, hot_ref, flip_ref = (
            [refs.pop(0) for _ in range(5)] if causal else (None,) * 5
        )
        dq_ref, dk_ref, dv_ref = refs[:3]
        refs = refs[3:]
        drel_ref = refs.pop(0) if causal else None
        dkn_ref, dvn_ref = (refs.pop(0), refs.pop(0)) if own else (None, None)
        qs, ks, vs, gs, dqs, dks, kt, vt, qt, gt, dkt, dvt = refs[:12]
        refs = refs[12:]
        rs, drs = (refs.pop(0), refs.pop(0)) if causal else (None, None)
        load_rows(meta_ref, qs, qkv_ref, 0, width_all)
        load_rows(meta_ref, ks, main_ref, width_all, 2 * width_all)
        load_rows(meta_ref, vs, main_ref, 2 * width_all, 3 * width_all)
        load_rows(meta_ref, gs, dctx_ref, 0, width_all)
        if causal:
            load_rows(meta_ref, rs, rel_ref, 0, rel.shape[1])
        if own:
            kn, vn, dkn, dvn = refs
            load_rows(meta_ref, kn, qkv_ref, width_all, 2 * width_all)
            load_rows(meta_ref, vn, qkv_ref, 2 * width_all, 3 * width_all)
        qs[...] = (qs[...].astype(F32) * HD**-0.5).astype(BF)
        kt[...] = ks[...].T
        vt[...] = vs[...].T
        qt[...] = qs[...].T
        gt[...] = gs[...].T
        dkt[...] = jnp.zeros_like(dkt)
        dvt[...] = jnp.zeros_like(dvt)
        each = range(heads)
        feat = [slice(HD * h, HD * (h + 1)) for h in each]
        for t in range(total // TILE):
            rows = slice(TILE * t, TILE * (t + 1))
            width = tile_width(t, causal, total)
            allowed = allowed_keys(t, width, meta_ref, causal, own)
            norms = [lse_ref[rows, h : h + 1] for h in each]
            query = [qs[rows, feat[h]] for h in each]
            grad = [gs[rows, feat[h]] for h in each]
            scores = [dot(query[h], kt[feat[h], 0:width]) for h in each]
            dprobs = [dot(grad[h], vt[feat[h], 0:width]) for h in each]
            if causal:
                biases = [rel_bias(rs[rows, :], h, table_ref[:, table_slice(t, width)]) for h in each]
                scores = [a + b for a, b in zip(scores, biases)]
            probs = [jnp.exp(jnp.where(allowed, scores[h], MASKED) - norms[h]) for h in each]
            rowdots = [jnp.sum(probs[h] * dprobs[h], axis=1, keepdims=True) for h in each]
            if own:
                own_keys = [kn[rows, feat[h]].astype(F32) for h in each]
                own_scores = [
                    jnp.sum(query[h].astype(F32) * own_keys[h], axis=1, keepdims=True)
                    + jnp.sum(rs[rows, :] * (hot_ref[...] * rel_mask(h)), axis=1, keepdims=True)
                    for h in each
                ]
                own_probs = [jnp.exp(own_scores[h] - norms[h]) for h in each]
                own_dprobs = [
                    jnp.sum(grad[h].astype(F32) * vn[rows, feat[h]].astype(F32), axis=1, keepdims=True) for h in each
                ]
                rowdots = [rowdots[h] + own_probs[h] * own_dprobs[h] for h in each]
                own_dscores = [
                    (own_probs[h] * (own_dprobs[h] - rowdots[h])).astype(BF).astype(F32) for h in each
                ]
            dscores = [(probs[h] * (dprobs[h] - rowdots[h])).astype(BF) for h in each]
            dqs_parts = [dot(dscores[h], ks[0:width, feat[h]]) for h in each]
            if own:
                dqs_parts = [dqs_parts[h] + own_dscores[h] * own_keys[h] for h in each]
                dkn[rows, :] = jnp.concatenate([own_dscores[h] * query[h].astype(F32) for h in each], axis=1)
                dvn[rows, :] = jnp.concatenate([own_probs[h] * grad[h].astype(F32) for h in each], axis=1)
            dqs[rows, :] = jnp.concatenate(dqs_parts, axis=1) * HD**-0.5
            for h in each:
                dkt[feat[h], 0:width] += dot(qt[feat[h], rows], dscores[h])
                dvt[feat[h], 0:width] += dot(gt[feat[h], rows], probs[h].astype(BF))
            if causal:
                drel = jnp.zeros((TILE, TILE), F32)
                for h in each:
                    blocks = [
                        dot(dscores[h][:, TILE * b : TILE * (b + 1)], flip_ref[...])
                        for b in reversed(range(width // TILE))
                    ]
                    mirrored = jnp.concatenate(blocks, axis=1) if len(blocks) > 1 else blocks[0]
                    turned = pltpu.roll(mirrored, 0, 1, stride=1, stride_axis=0).astype(BF)
                    drel = drel + dot(turned, back_ref[table_slice(t, width), :]) * rel_mask(h)
                    if own:
                        drel = drel + own_dscores[h] * (hot_ref[...] * rel_mask(h))
                drs[rows, :] = drel
        store_rows(meta_ref, dq_ref, dqs, 0, width_all)
        dks[...] = dkt[...].T
        store_rows(meta_ref, dk_ref, dks, 0, width_all)
        dks[...] = dvt[...].T
        store_rows(meta_ref, dv_ref, dks, 0, width_all)
        if causal:
            store_rows(meta_ref, drel_ref, drs, 0, rel.shape[1])
        if own:
            store_rows(meta_ref, dkn_ref, dkn, 0, width_all)
            store_rows(meta_ref, dvn_ref, dvn, 0, width_all)

    vmem = pl.BlockSpec(memory_space=pltpu.VMEM)
    args = [qkv, dctx, lse]
    shape = (total, width_all)
    turned = (width_all, total)
    outs = [jax.ShapeDtypeStruct(shape, BF), jax.ShapeDtypeStruct(shape, F32), jax.ShapeDtypeStruct(shape, F32)]
    scratch = [pltpu.VMEM(shape, BF) for _ in range(4)] + [pltpu.VMEM(shape, F32) for _ in range(2)]
    scratch += [pltpu.VMEM(turned, BF) for _ in range(4)] + [pltpu.VMEM(turned, F32) for _ in range(2)]
    if own:
        args.append(main)
    if causal:
        args += [rel, tables[0], tables[1], tables[2], tables[3]]
        outs.append(jax.ShapeDtypeStruct((total, rel.shape[1]), BF))
        scratch += [pltpu.VMEM((total, rel.shape[1]), F32) for _ in range(2)]
    if own:
        outs += [jax.ShapeDtypeStruct(shape, BF) for _ in range(2)]
        scratch += [pltpu.VMEM(shape, BF) for _ in range(2)] + [pltpu.VMEM(shape, F32) for _ in range(2)]
    return pl.pallas_call(
        kernel,
        out_shape=outs,
        in_specs=[pl.BlockSpec(memory_space=pltpu.SMEM)] + [vmem] * len(args),
        out_specs=[vmem] * len(outs),
        scratch_shapes=scratch,
        compiler_params=pltpu.CompilerParams(vmem_limit_bytes=VMEM_LIMIT),
    )(meta, *args)


def rel_tables(rel_table, total):
    ahead, back = [], []
    for t in range(total // TILE):
        width = TILE * (t + 1)
        here = rel_table[:width]
        ahead += [jnp.flip(here[: TILE * t + 1]), jnp.flip(here[TILE * t + 1 :])]
        back += [here[width - TILE + 1 :], here[: width - TILE + 1]]
    ahead, back = jnp.concatenate(ahead), jnp.concatenate(back)
    rows = jnp.arange(2 * TILE, dtype=jnp.int32) % NB
    forward = (rows[:, None] == ahead[None, :]).astype(BF)
    backward = (back[:, None] == rows[None, :TILE]).astype(BF)
    hot = (rows[None, :TILE] == rel_table[0]).astype(F32)
    ids = jnp.arange(TILE, dtype=jnp.int32)
    flip = (ids[:, None] + ids[None, :] == TILE - 1).astype(BF)
    return forward, backward, hot, flip


def whole(kernel, outs, *args):
    vmem = pl.BlockSpec(memory_space=pltpu.VMEM)
    return pl.pallas_call(
        kernel,
        out_shape=[jax.ShapeDtypeStruct(shape, kind) for shape, kind in outs],
        in_specs=[vmem] * len(args),
        out_specs=[vmem] * len(outs),
        compiler_params=pltpu.CompilerParams(vmem_limit_bytes=VMEM_LIMIT),
    )(*args)


def unit_of(values):
    center = values - jnp.mean(values, axis=-1, keepdims=True)
    spread = jnp.mean(center * center, axis=-1, keepdims=True)
    inverse = lax.rsqrt(spread + EPSILON)
    return center * inverse, inverse


def unit_back(grad, unit, inverse, gain):
    inner = grad * gain
    mean = jnp.mean(inner, axis=-1, keepdims=True)
    along = jnp.mean(inner * unit, axis=-1, keepdims=True)
    return inverse * (inner - mean - unit * along)


def column(values):
    return jnp.sum(values, axis=0, keepdims=True)


def norm_first(inputs, keep, far, w):
    rows, dim = inputs.shape

    def kernel(in_ref, keep_ref, far_ref, small_ref, unit_ref, inverse_ref, low_ref):
        values = in_ref[...].astype(F32) + keep_ref[...] + far_ref[...].astype(F32) + small_ref[2:3, :]
        unit, inverse = unit_of(values)
        unit_ref[...] = unit
        inverse_ref[...] = inverse
        low_ref[...] = (unit * small_ref[4:5, :] + small_ref[6:7, :]).astype(BF)

    return whole(kernel, [((rows, dim), F32), ((rows, 1), F32), ((rows, dim), BF)], inputs, keep, far, w.small)


def norm_second(unit0, keep, far, w):
    rows, dim = unit0.shape

    def kernel(unit_ref, keep_ref, far_ref, small_ref, unit1_ref, inverse_ref, out_ref, low_ref):
        hidden = unit_ref[...] * small_ref[4:5, :] + small_ref[6:7, :]
        unit, inverse = unit_of(hidden + keep_ref[...] + far_ref[...].astype(F32) + small_ref[3:4, :])
        out = unit * small_ref[5:6, :] + small_ref[7:8, :]
        unit1_ref[...] = unit
        inverse_ref[...] = inverse
        out_ref[...] = out
        low_ref[...] = out.astype(BF)

    outs = [((rows, dim), F32), ((rows, 1), F32), ((rows, dim), F32), ((rows, dim), BF)]
    return whole(kernel, outs, unit0, keep, far, w.small)


def norm_second_back(residual, keep, far, unit1, inverse, w):
    rows, dim = residual.shape

    def kernel(res_ref, keep_ref, far_ref, unit_ref, inverse_ref, small_ref, sum_ref, low_ref, tiny_ref):
        grad = res_ref[...] + keep_ref[...] + far_ref[...].astype(F32)
        unit = unit_ref[...]
        back = unit_back(grad, unit, inverse_ref[...], small_ref[5:6, :])
        low = back.astype(BF)
        sum_ref[...] = back
        low_ref[...] = low
        tiny_ref[...] = jnp.concatenate([column(low.astype(F32)), column(grad * unit), column(grad)], axis=0)

    outs = [((rows, dim), F32), ((rows, dim), BF), ((3, dim), F32)]
    return whole(kernel, outs, residual, keep, far, unit1, inverse, w.small)


def norm_second_both(unit0, keep, far, cotangent, w):
    rows, dim = unit0.shape

    def kernel(unit_ref, keep_ref, far_ref, cot_ref, small_ref, out_ref, sum_ref, low_ref, tiny_ref):
        hidden = unit_ref[...] * small_ref[4:5, :] + small_ref[6:7, :]
        unit, inverse = unit_of(hidden + keep_ref[...] + far_ref[...].astype(F32) + small_ref[3:4, :])
        out_ref[...] = unit * small_ref[5:6, :] + small_ref[7:8, :]
        grad = cot_ref[...].astype(F32)
        back = unit_back(grad, unit, inverse, small_ref[5:6, :])
        low = back.astype(BF)
        sum_ref[...] = back
        low_ref[...] = low
        tiny_ref[...] = jnp.concatenate([column(low.astype(F32)), column(grad * unit), column(grad)], axis=0)

    outs = [((rows, dim), F32), ((rows, dim), F32), ((rows, dim), BF), ((3, dim), F32)]
    return whole(kernel, outs, unit0, keep, far, cotangent, w.small)


def norm_first_back(sum_grad, keep, far, unit0, inverse, w):
    rows, dim = sum_grad.shape

    def kernel(sum_ref, keep_ref, far_ref, unit_ref, inverse_ref, small_ref, out_ref, low_ref, tiny_ref):
        grad = sum_ref[...] + keep_ref[...] + far_ref[...].astype(F32)
        unit = unit_ref[...]
        back = unit_back(grad, unit, inverse_ref[...], small_ref[4:5, :])
        low = back.astype(BF)
        out_ref[...] = back
        low_ref[...] = low
        tiny_ref[...] = jnp.concatenate([column(low.astype(F32)), column(grad * unit), column(grad)], axis=0)

    outs = [((rows, dim), F32), ((rows, dim), BF), ((3, dim), F32)]
    return whole(kernel, outs, sum_grad, keep, far, unit0, inverse, w.small)


def gelu_and_slope(x):
    bell = jnp.exp(-0.5 * x * x)
    under = 1.0 + (0.3275911 * 0.5**0.5) * jnp.abs(x)
    t = pl.reciprocal(under, approx=True)
    t = t * (2.0 - under * t)
    series = ((((1.061405429 * t - 1.453152027) * t + 1.421413741) * t - 0.284496736) * t + 0.254829592) * t
    tail = (0.5 * series) * bell
    below = jnp.where(x >= 0.0, 1.0 - tail, tail)
    return x * below, below + x * bell * 0.3989422804014327


FFN_TILE = 256


def ffn_forward(near_half, far_half, w):
    half, dim = near_half.shape
    units = w.ffn_in.shape[1]

    def kernel(a_ref, b_ref, in_ref, out_ref, bias_ref, keep_ref, near_ref, act_ref, slope_ref):
        for part, rows_ref in enumerate((a_ref, b_ref)):
            rows = slice(part * half, (part + 1) * half)
            for u in range(0, units, FFN_TILE):
                tile = slice(u, u + FFN_TILE)
                active, slope = gelu_and_slope(dot(rows_ref[...], in_ref[:, tile]) + bias_ref[:, tile])
                act_ref[rows, tile] = active.astype(BF)
                slope_ref[rows, tile] = slope.astype(BF)
            branch = dot(act_ref[rows, :], out_ref[...])
            if part == 0:
                keep_ref[...] = branch
            else:
                near_ref[...] = branch.astype(BF)

    outs = [((half, dim), F32), ((half, dim), BF), ((2 * half, units), BF), ((2 * half, units), BF)]
    return whole(kernel, outs, near_half, far_half, w.ffn_in, w.ffn_out, w.ffn_bias)


def ffn_backward(near_half, far_half, slope, w):
    half, dim = near_half.shape
    units = w.ffn_in.shape[1]

    def kernel(a_ref, b_ref, in_ref, out_ref, slope_ref, keep_ref, near_ref, inner_ref):
        for part, rows_ref in enumerate((a_ref, b_ref)):
            rows = slice(part * half, (part + 1) * half)
            for u in range(0, units, FFN_TILE):
                tile = slice(u, u + FFN_TILE)
                back = dot_nt(rows_ref[...], out_ref[tile, :])
                inner_ref[rows, tile] = (back * slope_ref[rows, tile].astype(F32)).astype(BF)
            hidden = dot_nt(inner_ref[rows, :], in_ref[...])
            if part == 0:
                keep_ref[...] = hidden
            else:
                near_ref[...] = hidden.astype(BF)

    outs = [((half, dim), F32), ((half, dim), BF), ((2 * half, units), BF)]
    return whole(kernel, outs, near_half, far_half, w.ffn_in, w.ffn_out, slope)


class Layer:
    pass


def own_columns(matrix, here):
    width = matrix.shape[-1] // STREAMS
    return lax.dynamic_slice_in_dim(matrix, here * width, width, axis=matrix.ndim - 1)


def forward_tail(inputs, context, w):
    keep, far = scatter_dots(dot(context, w.out))
    unit0, inverse0, low = norm_first(inputs, keep, far, w)
    halves = gather_halves(low)
    keep, near, active, slope = ffn_forward(*halves, w)
    return scatter_rows(keep, near), (unit0, inverse0, halves, active, slope)


def backward_tail(sum_grad, low, kept, context, w):
    unit0, inverse0, halves, active, slope = kept
    branch = gather_halves(low)
    keep, near, inner = ffn_backward(*branch, slope, w)
    keep, far = scatter_rows(keep, near)
    input_grad, attended_low, tiny = norm_first_back(sum_grad, keep, far, unit0, inverse0, w)
    attended = jnp.concatenate(gather_halves(attended_low), axis=0)
    context_grad = dot_nt(attended, w.out).astype(BF)
    weight_grads = (
        dot_tn(context, attended),
        dot_tn(jnp.concatenate(halves, axis=0), inner),
        dot_tn(active, jnp.concatenate(branch, axis=0)),
        jnp.sum(inner.astype(F32), axis=0),
    )
    return input_grad, context_grad, weight_grads, tiny


def per_device(
    enc_input, pred_input, cotangent, bucket_len, pad_len, rel_table,
    enc_qkv, enc_out, enc_ffn_in, enc_ffn_out, enc_ffn_bias, enc_bias, enc_gain, enc_shift,
    dec_qkv, dec_out, dec_rel, dec_rel_bias, dec_ffn_in, dec_ffn_out, dec_ffn_bias, dec_bias, dec_gain, dec_shift,
):
    here = lax.axis_index("stream")
    n = lax.axis_size("dp")
    group = lax.axis_index("dp")
    place = ring_place(group, n)
    rows = enc_input.shape[0]
    total = STREAMS * rows
    dim = enc_input.shape[1]
    share = enc_out.shape[0]
    quarter = dim // STREAMS
    ffn = enc_ffn_in.shape[1]
    ffn_share = enc_ffn_out.shape[0]
    ffn_part = ffn_share // STREAMS
    rel_all = dec_rel.shape[1]
    rel_part = rel_all // STREAMS

    bucket = bucket_len[0]
    starts = []
    for j in XOR:
        holder = here ^ j
        for chunk in range(2):
            starts.append(jnp.where(bucket == total, holder * rows + chunk * 64, chunk * bucket + holder * 64))
    meta = jnp.stack([v.astype(jnp.int32) for v in starts + [bucket, pad_len[0, 0], pad_len[0, 1]]])
    tables = rel_tables(rel_table, total)
    ring_index = jnp.stack([ring_member(place - o, n) for o in range(n)]).astype(jnp.int32)

    def ffn_columns(matrix):
        blocks = matrix.reshape(matrix.shape[0], n, ffn_share)
        part = lax.dynamic_slice_in_dim(blocks, here * ffn_part, ffn_part, axis=2)
        return part.reshape(matrix.shape[0], n * ffn_part)

    def ffn_rows(matrix):
        return lax.dynamic_slice_in_dim(matrix, here * ffn_part, ffn_part, axis=0)

    smalls = [
        a.reshape(-1)
        for a in (
            enc_ffn_bias, enc_bias, enc_gain, enc_shift, dec_ffn_bias, dec_bias, dec_gain, dec_shift, dec_rel_bias
        )
    ]
    small_own = jnp.concatenate(smalls)
    fixed = 4 * share
    small_rows = -(-small_own.shape[0] // quarter)
    small_rows += -small_rows % 16
    small_own = jnp.pad(small_own, (0, small_rows * quarter - small_own.shape[0])).reshape(small_rows, quarter)

    def attention_pack(qkv, out, more):
        return jnp.concatenate(
            [own_columns(qkv, here).reshape(3 * share, quarter), own_columns(out, here)] + more, axis=0
        )

    def ffn_pack(matrix_in, matrix_out):
        return jnp.concatenate([ffn_columns(matrix_in), ffn_rows(matrix_out)], axis=0)

    def attention_regions(extra):
        regions = [(i * share, (i + 1) * share, 0, quarter, 0, 0, i * quarter) for i in range(3)]
        regions.append((fixed - share, fixed, 0, quarter, 1, 0, 0))
        return regions + extra

    shapes = [(share, 3 * quarter), (share, quarter)]
    ffn_shapes = [(share, n * ffn_part), (ffn_part, dim)]
    ffn_regions = [
        (0, share, 0, dim, 0, 0, 0),
        (share, share + ffn_part, 0, dim, 1, 0, 0),
    ]
    pieces = ring_pieces(attention_pack(enc_qkv, enc_out, [small_own]), n)
    enc_wqkv, enc_wout, small_all = assemble(
        pieces,
        ring_index,
        attention_regions([(fixed, fixed + small_rows, 0, quarter, 2, 0, 0)]),
        shapes + [(small_rows, quarter)],
        n,
    )
    pieces = ring_pieces(ffn_pack(enc_ffn_in, enc_ffn_out), n)
    enc_win, enc_wback = assemble(pieces, ring_index, ffn_regions, ffn_shapes, n)
    half = share // 2
    rel_own = own_columns(dec_rel, here)
    rel_pack = jnp.concatenate([rel_own[:half], rel_own[half:]], axis=1)
    pieces = ring_pieces(attention_pack(dec_qkv, dec_out, [rel_pack]), n)
    dec_wqkv, dec_wout, dec_wrel = assemble(
        pieces,
        ring_index,
        attention_regions(
            [
                (fixed, fixed + half, 0, rel_part, 2, 0, 0),
                (fixed, fixed + half, rel_part, 2 * rel_part, 2, half, 0),
            ]
        ),
        shapes + [(share, rel_part)],
        n,
    )
    pieces = ring_pieces(ffn_pack(dec_ffn_in, dec_ffn_out), n)
    dec_win, dec_wback = assemble(pieces, ring_index, ffn_regions, ffn_shapes, n)

    small_all = small_all.reshape(n, -1).astype(F32)
    small_full = []
    offset = 0
    for arr in (enc_ffn_bias, enc_bias, enc_gain, enc_shift, dec_ffn_bias, dec_bias, dec_gain, dec_shift, dec_rel_bias):
        part = small_all[:, offset : offset + arr.size]
        offset += arr.size
        if arr.ndim == 1:
            small_full.append(part.reshape(-1))
        else:
            small_full.append(jnp.transpose(part.reshape((n,) + arr.shape), (1, 0, 2)).reshape(arr.shape[0], -1))

    def turn_out(columns):
        blocks = columns.reshape(dim, quarter)
        sent = [lax.dynamic_slice_in_dim(blocks, (here ^ j) * quarter, quarter, axis=0) for j in XOR]
        return jnp.concatenate(by_absolute(turn_blocks(sent), here), axis=1)

    def turn_out_back(grad):
        sent = [lax.dynamic_slice_in_dim(grad, (here ^ j) * quarter, quarter, axis=1) for j in XOR]
        return jnp.concatenate(by_absolute(turn_blocks(sent), here), axis=0).reshape(n, share, quarter)

    def layer(wqkv, wout, win, wback, bias_in, bias, gain, shift):
        w = Layer()
        w.qkv = wqkv.reshape(dim, 3 * quarter)
        w.out = turn_out(wout)
        w.ffn_in = win.reshape(dim, n * ffn_part)
        w.ffn_out = wback.reshape(n * ffn_part, dim)
        w.ffn_bias = lax.dynamic_slice_in_dim(
            bias_in.reshape(n, STREAMS, ffn_part), here, 1, axis=1
        ).reshape(1, -1)
        w.small = jnp.concatenate([bias, gain, shift], axis=0)
        mine = own_columns(bias, here)
        w.qkv_bias = jnp.concatenate([mine[0], jnp.zeros_like(mine[0]), mine[1]])
        return w

    enc = layer(enc_wqkv, enc_wout, enc_win, enc_wback, *small_full[:4])
    dec = layer(dec_wqkv, dec_wout, dec_win, dec_wback, *small_full[4:8])
    dec.rel = dec_wrel.reshape(dim, rel_part)
    dec.rel_bias = own_columns(small_full[8], here)

    enc_all = jnp.concatenate(gather_halves(enc_input), axis=0)
    enc_heads = (dot(enc_all, enc.qkv) + enc.qkv_bias).astype(BF)
    enc_context, enc_lse = attention_forward(meta, enc_heads)
    branch, enc_kept = forward_tail(enc_input, enc_context, enc)
    enc_unit1, enc_inverse1, main_rows, main_low = norm_second(enc_kept[0], *branch, enc)
    stream_inputs = (main_rows, pred_input[0], pred_input[1])
    stream_all = [
        jnp.concatenate(gather_halves(low), axis=0) for low in (main_low, pred_input[0], pred_input[1])
    ]
    heads = [(dot(low, dec.qkv) + dec.qkv_bias).astype(BF) for low in stream_all]
    rels = [dot(low, dec.rel) + dec.rel_bias for low in stream_all]
    contexts, lses, kept, outputs, firsts = [], [], [], [], []
    for i in range(3):
        context, lse = attention_forward(meta, heads[i], None if i == 0 else heads[0], rels[i], tables)
        branch, keep = forward_tail(stream_inputs[i], context, dec)
        output, *first = norm_second_both(keep[0], *branch, cotangent[i], dec)
        contexts.append(context)
        lses.append(lse)
        kept.append(keep)
        outputs.append(output)
        firsts.append(first)

    residuals, weight_grads, tinies, dheads, drels = [], [], [], [], []
    key_grad = val_grad = 0.0
    query_main = None
    for i in range(3):
        sum_grad, low, tiny1 = firsts[i]
        residual, dctx, weights, tiny0 = backward_tail(sum_grad, low, kept[i], contexts[i], dec)
        result = attention_backward(
            meta, heads[i], dctx, lses[i], None if i == 0 else heads[0], rels[i], tables
        )
        key_grad = key_grad + result[1]
        val_grad = val_grad + result[2]
        drels.append(result[3])
        if i == 0:
            query_main = result[0]
            dheads.append(None)
        else:
            dheads.append(jnp.concatenate([result[0], result[4], result[5]], axis=1))
        residuals.append(residual)
        weight_grads.append(weights)
        tinies.append((tiny0, tiny1))
    dheads[0] = jnp.concatenate([query_main, key_grad.astype(BF), val_grad.astype(BF)], axis=1)
    input_parts = [
        scatter_dots(dot_nt(dheads[i], dec.qkv) + dot_nt(drels[i], dec.rel)) for i in range(3)
    ]
    pred_grads = [residuals[i] + input_parts[i][0] + input_parts[i][1].astype(F32) for i in (1, 2)]
    dec_qkv_part = sum(dot_tn(stream_all[i], dheads[i]) for i in range(3)).astype(BF)
    dec_rel_part = sum(dot_tn(stream_all[i], drels[i]) for i in range(3)).astype(BF)
    dec_out_part, dec_in_part, dec_back_part = [
        sum(weight_grads[i][k] for i in range(3)).astype(BF) for k in range(3)
    ]
    dec_inner = sum(weight_grads[i][3] for i in range(3))
    dec_tiny0, dec_tiny1 = [sum(tinies[i][k] for i in range(3)) for k in range(2)]
    head_sum = sum(jnp.sum(dheads[i].astype(F32), axis=0) for i in range(3))
    rel_sum = sum(jnp.sum(drels[i].astype(F32), axis=0) for i in range(3))

    def widen(part, size):
        return lax.dynamic_update_slice(jnp.zeros((size,), F32), part, (here * part.shape[0],))

    def small_pack(inner_grad, tiny0, tiny1, heads_grad, rel_grad=None):
        wide = jnp.concatenate(
            [
                widen(heads_grad[:quarter], dim)[None],
                widen(heads_grad[2 * quarter :], dim)[None],
                tiny0[0:1],
                tiny1[0:1],
                tiny0[1:2],
                tiny1[1:2],
                tiny0[2:3],
                tiny1[2:3],
            ],
            axis=0,
        )
        parts = [
            jnp.transpose(wide.reshape(8, n, share), (1, 0, 2)).reshape(n, 8 * share),
            inner_grad.reshape(n, ffn_part),
        ]
        if rel_grad is not None:
            parts.append(widen(rel_grad, rel_all).reshape(n, rel_all // n))
        used = sum(p.shape[1] for p in parts)
        rows_used = -(-used // quarter)
        rows_used += -rows_used % 16
        parts.append(jnp.zeros((n, rows_used * quarter - used), F32))
        return jnp.concatenate(parts, axis=1).reshape(n, rows_used, quarter).astype(BF)

    def attention_sum(qkv_grad, out_grad, more):
        arrays = [qkv_grad.reshape(n, share, 3 * quarter)[:, :, i * quarter : (i + 1) * quarter] for i in range(3)]
        return ring_sum(arrays + [turn_out_back(out_grad)] + more, n, place)

    def ffn_sum(in_grad, back_grad):
        return ring_sum([in_grad.reshape(n, share, dim), back_grad.reshape(n, ffn_part, dim)], n, place)

    dec_ffn_sum = ffn_sum(dec_in_part, dec_back_part)
    rel_blocks = dec_rel_part.reshape(n, share, rel_part)
    dec_attention_sum = attention_sum(
        dec_qkv_part,
        dec_out_part,
        [
            jnp.concatenate([rel_blocks[:, :half], rel_blocks[:, half:]], axis=2),
            small_pack(dec_inner, dec_tiny0, dec_tiny1, head_sum, rel_sum),
        ],
    )

    sum_grad, low, enc_tiny1 = norm_second_back(residuals[0], *input_parts[0], enc_unit1, enc_inverse1, enc)
    residual, dctx, enc_weights, enc_tiny0 = backward_tail(sum_grad, low, enc_kept, enc_context, enc)
    dq, dk, dv = attention_backward(meta, enc_heads, dctx, enc_lse)
    enc_dheads = jnp.concatenate([dq, dk.astype(BF), dv.astype(BF)], axis=1)
    keep, far = scatter_dots(dot_nt(enc_dheads, enc.qkv))
    enc_input_grad = residual + keep + far.astype(F32)
    enc_ffn_sum = ffn_sum(enc_weights[1].astype(BF), enc_weights[2].astype(BF))
    enc_head_sum = jnp.sum(enc_dheads.astype(F32), axis=0)
    enc_attention_sum = attention_sum(
        dot_tn(enc_all, enc_dheads).astype(BF),
        enc_weights[0].astype(BF),
        [small_pack(enc_weights[3], enc_tiny0, enc_tiny1, enc_head_sum)],
    )

    def spread(total_rows):
        low = total_rows.astype(BF)
        far = swap(low, 2)
        near = swap(jnp.stack([low, far]), 1)
        return by_absolute([low, far, near[0], near[1]], here)

    def attention_out(total_rows, with_rel):
        blocks = spread(total_rows)
        wide = jnp.concatenate([b[:fixed] for b in blocks], axis=1).astype(F32)
        qkv = wide[: 3 * share].reshape(3, share, dim)
        out = wide[3 * share :]
        at = fixed
        results = [qkv, out]
        if with_rel:
            parts = [
                jnp.concatenate([b[at : at + half, :rel_part], b[at : at + half, rel_part:]], axis=0) for b in blocks
            ]
            results.append(jnp.concatenate(parts, axis=1).astype(F32))
            at += half
        tiny = jnp.stack([b[at:] for b in blocks]).astype(F32).reshape(STREAMS, -1)
        inner = tiny[:, 8 * share : 8 * share + ffn_part].reshape(-1)
        summed = jnp.sum(tiny, axis=0)
        wide_sum = summed[: 8 * share].reshape(8, share)
        results += [inner, wide_sum[:4], wide_sum[4:6], wide_sum[6:8]]
        if with_rel:
            first = 8 * share + ffn_part
            results.append(summed[first : first + rel_all // n])
        return results

    def ffn_out(total_rows):
        blocks = spread(total_rows)
        grad_in = jnp.stack([b[:share].reshape(share, n, ffn_part) for b in blocks], axis=2)
        grad_out = jnp.concatenate([b[share:] for b in blocks], axis=0)
        return grad_in.reshape(share, ffn).astype(F32), grad_out.astype(F32)

    dec_in_grad, dec_back_grad = ffn_out(dec_ffn_sum)
    dec_qkv_grad, dec_out_grad, dec_rel_grad, *dec_tiny, dec_rel_bias_grad = attention_out(dec_attention_sum, True)
    enc_in_grad, enc_back_grad = ffn_out(enc_ffn_sum)
    enc_qkv_grad, enc_out_grad, *enc_tiny = attention_out(enc_attention_sum, False)

    return (
        jnp.stack(outputs),
        enc_input_grad,
        jnp.stack(pred_grads),
        enc_qkv_grad,
        enc_out_grad,
        enc_in_grad,
        enc_back_grad,
        *enc_tiny,
        dec_qkv_grad,
        dec_out_grad,
        dec_rel_grad,
        dec_rel_bias_grad,
        dec_in_grad,
        dec_back_grad,
        *dec_tiny,
    )


def solution(mesh):
    tokens = P(("stream", "dp"), None)
    streams = P(None, ("stream", "dp"), None)
    first, second, cube = P("dp", None), P(None, "dp"), P(None, "dp", None)
    flat = P("dp")
    return jax.shard_map(
        per_device,
        mesh=mesh,
        in_specs=(
            tokens, streams, streams, flat, first, P(),
            cube, first, first, first, flat, second, second, second,
            cube, first, first, flat, first, first, flat, second, second, second,
        ),
        out_specs=(
            streams, tokens, streams,
            cube, first, first, first, flat, second, second, second,
            cube, first, first, flat, first, first, flat, second, second, second,
        ),
        check_vma=False,
    )
```

```python
from functools import partial

import jax
import jax.numpy as jnp
from jax import lax
from jax.experimental import pallas as pl
from jax.experimental.pallas import tpu as pltpu
from jax.sharding import PartitionSpec as P

H = 16
NB = 32
HD = 64
EPSILON = 1e-05
MASKED = -1000000000.0
BF = jnp.bfloat16
F32 = jnp.float32
TILE = 128
STREAMS = 4
XOR = (0, 2, 1, 3)
MIB = 1024 * 1024


def dot(a, b):
    return jnp.dot(a, b, preferred_element_type=F32)


def dot_nt(a, b):
    return lax.dot_general(a, b, (((1,), (1,)), ((), ())), preferred_element_type=F32)


def dot_tn(a, b):
    return lax.dot_general(a, b, (((0,), (0,)), ((), ())), preferred_element_type=F32)


def swap(values, bit):
    return lax.ppermute(values, "stream", [(i, i ^ bit) for i in range(STREAMS)])


class Chain:
    def __init__(self):
        self.last = None

    def __call__(self, kernel, outs, args, scalars=(), away=(), stored=(), scratch=(), after=(), room=3, cost=1):
        ties = list(after)
        if self.last is not None:
            ties.append(self.last)
        reads = len(scalars) + len(args) + len(away) + len(stored)

        def body(*refs):
            kernel(*refs[:reads], *refs[reads + len(ties) :])

        vmem = pl.BlockSpec(memory_space=pltpu.VMEM)
        anywhere = pl.BlockSpec(memory_space=pl.ANY)
        results = pl.pallas_call(
            body,
            out_shape=[jax.ShapeDtypeStruct(shape, kind) for shape, kind in outs],
            in_specs=[pl.BlockSpec(memory_space=pltpu.SMEM)] * len(scalars)
            + [vmem] * len(args)
            + [anywhere] * len(away)
            + [pl.BlockSpec(memory_space=pltpu.HBM)] * len(stored)
            + [anywhere] * len(ties),
            out_specs=[vmem] * len(outs),
            scratch_shapes=list(scratch),
            compiler_params=pltpu.CompilerParams(vmem_limit_bytes=room * MIB),
            cost_estimate=pl.CostEstimate(flops=10**10, bytes_accessed=10**7, transcendentals=0),
        )(*scalars, *args, *away, *[pltpu.with_memory_space_constraint(a, pltpu.HBM) for a in stored], *ties)
        self.last = results[0]
        return results


def gather_rows(rows):
    far = swap(rows, 2)
    return rows, far, swap(rows, 1), swap(far, 1)


class Scatter:
    def __init__(self, parts):
        self.own, self.across, near = parts
        self.near = swap(near, 1)

    def middle(self, chain, after=()):
        rows, dim = self.own.shape

        def kernel(across_ref, near_ref, out_ref):
            out_ref[...] = (across_ref[...] + near_ref[rows:, :].astype(F32)).astype(BF)

        (low,) = chain(kernel, [((rows, dim), BF)], [self.across, self.near], after=after, cost=0.1)
        self.far = swap(low, 2)

    def parts(self):
        return [self.own, self.near, self.far]


def scattered(own_ref, near_ref, far_ref):
    rows = own_ref.shape[0]
    return own_ref[...] + near_ref[:rows, :].astype(F32) + far_ref[...].astype(F32)


def scatter_outs(rows, dim):
    return [((rows, dim), F32), ((rows, dim), F32), ((2 * rows, dim), BF)]


def store_partials(part, value, own_ref, across_ref, near_ref):
    rows = own_ref.shape[0]
    if part == 0:
        own_ref[...] = value[:rows, :]
        across_ref[...] = value[rows:, :]
    else:
        near_ref[...] = value.astype(BF)


def join(target, refs):
    rows = refs[0].shape[0]
    for i, ref in enumerate(refs):
        target[i * rows : (i + 1) * rows, :] = ref[...]


def turn_blocks(blocks):
    far = swap(jnp.stack([blocks[1], blocks[3]]), 2)
    near = swap(jnp.stack([blocks[2], far[1]]), 1)
    return [blocks[0], far[0], near[0], near[1]]


def by_absolute(blocks, here):
    stacked = jnp.stack([blocks[XOR.index(j)] for j in range(4)])
    return [lax.dynamic_index_in_dim(stacked, here ^ a, 0, keepdims=False) for a in range(4)]


def ring_order(n):
    return list(range(0, n, 2)) + list(range(n - 1, 0, -2))


def ring_member(place, n):
    place = lax.rem(place + 2 * n, n)
    return jnp.where(place < n // 2, 2 * place, 2 * (n - place) - 1)


def ring_place(g, n):
    return jnp.where(g % 2 == 0, g // 2, n - (g + 1) // 2)


def ring_step(values, n, step):
    order = ring_order(n)
    pairs = [(order[i], order[(i + step) % n]) for i in range(n)]
    return lax.ppermute(values, "dp", pairs)


def ring_pieces(own, n):
    rows = own.shape[0]
    pieces = [(0, 0, own)]
    ahead = back = own
    for k in range(1, n // 2):
        ahead = ring_step(ahead, n, 1)
        back = ring_step(back, n, -1)
        pieces += [(k, 0, ahead), (n - k, 0, back)]
    half = halved(rows)
    top = ring_step(ahead[:half], n, 1)
    bottom = ring_step(back[half:], n, -1)
    pieces += [(n // 2, 0, top), (n // 2, half, bottom)]
    return pieces


def halved(rows):
    return rows // 32 * 16


def assemble(chain, pieces, index, regions, shapes, n, after=()):
    moves = []
    for number, (behind, first, piece) in enumerate(pieces):
        last = first + piece.shape[0]
        for r0, r1, c0, c1, which, to_row, to_col in regions:
            lo, hi = max(r0, first), min(r1, last)
            if lo < hi:
                moves.append((number, behind, lo - first, hi - first, c0, c1, which, to_row + lo - r0, to_col))

    def kernel(index_ref, *refs):
        sources = refs[: len(pieces)]
        outs = refs[len(pieces) : -1]
        copy_all(
            [
                (
                    sources[number].at[lo:hi, c0:c1],
                    outs[which].at[index_ref[behind], row : row + hi - lo, col : col + c1 - c0],
                )
                for number, behind, lo, hi, c0, c1, which, row, col in moves
            ],
            refs[-1],
        )

    return chain(
        kernel,
        [((n,) + shape, BF) for shape in shapes],
        [],
        scalars=[index],
        away=[piece for _, _, piece in pieces],
        scratch=[pltpu.SemaphoreType.DMA((len(moves),))],
        after=after,
    )


class RingSum:
    def __init__(self, chain, arrays, regions, columns, n, index):
        self.chain, self.arrays, self.regions, self.n, self.index = chain, arrays, regions, n, index
        self.columns = columns
        self.rows = sum(r[3] for r in regions)
        self.half = halved(self.rows)
        self.up = self.down = None
        self.done = 0
        self.left = n // 2

    def fetch(self, index_ref, offsets, refs, buffers, sems):
        copies = []
        for slot, offset in enumerate(offsets):
            g = index_ref[offset]
            for i, (which, column, row, rows) in enumerate(self.regions):
                copies.append(
                    pltpu.make_async_copy(
                        refs[which].at[g, :, column : column + self.columns],
                        buffers.at[slot, row : row + rows, :],
                        sems.at[slot * len(self.regions) + i],
                    )
                )
                copies[-1].start()
        for copy in copies:
            copy.wait()

    def step(self, after=()):
        rows, half, columns, count = self.rows, self.half, self.columns, len(self.arrays)
        first = self.left == self.n // 2
        last = self.left == 0
        joined = self.left == self.n // 2 - 1
        offsets = [(self.n - self.left) % self.n] + ([] if first or last else [self.left])
        received = [] if first else [self.up, self.down]

        def kernel(index_ref, *refs):
            ups = refs[: len(received)]
            arrays = refs[len(received) : len(received) + count]
            outs = refs[len(received) + count : -2]
            buffers, sems = refs[-2:]
            self.fetch(index_ref, offsets, arrays, buffers, sems)
            if first:
                outs[0][...] = buffers[0, :half, :]
                outs[1][...] = buffers[0, half:, :]
            elif last:
                outs[0][...] = (
                    buffers[0].astype(F32) + ups[0][...].astype(F32) + ups[1][...].astype(F32)
                ).astype(BF)
            elif joined:
                outs[0][:half, :] = (buffers[0, :half, :].astype(F32) + ups[0][...].astype(F32)).astype(BF)
                outs[0][half:, :] = buffers[0, half:, :]
                outs[1][:half, :] = buffers[1, :half, :]
                outs[1][half:, :] = (buffers[1, half:, :].astype(F32) + ups[1][...].astype(F32)).astype(BF)
            else:
                outs[0][...] = (buffers[0].astype(F32) + ups[0][...].astype(F32)).astype(BF)
                outs[1][...] = (buffers[1].astype(F32) + ups[1][...].astype(F32)).astype(BF)

        if first:
            outs = [((half, columns), BF), ((rows - half, columns), BF)]
        else:
            outs = [((rows, columns), BF)] * (1 if last else 2)
        results = self.chain(
            kernel,
            outs,
            received,
            scalars=[self.index],
            away=self.arrays,
            scratch=[
                pltpu.VMEM((len(offsets), rows, columns), BF),
                pltpu.SemaphoreType.DMA((len(offsets) * len(self.regions),)),
            ],
            after=after,
        )
        self.left -= 1
        if last:
            return results[0]
        self.up = ring_step(results[0], self.n, 1)
        self.down = ring_step(results[1], self.n, -1)
        return None


def tile_width(t, causal, total):
    return TILE * (t + 1) if causal else total


def head_mask(e):
    lane = lax.broadcasted_iota(jnp.int32, (1, TILE), 1)
    return ((lane // HD) == e).astype(F32)


def rel_mask(h):
    lane = lax.broadcasted_iota(jnp.int32, (1, TILE), 1)
    return ((lane // NB) == h).astype(F32)


def allowed_keys(t, width, meta, causal, strict):
    bucket = meta[8]
    shape = (TILE, width)
    row = lax.broadcasted_iota(jnp.int32, shape, 0) + t * TILE
    col = lax.broadcasted_iota(jnp.int32, shape, 1)
    pos = col & (bucket - 1)
    first = col < bucket
    limit = bucket - jnp.where(first, meta[9], meta[10])
    allowed = (pos < limit) & ((row < bucket) == first)
    if causal:
        allowed = allowed & ((col < row) if strict else (col <= row))
    return allowed


def load_rows(meta, target, source, c0, c1):
    for chunk in range(8):
        start = pl.multiple_of(meta[chunk], 64)
        target[pl.ds(start, 64), :] = source[chunk * 64 : chunk * 64 + 64, c0:c1].astype(target.dtype)


def store_rows(meta, target, source, c0, c1):
    for chunk in range(8):
        start = pl.multiple_of(meta[chunk], 64)
        target[chunk * 64 : chunk * 64 + 64, c0:c1] = source[pl.ds(start, 64), :].astype(target.dtype)


def rel_bias(rel_rows, h, table):
    high = rel_rows.astype(BF)
    rest = (rel_rows - high.astype(F32)).astype(BF)
    mask = rel_mask(h)
    both = jnp.concatenate(
        [(high.astype(F32) * mask).astype(BF), (rest.astype(F32) * mask).astype(BF)], axis=1
    )
    spread = dot(both, table)
    return pltpu.roll(spread, 0, 1, stride=1, stride_axis=0)


def table_slice(t, width):
    first = sum(TILE * (u + 1) for u in range(t))
    return slice(first, first + width)


def attention_forward(chain, meta, qkv, main=None, rel=None, tables=None, w_out=None, after=()):
    total = qkv.shape[0]
    width_all = qkv.shape[1] // 3
    heads = width_all // HD
    causal = rel is not None
    own = main is not None
    project = w_out is not None
    block = total // STREAMS

    def kernel(meta_ref, *refs):
        refs = list(refs)
        qkv_ref = refs.pop(0)
        main_ref = refs.pop(0) if own else qkv_ref
        rel_ref, table_ref, hot_ref = (refs.pop(0), refs.pop(0), refs.pop(0)) if causal else (None,) * 3
        out_ref = refs.pop(0) if project else None
        ctx_ref, lse_ref = refs.pop(0), refs.pop(0)
        parts_refs = [refs.pop(0) for _ in range(3)] if project else None
        qs, ks, vs, cs, kt = refs[:5]
        refs = refs[5:]
        rs = refs.pop(0) if causal else None
        load_rows(meta_ref, qs, qkv_ref, 0, width_all)
        load_rows(meta_ref, ks, main_ref, width_all, 2 * width_all)
        load_rows(meta_ref, vs, main_ref, 2 * width_all, 3 * width_all)
        if causal:
            load_rows(meta_ref, rs, rel_ref, 0, rel.shape[1])
        if own:
            kn, vn = refs
            load_rows(meta_ref, kn, qkv_ref, width_all, 2 * width_all)
            load_rows(meta_ref, vn, qkv_ref, 2 * width_all, 3 * width_all)
        kt[...] = ks[...].T
        for t in range(total // TILE):
            rows = slice(TILE * t, TILE * (t + 1))
            width = tile_width(t, causal, total)
            allowed = allowed_keys(t, width, meta_ref, causal, own)
            lse_lane = lax.broadcasted_iota(jnp.int32, (TILE, TILE), 1)
            lse = jnp.zeros((TILE, TILE), F32)
            query = [(qs[rows, HD * h : HD * (h + 1)].astype(F32) * HD**-0.5).astype(BF) for h in range(heads)]
            scores = [dot(query[h], kt[HD * h : HD * (h + 1), 0:width]) for h in range(heads)]
            if causal:
                biases = [rel_bias(rs[rows, :], h, table_ref[:, table_slice(t, width)]) for h in range(heads)]
                scores = [a + b for a, b in zip(scores, biases)]
            scores = [jnp.where(allowed, a, MASKED) for a in scores]
            tops = [jnp.max(a, axis=1, keepdims=True) for a in scores]
            if own:
                own_scores = [
                    jnp.sum(
                        query[h].astype(F32) * kn[rows, HD * h : HD * (h + 1)].astype(F32), axis=1, keepdims=True
                    )
                    + jnp.sum(rs[rows, :] * (hot_ref[...] * rel_mask(h)), axis=1, keepdims=True)
                    for h in range(heads)
                ]
                tops = [jnp.maximum(a, b) for a, b in zip(tops, own_scores)]
            expos = [jnp.exp(a - b) for a, b in zip(scores, tops)]
            sums = [jnp.sum(a, axis=1, keepdims=True) for a in expos]
            if own:
                own_expos = [jnp.exp(a - b) for a, b in zip(own_scores, tops)]
                sums = [a + b for a, b in zip(sums, own_expos)]
            inverses = [1.0 / a for a in sums]
            parts = [
                dot((expos[h] * inverses[h]).astype(BF), vs[0:width, HD * h : HD * (h + 1)]) for h in range(heads)
            ]
            if own:
                own_probs = [own_expos[h] * inverses[h] for h in range(heads)]
                parts = [
                    parts[h] + own_probs[h] * vn[rows, HD * h : HD * (h + 1)].astype(F32) for h in range(heads)
                ]
            cs[rows, :] = jnp.concatenate(parts, axis=1).astype(BF)
            for h in range(heads):
                lse = jnp.where(lse_lane == h, tops[h] + jnp.log(sums[h]), lse)
                if own:
                    lse = jnp.where(lse_lane == heads + h, own_probs[h], lse)
            lse_ref[rows, :] = lse
        store_rows(meta_ref, ctx_ref, cs, 0, width_all)
        if project:
            for part in range(2):
                value = dot(ctx_ref[part * 2 * block : (part + 1) * 2 * block, :], out_ref[...])
                store_partials(part, value, *parts_refs)

    args = [qkv]
    scratch = [pltpu.VMEM((total, width_all), BF) for _ in range(4)] + [pltpu.VMEM((width_all, total), BF)]
    outs = [((total, width_all), BF), ((total, TILE), F32)]
    if own:
        args.append(main)
    if causal:
        args += [rel, tables[0], tables[2]]
        scratch.append(pltpu.VMEM((total, rel.shape[1]), F32))
    if own:
        scratch += [pltpu.VMEM((total, width_all), BF) for _ in range(2)]
    if project:
        args.append(w_out)
        outs += scatter_outs(block, w_out.shape[1])
    context, lse, *parts = chain(kernel, outs, args, scalars=[meta], scratch=scratch, after=after, room=8, cost=6)
    return context, lse, parts


def attention_backward(chain, meta, qkv, attended, w_out, lse, main=None, rel=None, tables=None, after=()):
    total = qkv.shape[0]
    width_all = qkv.shape[1] // 3
    heads = width_all // HD
    causal = rel is not None
    own = main is not None

    def kernel(meta_ref, *refs):
        refs = list(refs)
        qkv_ref = refs.pop(0)
        attended_refs = [refs.pop(0) for _ in range(STREAMS)]
        out_ref, lse_ref = refs.pop(0), refs.pop(0)
        main_ref = refs.pop(0) if own else qkv_ref
        rel_ref, table_ref, back_ref, hot_ref, flip_ref = (
            [refs.pop(0) for _ in range(5)] if causal else (None,) * 5
        )
        dq_ref, dk_ref, dv_ref, joined_ref = refs[:4]
        refs = refs[4:]
        drel_ref = refs.pop(0) if causal else None
        dkn_ref, dvn_ref = (refs.pop(0), refs.pop(0)) if own else (None, None)
        qs, ks, vs, gs, dqs, dks, kt, vt, qt, gt, dkt, dvt = refs[:12]
        refs = refs[12:]
        rs, drs = (refs.pop(0), refs.pop(0)) if causal else (None, None)
        join(joined_ref, attended_refs)
        dqs[...] = dot_nt(joined_ref[...], out_ref[...])
        load_rows(meta_ref, qs, qkv_ref, 0, width_all)
        load_rows(meta_ref, ks, main_ref, width_all, 2 * width_all)
        load_rows(meta_ref, vs, main_ref, 2 * width_all, 3 * width_all)
        load_rows(meta_ref, gs, dqs, 0, width_all)
        if causal:
            load_rows(meta_ref, rs, rel_ref, 0, rel.shape[1])
        if own:
            kn, vn, dkn, dvn = refs
            load_rows(meta_ref, kn, qkv_ref, width_all, 2 * width_all)
            load_rows(meta_ref, vn, qkv_ref, 2 * width_all, 3 * width_all)
        qs[...] = (qs[...].astype(F32) * HD**-0.5).astype(BF)
        kt[...] = ks[...].T
        vt[...] = vs[...].T
        qt[...] = qs[...].T
        gt[...] = gs[...].T
        dkt[...] = jnp.zeros_like(dkt)
        dvt[...] = jnp.zeros_like(dvt)
        each = range(heads)
        feat = [slice(HD * h, HD * (h + 1)) for h in each]
        for t in range(total // TILE):
            rows = slice(TILE * t, TILE * (t + 1))
            width = tile_width(t, causal, total)
            allowed = allowed_keys(t, width, meta_ref, causal, own)
            norms = [lse_ref[rows, h : h + 1] for h in each]
            query = [qs[rows, feat[h]] for h in each]
            grad = [gs[rows, feat[h]] for h in each]
            scores = [dot(query[h], kt[feat[h], 0:width]) for h in each]
            dprobs = [dot(grad[h], vt[feat[h], 0:width]) for h in each]
            if causal:
                biases = [rel_bias(rs[rows, :], h, table_ref[:, table_slice(t, width)]) for h in each]
                scores = [a + b for a, b in zip(scores, biases)]
            probs = [jnp.exp(jnp.where(allowed, scores[h], MASKED) - norms[h]) for h in each]
            rowdots = [jnp.sum(probs[h] * dprobs[h], axis=1, keepdims=True) for h in each]
            if own:
                own_probs = [lse_ref[rows, heads + h : heads + h + 1] for h in each]
                own_dprobs = [
                    jnp.sum(grad[h].astype(F32) * vn[rows, feat[h]].astype(F32), axis=1, keepdims=True) for h in each
                ]
                rowdots = [rowdots[h] + own_probs[h] * own_dprobs[h] for h in each]
                own_dscores = [
                    (own_probs[h] * (own_dprobs[h] - rowdots[h])).astype(BF).astype(F32) for h in each
                ]
            dscores = [(probs[h] * (dprobs[h] - rowdots[h])).astype(BF) for h in each]
            dqs_parts = [dot(dscores[h], ks[0:width, feat[h]]) for h in each]
            if own:
                dqs_parts = [dqs_parts[h] + own_dscores[h] * kn[rows, feat[h]].astype(F32) for h in each]
                dkn[rows, :] = jnp.concatenate([own_dscores[h] * query[h].astype(F32) for h in each], axis=1)
                dvn[rows, :] = jnp.concatenate([own_probs[h] * grad[h].astype(F32) for h in each], axis=1)
            dqs[rows, :] = jnp.concatenate(dqs_parts, axis=1) * HD**-0.5
            for h in each:
                dkt[feat[h], 0:width] += dot(qt[feat[h], rows], dscores[h])
                dvt[feat[h], 0:width] += dot(gt[feat[h], rows], probs[h].astype(BF))
            if causal:
                drel = jnp.zeros((TILE, TILE), F32)
                for h in each:
                    blocks = [
                        dot(dscores[h][:, TILE * b : TILE * (b + 1)], flip_ref[...])
                        for b in reversed(range(width // TILE))
                    ]
                    mirrored = jnp.concatenate(blocks, axis=1) if len(blocks) > 1 else blocks[0]
                    turned = pltpu.roll(mirrored, 0, 1, stride=1, stride_axis=0).astype(BF)
                    drel = drel + dot(turned, back_ref[table_slice(t, width), :]) * rel_mask(h)
                    if own:
                        drel = drel + own_dscores[h] * (hot_ref[...] * rel_mask(h))
                drs[rows, :] = drel
        store_rows(meta_ref, dq_ref, dqs, 0, width_all)
        dks[...] = dkt[...].T
        store_rows(meta_ref, dk_ref, dks, 0, width_all)
        dks[...] = dvt[...].T
        store_rows(meta_ref, dv_ref, dks, 0, width_all)
        if causal:
            store_rows(meta_ref, drel_ref, drs, 0, rel.shape[1])
        if own:
            store_rows(meta_ref, dkn_ref, dkn, 0, width_all)
            store_rows(meta_ref, dvn_ref, dvn, 0, width_all)

    args = [qkv, *attended, w_out, lse]
    shape = (total, width_all)
    turned = (width_all, total)
    outs = [(shape, BF), (shape, F32), (shape, F32), ((total, w_out.shape[1]), BF)]
    scratch = [pltpu.VMEM(shape, BF) for _ in range(4)] + [pltpu.VMEM(shape, F32) for _ in range(2)]
    scratch += [pltpu.VMEM(turned, BF) for _ in range(4)] + [pltpu.VMEM(turned, F32) for _ in range(2)]
    if own:
        args.append(main)
    if causal:
        args += [rel, *tables]
        outs.append(((total, rel.shape[1]), BF))
        scratch += [pltpu.VMEM((total, rel.shape[1]), F32) for _ in range(2)]
    if own:
        outs += [(shape, BF), (shape, BF)]
        scratch += [pltpu.VMEM(shape, BF) for _ in range(2)] + [pltpu.VMEM(shape, F32) for _ in range(2)]
    return chain(kernel, outs, args, scalars=[meta], scratch=scratch, after=after, room=12, cost=10 if causal else 6)


def rel_tables(rel_table, total):
    ahead, back = [], []
    for t in range(total // TILE):
        width = TILE * (t + 1)
        here = rel_table[:width]
        ahead += [jnp.flip(here[: TILE * t + 1]), jnp.flip(here[TILE * t + 1 :])]
        back += [here[width - TILE + 1 :], here[: width - TILE + 1]]
    ahead, back = jnp.concatenate(ahead), jnp.concatenate(back)
    rows = jnp.arange(2 * TILE, dtype=jnp.int32) % NB
    forward = (rows[:, None] == ahead[None, :]).astype(BF)
    backward = (back[:, None] == rows[None, :TILE]).astype(BF)
    hot = (rows[None, :TILE] == rel_table[0]).astype(F32)
    ids = jnp.arange(TILE, dtype=jnp.int32)
    flip = (ids[:, None] + ids[None, :] == TILE - 1).astype(BF)
    return forward, backward, hot, flip


def unit_of(values):
    center = values - jnp.mean(values, axis=-1, keepdims=True)
    spread = jnp.mean(center * center, axis=-1, keepdims=True)
    inverse = lax.rsqrt(spread + EPSILON)
    return center * inverse, inverse


def unit_back(grad, unit, inverse, gain):
    inner = grad * gain
    mean = jnp.mean(inner, axis=-1, keepdims=True)
    along = jnp.mean(inner * unit, axis=-1, keepdims=True)
    return inverse * (inner - mean - unit * along)


def column(values):
    return jnp.sum(values, axis=0, keepdims=True)


def tiny_sums(low, grad, unit):
    return jnp.concatenate([column(low.astype(F32)), column(grad * unit), column(grad)], axis=0)


def norm_first(chain, inputs, parts, w, after=()):
    rows, dim = inputs.shape

    def kernel(in_ref, own_ref, near_ref, far_ref, small_ref, unit_ref, inverse_ref, low_ref):
        values = in_ref[...].astype(F32) + scattered(own_ref, near_ref, far_ref) + small_ref[2:3, :]
        unit, inverse = unit_of(values)
        unit_ref[...] = unit
        inverse_ref[...] = inverse
        low_ref[...] = (unit * small_ref[4:5, :] + small_ref[6:7, :]).astype(BF)

    outs = [((rows, dim), F32), ((rows, 1), F32), ((rows, dim), BF)]
    return chain(kernel, outs, [inputs, *parts, w.small], after=after)


def norm_second(chain, unit0, parts, w, after=()):
    rows, dim = unit0.shape

    def kernel(unit_ref, own_ref, near_ref, far_ref, small_ref, unit1_ref, inverse_ref, out_ref, low_ref):
        hidden = unit_ref[...] * small_ref[4:5, :] + small_ref[6:7, :]
        unit, inverse = unit_of(hidden + scattered(own_ref, near_ref, far_ref) + small_ref[3:4, :])
        out = unit * small_ref[5:6, :] + small_ref[7:8, :]
        unit1_ref[...] = unit
        inverse_ref[...] = inverse
        out_ref[...] = out
        low_ref[...] = out.astype(BF)

    outs = [((rows, dim), F32), ((rows, 1), F32), ((rows, dim), F32), ((rows, dim), BF)]
    return chain(kernel, outs, [unit0, *parts, w.small], after=after)


def norm_second_back(chain, residual, parts, unit1, inverse, w, after=()):
    rows, dim = residual.shape

    def kernel(res_ref, own_ref, near_ref, far_ref, unit_ref, inverse_ref, small_ref, sum_ref, low_ref, tiny_ref):
        grad = res_ref[...] + scattered(own_ref, near_ref, far_ref)
        unit = unit_ref[...]
        back = unit_back(grad, unit, inverse_ref[...], small_ref[5:6, :])
        low = back.astype(BF)
        sum_ref[...] = back
        low_ref[...] = low
        tiny_ref[...] = tiny_sums(low, grad, unit)

    outs = [((rows, dim), F32), ((rows, dim), BF), ((3, dim), F32)]
    return chain(kernel, outs, [residual, *parts, unit1, inverse, w.small], after=after)


def norm_second_both(chain, unit0, parts, cotangent, w, after=()):
    rows, dim = unit0.shape

    def kernel(unit_ref, own_ref, near_ref, far_ref, cot_ref, small_ref, out_ref, sum_ref, low_ref, tiny_ref):
        hidden = unit_ref[...] * small_ref[4:5, :] + small_ref[6:7, :]
        unit, inverse = unit_of(hidden + scattered(own_ref, near_ref, far_ref) + small_ref[3:4, :])
        out_ref[...] = unit * small_ref[5:6, :] + small_ref[7:8, :]
        grad = cot_ref[...].astype(F32)
        back = unit_back(grad, unit, inverse, small_ref[5:6, :])
        low = back.astype(BF)
        sum_ref[...] = back
        low_ref[...] = low
        tiny_ref[...] = tiny_sums(low, grad, unit)

    outs = [((rows, dim), F32), ((rows, dim), F32), ((rows, dim), BF), ((3, dim), F32)]
    return chain(kernel, outs, [unit0, *parts, cotangent, w.small], after=after)


def norm_first_back(chain, sum_grad, parts, unit0, inverse, w, after=()):
    rows, dim = sum_grad.shape

    def kernel(sum_ref, own_ref, near_ref, far_ref, unit_ref, inverse_ref, small_ref, out_ref, low_ref, tiny_ref):
        grad = sum_ref[...] + scattered(own_ref, near_ref, far_ref)
        unit = unit_ref[...]
        back = unit_back(grad, unit, inverse_ref[...], small_ref[4:5, :])
        low = back.astype(BF)
        out_ref[...] = back
        low_ref[...] = low
        tiny_ref[...] = tiny_sums(low, grad, unit)

    outs = [((rows, dim), F32), ((rows, dim), BF), ((3, dim), F32)]
    return chain(kernel, outs, [sum_grad, *parts, unit0, inverse, w.small], after=after)


def input_gradient(chain, residual, parts, after=()):
    rows, dim = residual.shape

    def kernel(res_ref, own_ref, near_ref, far_ref, out_ref):
        out_ref[...] = res_ref[...] + scattered(own_ref, near_ref, far_ref)

    return chain(kernel, [((rows, dim), F32)], [residual, *parts], after=after)[0]


def project(chain, quads, w, with_rel, after=()):
    rows, dim = quads[0].shape
    width = w.qkv.shape[1]

    def kernel(*refs):
        refs = list(refs)
        quad_refs = [refs.pop(0) for _ in range(STREAMS)]
        qkv_ref, bias_ref = refs.pop(0), refs.pop(0)
        rel_ref, rel_bias_ref = (refs.pop(0), refs.pop(0)) if with_rel else (None, None)
        joined_ref, heads_ref = refs.pop(0), refs.pop(0)
        join(joined_ref, quad_refs)
        heads_ref[...] = (dot(joined_ref[...], qkv_ref[...]) + bias_ref[...]).astype(BF)
        if with_rel:
            refs[0][...] = dot(joined_ref[...], rel_ref[...]) + rel_bias_ref[...]

    args = [*quads, w.qkv, w.qkv_bias]
    outs = [((STREAMS * rows, dim), BF), ((STREAMS * rows, width), BF)]
    if with_rel:
        args += [w.rel, w.rel_bias]
        outs.append(((STREAMS * rows, w.rel.shape[1]), F32))
    return chain(kernel, outs, args, after=after)


def out_project(chain, context, w, after=()):
    total, _ = context.shape
    block = total // STREAMS

    def kernel(context_ref, out_ref, *parts_refs):
        for part in range(2):
            value = dot(context_ref[part * 2 * block : (part + 1) * 2 * block, :], out_ref[...])
            store_partials(part, value, *parts_refs)

    return chain(kernel, scatter_outs(block, w.out.shape[1]), [context, w.out], after=after)


def project_back(chain, dq, dk, dv, drel, w, after=()):
    total, width = dq.shape
    block = total // STREAMS
    dim = w.qkv.shape[0]
    with_rel = drel is not None
    keys, vals = len(dk), len(dv)

    def kernel(*refs):
        refs = list(refs)
        dq_ref = refs.pop(0)
        dk_refs = [refs.pop(0) for _ in range(keys)]
        dv_refs = [refs.pop(0) for _ in range(vals)]
        drel_ref = refs.pop(0) if with_rel else None
        qkv_ref = refs.pop(0)
        rel_ref = refs.pop(0) if with_rel else None
        parts_refs = [refs.pop(0) for _ in range(3)]
        heads_ref, sums_ref = refs.pop(0), refs.pop(0)
        heads_ref[:, :width] = dq_ref[...]
        heads_ref[:, width : 2 * width] = sum(r[...] for r in dk_refs).astype(BF)
        heads_ref[:, 2 * width :] = sum(r[...] for r in dv_refs).astype(BF)
        sums_ref[...] = column(heads_ref[...].astype(F32))
        if with_rel:
            refs[0][...] = column(drel_ref[...].astype(F32))
        for part in range(2):
            rows = slice(part * 2 * block, (part + 1) * 2 * block)
            value = dot_nt(heads_ref[rows, :], qkv_ref[...])
            if with_rel:
                value = value + dot_nt(drel_ref[rows, :], rel_ref[...])
            store_partials(part, value, *parts_refs)

    args = [dq, *dk, *dv]
    outs = scatter_outs(block, dim) + [((total, 3 * width), BF), ((1, 3 * width), F32)]
    if with_rel:
        args += [drel, w.qkv, w.rel]
        outs.append(((1, w.rel.shape[1]), F32))
    else:
        args.append(w.qkv)
    return chain(kernel, outs, args, after=after)


def gelu_and_slope(x):
    bell = jnp.exp(-0.5 * x * x)
    under = 1.0 + (0.3275911 * 0.5**0.5) * jnp.abs(x)
    t = pl.reciprocal(under, approx=True)
    t = t * (2.0 - under * t)
    series = ((((1.061405429 * t - 1.453152027) * t + 1.421413741) * t - 0.284496736) * t + 0.254829592) * t
    tail = (0.5 * series) * bell
    below = jnp.where(x >= 0.0, 1.0 - tail, tail)
    return x * below, below + x * bell * 0.3989422804014327


FFN_TILE = 256


def ffn_in_tile(ref, share, first):
    tile = ref[:, :share, first : first + FFN_TILE]
    return tile.reshape(tile.shape[0] * share, FFN_TILE)


def ffn_out_rows(ref, share, first, last):
    part = ref.shape[1] - share
    tile = ref[first // part : last // part, share:, :]
    return tile.reshape(last - first, ref.shape[2])


def ffn_forward(chain, quads, w, after=()):
    rows, dim = quads[0].shape
    n, both, units = w.ffn.shape
    share = dim // n
    half = 2 * rows

    def kernel(a_ref, b_ref, c_ref, d_ref, w_ref, bias_ref, own_ref, across_ref, near_ref, joined_ref, act_ref, slope_ref):
        join(joined_ref, (a_ref, b_ref, c_ref, d_ref))
        for part in range(2):
            block = slice(part * half, (part + 1) * half)
            for u in range(0, units, FFN_TILE):
                tile = slice(u, u + FFN_TILE)
                inner = dot(joined_ref[block, :], ffn_in_tile(w_ref, share, u)) + bias_ref[:, tile]
                active, slope = gelu_and_slope(inner)
                act_ref[block, tile] = active.astype(BF)
                slope_ref[block, tile] = slope.astype(BF)
            branch = dot(act_ref[block, :], ffn_out_rows(w_ref, share, 0, units))
            store_partials(part, branch, own_ref, across_ref, near_ref)

    wide = ((4 * rows, units), BF)
    outs = scatter_outs(rows, dim) + [((4 * rows, dim), BF), wide, wide]
    return chain(kernel, outs, [*quads, w.ffn, w.ffn_bias], after=after, cost=5)


def ffn_backward(chain, quads, slope, w, after=()):
    rows, dim = quads[0].shape
    n, both, units = w.ffn.shape
    share = dim // n
    half = 2 * rows

    def kernel(a_ref, b_ref, c_ref, d_ref, w_ref, slope_ref, own_ref, across_ref, near_ref, joined_ref, inner_ref, sums_ref):
        join(joined_ref, (a_ref, b_ref, c_ref, d_ref))
        for part in range(2):
            block = slice(part * half, (part + 1) * half)
            for u in range(0, units, FFN_TILE):
                tile = slice(u, u + FFN_TILE)
                back = dot_nt(joined_ref[block, :], ffn_out_rows(w_ref, share, u, u + FFN_TILE))
                inner = (back * slope_ref[block, tile].astype(F32)).astype(BF)
                inner_ref[block, tile] = inner
                if part == 0:
                    sums_ref[:, tile] = column(inner.astype(F32))
                else:
                    sums_ref[:, tile] += column(inner.astype(F32))
            hidden = sum(
                dot_nt(inner_ref[block, u : u + FFN_TILE], ffn_in_tile(w_ref, share, u))
                for u in range(0, units, FFN_TILE)
            )
            store_partials(part, hidden, own_ref, across_ref, near_ref)

    outs = scatter_outs(rows, dim) + [((4 * rows, dim), BF), ((4 * rows, units), BF), ((1, units), F32)]
    return chain(kernel, outs, [*quads, w.ffn, slope], after=after, cost=4)


def copy_all(moves, sems):
    copies = [pltpu.make_async_copy(source, target, sems.at[i]) for i, (source, target) in enumerate(moves)]
    for copy in copies:
        copy.start()
    for copy in copies:
        copy.wait()


def pack_attention(chain, devices, qkv, out, smalls=None, rel=None, after=()):
    share, dim = out.shape
    quarter = dim // STREAMS
    fixed = 4 * share
    half = share // 2
    more = 16 if rel is None else half
    extra = list(smalls) if rel is None else [rel]

    def kernel(devices_ref, qkv_ref, out_ref, *refs):
        sources, packed_ref, targets, sems = refs[: len(extra)], refs[len(extra)], refs[len(extra) + 1 : -1], refs[-1]
        columns = pl.ds(pl.multiple_of(devices_ref[0] * quarter, quarter), quarter)
        moves = [(qkv_ref.at[i, :, columns], packed_ref.at[i * share : (i + 1) * share, :]) for i in range(3)]
        moves.append((out_ref.at[:, columns], packed_ref.at[3 * share : fixed, :]))
        if rel is None:
            moves += list(zip(sources, targets))
        else:
            part = rel.shape[1] // STREAMS
            columns = pl.ds(pl.multiple_of(devices_ref[0] * part, part), part)
            for i in range(2):
                moves.append(
                    (
                        sources[0].at[i * half : (i + 1) * half, columns],
                        packed_ref.at[fixed:, i * part : (i + 1) * part],
                    )
                )
        copy_all(moves, sems)
        if rel is None:
            lines = []
            for layer in range(2):
                ffn_ref, bias_ref, gain_ref, shift_ref, last_ref = targets[5 * layer : 5 * layer + 5]
                left = jnp.concatenate([r[...].astype(F32) for r in (bias_ref, gain_ref, shift_ref)], axis=0)
                right = [ffn_ref[:, i * share : (i + 1) * share].astype(F32) for i in range(STREAMS)]
                last = last_ref[...].astype(F32)
                right.append(jnp.concatenate([last, jnp.zeros((1, share - last.shape[1]), F32)], axis=1))
                right.append(jnp.zeros((3, share), F32))
                lines.append(jnp.concatenate([left, jnp.concatenate(right, axis=0)], axis=1))
            lines = jnp.concatenate(lines, axis=0)
            packed_ref[fixed:, : 2 * share] = lines.astype(BF)
            if 2 * share < quarter:
                packed_ref[fixed:, 2 * share :] = jnp.zeros((more, quarter - 2 * share), BF)

    scratch = [pltpu.VMEM(a.shape, BF) for a in extra] if rel is None else []
    scratch.append(pltpu.SemaphoreType.DMA((4 + (len(extra) if rel is None else 2),)))
    outs = [((fixed + more, quarter), BF)]
    return chain(kernel, outs, [], scalars=[devices], stored=[qkv, out] + extra, scratch=scratch, after=after)[0]


def pack_ffn(chain, devices, here, matrix_in, matrix_out, n, after=()):
    share, ffn = matrix_in.shape
    ffn_share, dim = matrix_out.shape
    part = ffn_share // STREAMS
    if part % TILE:
        blocks = lax.dynamic_slice_in_dim(matrix_in.reshape(share, n, ffn_share), here * part, part, axis=2)
        rows = lax.dynamic_slice_in_dim(matrix_out, here * part, part, axis=0)
        return jnp.concatenate([blocks.reshape(share, n * part), rows], axis=0)

    def kernel(devices_ref, in_ref, out_ref, packed_ref, sems):
        first = devices_ref[0] * part
        moves = [(out_ref.at[pl.ds(pl.multiple_of(first, TILE), part), :], packed_ref.at[share:, :])]
        for g in range(n):
            columns = pl.ds(pl.multiple_of(g * ffn_share + first, TILE), part)
            moves.append((in_ref.at[:, columns], packed_ref.at[:share, g * part : (g + 1) * part]))
        copy_all(moves, sems)

    return chain(
        kernel,
        [((share + part, n * part), BF)],
        [],
        scalars=[devices],
        stored=[matrix_in, matrix_out],
        scratch=[pltpu.SemaphoreType.DMA((n + 1,))],
        after=after,
    )[0]


def place_ffn(chain, devices, here, blocks, share, n, after=()):
    rows, dim = blocks[0].shape
    part = rows - share
    ffn = n * part * STREAMS
    if part % TILE:
        stacked = jnp.stack([blocks[XOR.index(j)] for j in range(STREAMS)])
        ordered = [lax.dynamic_index_in_dim(stacked, here ^ a, 0, keepdims=False) for a in range(STREAMS)]
        grad_in = jnp.stack([b[:share].reshape(share, n, part) for b in ordered], axis=2)
        grad_out = jnp.concatenate([b[share:] for b in ordered], axis=0)
        return grad_in.reshape(share, ffn).astype(F32), grad_out.astype(F32)

    def kernel(devices_ref, *refs):
        in_ref, out_ref = refs[STREAMS:]
        for i in range(STREAMS):
            first = devices_ref[i] * part
            for g in range(n):
                columns = pl.ds(pl.multiple_of(g * part * STREAMS + first, TILE), part)
                in_ref[:, columns] = refs[i][:share, g * part : (g + 1) * part].astype(F32)
            out_ref[pl.ds(pl.multiple_of(first, TILE), part), :] = refs[i][share:, :].astype(F32)

    outs = [((share, ffn), F32), ((STREAMS * part, dim), F32)]
    return chain(kernel, outs, blocks, scalars=[devices], after=after, room=6)


def place_attention(chain, devices, blocks, share, ffn_part, rel_part, after=()):
    quarter = blocks[0].shape[1]
    dim = quarter * STREAMS
    fixed = 4 * share
    half = share // 2
    tiny = fixed + (half if rel_part else 0)
    tiny_rows = blocks[0].shape[0] - tiny

    def kernel(devices_ref, *refs):
        refs = list(refs)
        block_refs = [refs.pop(0) for _ in range(STREAMS)]
        qkv_ref, out_ref, tiny_ref, inner_ref = refs[:4]
        total = jnp.zeros((tiny_rows, quarter), F32)
        for i, ref in enumerate(block_refs):
            columns = pl.ds(pl.multiple_of(devices_ref[i] * quarter, quarter), quarter)
            for k in range(3):
                qkv_ref[k, :, columns] = ref[k * share : (k + 1) * share, :].astype(F32)
            out_ref[:, columns] = ref[3 * share : fixed, :].astype(F32)
            if rel_part:
                columns = pl.ds(pl.multiple_of(devices_ref[i] * rel_part, rel_part), rel_part)
                refs[4][:half, columns] = ref[fixed : fixed + half, :rel_part].astype(F32)
                refs[4][half:, columns] = ref[fixed : fixed + half, rel_part:].astype(F32)
            mine = ref[tiny:, :].astype(F32)
            total = total + mine
            inner_ref[pl.ds(devices_ref[i], 1), :] = mine[0:1, share : share + ffn_part]
        tiny_ref[...] = total

    outs = [
        ((3, share, dim), F32),
        ((share, dim), F32),
        ((tiny_rows, quarter), F32),
        ((STREAMS, ffn_part), F32),
    ]
    if rel_part:
        outs.append(((share, rel_part * STREAMS), F32))
    return chain(kernel, outs, blocks, scalars=[devices], after=after, room=6)


class Layer:
    pass


def own_columns(matrix, here):
    width = matrix.shape[-1] // STREAMS
    return lax.dynamic_slice_in_dim(matrix, here * width, width, axis=matrix.ndim - 1)


def per_device(
    enc_input, pred_input, cotangent, bucket_len, pad_len, rel_table,
    enc_qkv, enc_out, enc_ffn_in, enc_ffn_out, enc_ffn_bias, enc_bias, enc_gain, enc_shift,
    dec_qkv, dec_out, dec_rel, dec_rel_bias, dec_ffn_in, dec_ffn_out, dec_ffn_bias, dec_bias, dec_gain, dec_shift,
):
    chain = Chain()
    here = lax.axis_index("stream")
    n = lax.axis_size("dp")
    group = lax.axis_index("dp")
    place = ring_place(group, n)
    rows = enc_input.shape[0]
    total = STREAMS * rows
    dim = enc_input.shape[1]
    share = enc_out.shape[0]
    quarter = dim // STREAMS
    ffn_share = enc_ffn_out.shape[0]
    ffn_part = ffn_share // STREAMS
    rel_all = dec_rel.shape[1]
    rel_part = rel_all // STREAMS
    fixed = 4 * share
    half = share // 2

    bucket = bucket_len[0]
    starts = []
    for j in XOR:
        holder = here ^ j
        for chunk in range(2):
            starts.append(jnp.where(bucket == total, holder * rows + chunk * 64, chunk * bucket + holder * 64))
    meta = jnp.stack([v.astype(jnp.int32) for v in starts + [bucket, pad_len[0, 0], pad_len[0, 1]]])
    devices = jnp.stack([here ^ j for j in XOR]).astype(jnp.int32)
    ring_index = jnp.stack([ring_member(place - o, n) for o in range(n)]).astype(jnp.int32)
    tables = rel_tables(rel_table, total)

    smalls = (
        enc_ffn_bias[None], enc_bias, enc_gain, enc_shift, dec_rel_bias[None],
        dec_ffn_bias[None], dec_bias, dec_gain, dec_shift, dec_rel_bias[None],
    )
    small_rows = 16

    def pins(pieces, stage):
        k = stage * (n // 2) // 4
        return [piece for _, _, piece in pieces[2 * k - 1 : 2 * k + 1]]

    def attention_regions(extra):
        regions = [(i * share, (i + 1) * share, 0, quarter, 0, 0, i * quarter) for i in range(3)]
        regions.append((fixed - share, fixed, 0, quarter, 1, 0, 0))
        return regions + extra

    shapes = [(share, 3 * quarter), (share, quarter)]

    enc_pieces = ring_pieces(pack_attention(chain, devices, enc_qkv, enc_out, smalls=smalls), n)
    enc_quads = gather_rows(enc_input)
    pred_quads = [gather_rows(pred_input[i]) for i in range(2)]
    def ffn_gather(matrix_in, matrix_out, after=()):
        packed = pack_ffn(chain, devices, here, matrix_in, matrix_out, n, after)
        return lax.all_gather(packed, "dp", axis=0, tiled=False)

    enc_ffn = ffn_gather(enc_ffn_in, enc_ffn_out, pins(enc_pieces, 1))
    dec_pieces = ring_pieces(pack_attention(chain, devices, dec_qkv, dec_out, rel=dec_rel, after=pins(enc_pieces, 4)), n)
    dec_ffn = ffn_gather(dec_ffn_in, dec_ffn_out)

    def turn_out(columns):
        blocks = columns.reshape(dim, quarter)
        sent = [lax.dynamic_slice_in_dim(blocks, (here ^ j) * quarter, quarter, axis=0) for j in XOR]
        return jnp.concatenate(by_absolute(turn_blocks(sent), here), axis=1)

    def turn_out_back(grad):
        sent = [lax.dynamic_slice_in_dim(grad, (here ^ j) * quarter, quarter, axis=1) for j in XOR]
        return jnp.concatenate(by_absolute(turn_blocks(sent), here), axis=0).reshape(n, share, quarter)

    enc_wqkv, enc_wout, small_all = assemble(
        chain,
        enc_pieces,
        ring_index,
        attention_regions([(fixed, fixed + small_rows, 0, quarter, 2, 0, 0)]),
        shapes + [(small_rows, quarter)],
        n,
    )

    small_all = small_all.astype(F32)

    def attention_layer(number, wqkv, wout):
        w = Layer()
        w.qkv = wqkv.reshape(dim, 3 * quarter)
        w.out = turn_out(wout)
        block = small_all[:, 8 * number : 8 * number + 8]
        w.ffn_bias = lax.dynamic_slice_in_dim(block, here, 1, axis=1)[:, 0, share : 2 * share].reshape(1, -1)
        w.small = jnp.transpose(block[:, :, :share], (1, 0, 2)).reshape(8, dim)
        mine = own_columns(w.small, here)
        w.qkv_bias = jnp.concatenate([mine[0:1], jnp.zeros_like(mine[0:1]), mine[1:2]], axis=1)
        return w

    enc = attention_layer(0, enc_wqkv, enc_wout)
    enc_all, enc_heads = project(chain, enc_quads, enc, False)
    enc_context, enc_lse, _ = attention_forward(chain, meta, enc_heads)
    scatter = Scatter(out_project(chain, enc_context, enc))
    scatter.middle(chain, pins(dec_pieces, 1))
    enc_unit0, enc_inverse0, low = norm_first(chain, enc_input, scatter.parts(), enc, after=pins(dec_pieces, 2))
    quads = gather_rows(low)
    enc.ffn = enc_ffn
    *parts, enc_hidden, enc_active, enc_slope = ffn_forward(chain, quads, enc, after=pins(dec_pieces, 3))
    scatter = Scatter(parts)
    scatter.middle(chain, pins(dec_pieces, 4))
    dec_wqkv, dec_wout, dec_wrel = assemble(
        chain,
        dec_pieces,
        ring_index,
        attention_regions(
            [
                (fixed, fixed + half, 0, rel_part, 2, 0, 0),
                (fixed, fixed + half, rel_part, 2 * rel_part, 2, half, 0),
            ]
        ),
        shapes + [(share, rel_part)],
        n,
    )
    dec = attention_layer(1, dec_wqkv, dec_wout)
    dec.rel = dec_wrel.reshape(dim, rel_part)
    dec.rel_bias = own_columns(small_all[:, 12, share : share + rel_all // n].reshape(1, -1), here)
    alls, heads, rels = [None] * 3, [None] * 3, [None] * 3

    def project_stream(i, quads):
        alls[i], heads[i], rels[i] = project(chain, quads, dec, True)

    project_stream(1, pred_quads[0])
    project_stream(2, pred_quads[1])
    enc_unit1, enc_inverse1, main_rows, main_low = norm_second(chain, enc_unit0, scatter.parts(), enc)
    main_quads = gather_rows(main_low)

    stream_inputs = (main_rows, pred_input[0], pred_input[1])
    project_stream(0, main_quads)
    contexts, lses = [None] * 3, [None] * 3

    def attend(i, after=()):
        contexts[i], lses[i], parts = attention_forward(
            chain, meta, heads[i], None if i == 0 else heads[0], rels[i], tables, dec.out, after
        )
        return Scatter(parts)

    def staged(work, finish):
        scatters = []
        for i in range(3):
            scatters.append(work(i))
            if i:
                scatters[i - 1].middle(chain)
        results = [finish(0, scatters[0])]
        scatters[2].middle(chain)
        results += [finish(1, scatters[1]), finish(2, scatters[2])]
        return results

    firsts = staged(
        lambda i: attend(i),
        lambda i, scatter: norm_first(chain, stream_inputs[i], scatter.parts(), dec),
    )
    hidden_quads = [gather_rows(first[2]) for first in firsts]
    dec.ffn = dec_ffn
    kept = [None] * 3

    def feed(i):
        *parts, hidden, active, slope = ffn_forward(chain, hidden_quads[i], dec)
        kept[i] = (hidden, active, slope)
        return Scatter(parts)

    seconds = staged(
        feed, lambda i, scatter: norm_second_both(chain, firsts[i][0], scatter.parts(), cotangent[i], dec)
    )
    outputs = [second[0] for second in seconds]

    branch_quads = [gather_rows(second[2]) for second in seconds]
    branches = [None] * 3

    def feed_back(i):
        *parts, branch, inner, inner_sum = ffn_backward(chain, branch_quads[i], kept[i][2], dec)
        branches[i] = (branch, inner, inner_sum)
        return Scatter(parts)

    backs = staged(
        feed_back,
        lambda i, scatter: norm_first_back(
            chain, seconds[i][1], scatter.parts(), firsts[i][0], firsts[i][1], dec
        ),
    )
    attended_quads = [gather_rows(back[1]) for back in backs]

    def ffn_grads(pairs):
        grad_in = sum(dot_tn(hidden, inner) for hidden, _, inner, _ in pairs).astype(BF)
        grad_out = sum(dot_tn(active, branch) for _, active, _, branch in pairs).astype(BF)
        return grad_in.reshape(n, share, dim), grad_out.reshape(n, ffn_part, dim)

    def ffn_sum(pairs):
        regions = [(0, 0, 0, share), (1, 0, share, ffn_part)]
        return RingSum(chain, list(ffn_grads(pairs)), regions, dim, n, ring_index)

    def advance(ring, stage):
        result = None
        while ring.done < stage * (n // 2 + 1) // 5:
            result = ring.step()
            ring.done += 1
        return result

    dec_ffn_total = lax.psum_scatter(
        jnp.concatenate(
            ffn_grads([(kept[i][0], kept[i][1], branches[i][1], branches[i][0]) for i in range(3)]), axis=1
        ),
        "dp",
        scatter_dimension=0,
        tiled=False,
    )
    results = [None] * 3
    for i in (1, 2, 0):
        results[i] = attention_backward(
            chain, meta, heads[i], attended_quads[i], dec.out, lses[i], None if i == 0 else heads[0], rels[i], tables
        )
    dheads, head_sums, rel_sums = [None] * 3, [None] * 3, [None] * 3

    def back_project(i):
        dq, dk, dv, _, drel = results[i][:5]
        keys = [r[1] for r in results] if i == 0 else [results[i][5]]
        vals = [r[2] for r in results] if i == 0 else [results[i][6]]
        *parts, dheads[i], head_sums[i], rel_sums[i] = project_back(chain, dq, keys, vals, drel, dec)
        return Scatter(parts)

    main_scatter = back_project(0)
    pred_scatters = [back_project(1)]
    main_scatter.middle(chain)
    pred_scatters.append(back_project(2))
    pred_scatters[0].middle(chain)

    def widen(part, size):
        return lax.dynamic_update_slice(jnp.zeros((1, size), F32), part, (0, here * part.shape[1]))

    def small_pack(inner_sum, tiny0, tiny1, heads_sum, rel_sum=None):
        wide = jnp.concatenate(
            [
                widen(heads_sum[:, :quarter], dim),
                widen(heads_sum[:, 2 * quarter :], dim),
                tiny0[0:1],
                tiny1[0:1],
                tiny0[1:2],
                tiny1[1:2],
                tiny0[2:3],
                tiny1[2:3],
            ],
            axis=0,
        )
        left = jnp.transpose(wide.reshape(8, n, share), (1, 0, 2))
        spare = quarter - share
        lines = [jnp.pad(inner_sum.reshape(n, 1, ffn_part), ((0, 0), (0, 0), (0, spare - ffn_part)))]
        if rel_sum is not None:
            line = widen(rel_sum, rel_all).reshape(n, 1, rel_all // n)
            lines.append(jnp.pad(line, ((0, 0), (0, 0), (0, spare - rel_all // n))))
        lines.append(jnp.zeros((n, 8 - len(lines), spare), F32))
        packed = jnp.concatenate([left, jnp.concatenate(lines, axis=1)], axis=2)
        return jnp.pad(packed, ((0, 0), (0, 8), (0, 0))).astype(BF)

    def attention_grads(qkv_grad, out_grad, more):
        return [qkv_grad.astype(BF).reshape(n, share, 3 * quarter), turn_out_back(out_grad.astype(BF))] + more

    def attention_ring(*grads):
        arrays = attention_grads(*grads)
        regions = [(0, i * quarter, i * share, share) for i in range(3)] + [(1, 0, 3 * share, share)]
        at = fixed
        for which, array in enumerate(arrays[2:]):
            regions.append((2 + which, 0, at, array.shape[1]))
            at += array.shape[1]
        return RingSum(chain, arrays, regions, quarter, n, ring_index)

    dec_out_part = sum(dot_tn(contexts[i], results[i][3]) for i in range(3))
    dec_qkv_part = sum(dot_tn(alls[i], dheads[i]) for i in range(3))
    rel_blocks = sum(dot_tn(alls[i], results[i][4]) for i in range(3)).astype(BF).reshape(n, share, rel_part)
    dec_small = small_pack(
        sum(branches[i][2] for i in range(3)),
        sum(backs[i][2] for i in range(3)),
        sum(seconds[i][3] for i in range(3)),
        sum(head_sums),
        sum(rel_sums),
    )
    wide, *others = attention_grads(
        dec_qkv_part,
        dec_out_part,
        [jnp.concatenate([rel_blocks[:, :half], rel_blocks[:, half:]], axis=2), dec_small],
    )
    thirds = [wide[:, :, i * quarter : (i + 1) * quarter] for i in range(3)]
    dec_total = lax.psum_scatter(
        jnp.concatenate(thirds + others, axis=1), "dp", scatter_dimension=0, tiled=False
    )

    enc_sum_grad, low, enc_tiny1 = norm_second_back(
        chain, backs[0][0], main_scatter.parts(), enc_unit1, enc_inverse1, enc
    )
    quads = gather_rows(low)
    pred_scatters[1].middle(chain)
    *parts, enc_branch, enc_inner, enc_inner_sum = ffn_backward(chain, quads, enc_slope, enc)
    scatter = Scatter(parts)
    pred_grads = [input_gradient(chain, backs[1][0], pred_scatters[0].parts())]
    scatter.middle(chain)
    pred_grads.append(input_gradient(chain, backs[2][0], pred_scatters[1].parts()))
    enc_ffn_ring = ffn_sum([(enc_hidden, enc_active, enc_inner, enc_branch)])
    advance(enc_ffn_ring, 1)
    dec_ffn_blocks = gather_rows(dec_ffn_total)
    residual, attended_low, enc_tiny0 = norm_first_back(
        chain, enc_sum_grad, scatter.parts(), enc_unit0, enc_inverse0, enc
    )
    quads = gather_rows(attended_low)
    advance(enc_ffn_ring, 2)
    dq, dk, dv, attended = attention_backward(chain, meta, enc_heads, quads, enc.out, enc_lse)
    *parts, enc_dheads, enc_head_sum = project_back(chain, dq, [dk], [dv], None, enc)
    scatter = Scatter(parts)
    advance(enc_ffn_ring, 3)
    enc_ring = attention_ring(
        dot_tn(enc_all, enc_dheads),
        dot_tn(enc_context, attended),
        [small_pack(enc_inner_sum, enc_tiny0, enc_tiny1, enc_head_sum)],
    )
    advance(enc_ring, 1)
    scatter.middle(chain)
    advance(enc_ffn_ring, 4)
    advance(enc_ring, 2)
    dec_in_grad, dec_back_grad = place_ffn(chain, devices, here, dec_ffn_blocks, share, n)
    enc_input_grad = input_gradient(chain, residual, scatter.parts())
    advance(enc_ring, 3)
    enc_ffn_blocks = gather_rows(advance(enc_ffn_ring, 5))
    dec_blocks = gather_rows(dec_total)
    advance(enc_ring, 4)
    dec_results = place_attention(chain, devices, dec_blocks, share, ffn_part, rel_part)
    enc_blocks = gather_rows(advance(enc_ring, 5))
    enc_in_grad, enc_back_grad = place_ffn(chain, devices, here, enc_ffn_blocks, share, n)
    enc_results = place_attention(chain, devices, enc_blocks, share, ffn_part, 0)

    def tiny_out(results):
        tiny, inner = results[2], results[3]
        return inner.reshape(-1), tiny[0:4, :share], tiny[4:6, :share], tiny[6:8, :share]

    return (
        jnp.stack(outputs),
        enc_input_grad,
        jnp.stack(pred_grads),
        enc_results[0],
        enc_results[1],
        enc_in_grad,
        enc_back_grad,
        *tiny_out(enc_results),
        dec_results[0],
        dec_results[1],
        dec_results[4],
        dec_results[2][1, share : share + rel_all // n],
        dec_in_grad,
        dec_back_grad,
        *tiny_out(dec_results),
    )


def solution(mesh):
    tokens = P(("stream", "dp"), None)
    streams = P(None, ("stream", "dp"), None)
    first, second, cube = P("dp", None), P(None, "dp"), P(None, "dp", None)
    flat = P("dp")
    return jax.shard_map(
        per_device,
        mesh=mesh,
        in_specs=(
            tokens, streams, streams, flat, first, P(),
            cube, first, first, first, flat, second, second, second,
            cube, first, first, flat, first, first, flat, second, second, second,
        ),
        out_specs=(
            streams, tokens, streams,
            cube, first, first, first, flat, second, second, second,
            cube, first, first, flat, first, first, flat, second, second, second,
        ),
        check_vma=False,
    )
```

```python
from functools import partial

import jax
import jax.numpy as jnp
from jax import lax
from jax.experimental import pallas as pl
from jax.experimental.pallas import tpu as pltpu
from jax.sharding import PartitionSpec as P

H = 16
NB = 32
HD = 64
EPSILON = 1e-05
MASKED = -1000000000.0
BF = jnp.bfloat16
F32 = jnp.float32
TILE = 128
STREAMS = 4
XOR = (0, 2, 1, 3)
MIB = 1024 * 1024


def dot(a, b):
    return jnp.dot(a, b, preferred_element_type=F32)


def dot_nt(a, b):
    return lax.dot_general(a, b, (((1,), (1,)), ((), ())), preferred_element_type=F32)


def dot_tn(a, b):
    return lax.dot_general(a, b, (((0,), (0,)), ((), ())), preferred_element_type=F32)


def swap(values, bit):
    return lax.ppermute(values, "stream", [(i, i ^ bit) for i in range(STREAMS)])


class Chain:
    def __init__(self):
        self.last = None

    def __call__(self, kernel, outs, args, scalars=(), away=(), stored=(), scratch=(), after=(), room=3, cost=1):
        ties = list(after)
        if self.last is not None:
            ties.append(self.last)
        reads = len(scalars) + len(args) + len(away) + len(stored)

        def body(*refs):
            kernel(*refs[:reads], *refs[reads + len(ties) :])

        vmem = pl.BlockSpec(memory_space=pltpu.VMEM)
        anywhere = pl.BlockSpec(memory_space=pl.ANY)
        results = pl.pallas_call(
            body,
            out_shape=[jax.ShapeDtypeStruct(shape, kind) for shape, kind in outs],
            in_specs=[pl.BlockSpec(memory_space=pltpu.SMEM)] * len(scalars)
            + [vmem] * len(args)
            + [anywhere] * len(away)
            + [pl.BlockSpec(memory_space=pltpu.HBM)] * len(stored)
            + [anywhere] * len(ties),
            out_specs=[vmem] * len(outs),
            scratch_shapes=list(scratch),
            compiler_params=pltpu.CompilerParams(vmem_limit_bytes=room * MIB),
            cost_estimate=pl.CostEstimate(flops=10**10, bytes_accessed=10**7, transcendentals=0),
        )(*scalars, *args, *away, *[pltpu.with_memory_space_constraint(a, pltpu.HBM) for a in stored], *ties)
        self.last = results[0]
        return results


def gather_rows(rows):
    far = swap(rows, 2)
    return rows, far, swap(rows, 1), swap(far, 1)


class Scatter:
    def __init__(self, parts):
        self.own, self.across, near = parts
        self.near = swap(near, 1)

    def middle(self, chain, after=()):
        rows, dim = self.own.shape

        def kernel(across_ref, near_ref, out_ref):
            out_ref[...] = (across_ref[...] + near_ref[rows:, :].astype(F32)).astype(BF)

        (low,) = chain(kernel, [((rows, dim), BF)], [self.across, self.near], after=after, cost=0.1)
        self.far = swap(low, 2)

    def parts(self):
        return [self.own, self.near, self.far]


def scattered(own_ref, near_ref, far_ref):
    rows = own_ref.shape[0]
    return own_ref[...] + near_ref[:rows, :].astype(F32) + far_ref[...].astype(F32)


def scatter_outs(rows, dim):
    return [((rows, dim), F32), ((rows, dim), F32), ((2 * rows, dim), BF)]


def store_partials(part, value, own_ref, across_ref, near_ref):
    rows = own_ref.shape[0]
    if part == 0:
        own_ref[...] = value[:rows, :]
        across_ref[...] = value[rows:, :]
    else:
        near_ref[...] = value.astype(BF)


def join(target, refs):
    rows = refs[0].shape[0]
    for i, ref in enumerate(refs):
        target[i * rows : (i + 1) * rows, :] = ref[...]


def turn_blocks(blocks):
    far = swap(jnp.stack([blocks[1], blocks[3]]), 2)
    near = swap(jnp.stack([blocks[2], far[1]]), 1)
    return [blocks[0], far[0], near[0], near[1]]


def by_absolute(blocks, here):
    stacked = jnp.stack([blocks[XOR.index(j)] for j in range(4)])
    return [lax.dynamic_index_in_dim(stacked, here ^ a, 0, keepdims=False) for a in range(4)]


class Turn:
    def __init__(self, chain, devices, array, by_rows):
        self.devices, self.by_rows = devices, by_rows
        size = array.shape[0 if by_rows else 1] // STREAMS
        self.size = size

        def kernel(devices_ref, array_ref, *part_refs):
            for i in range(STREAMS):
                place = pl.ds(pl.multiple_of(devices_ref[i] * size, size), size)
                part_refs[i][...] = (array_ref[place, :] if by_rows else array_ref[:, place]).astype(BF)

        own, *others = chain(kernel, [((size, size), BF)] * STREAMS, [array], scalars=[devices])
        self.parts = [own] + [swap(part, bit) for part, bit in zip(others, XOR[1:])]

    def join(self, chain, after=()):
        size, by_rows = self.size, self.by_rows

        def kernel(devices_ref, *refs):
            for i in range(STREAMS):
                place = pl.ds(pl.multiple_of(devices_ref[i] * size, size), size)
                if by_rows:
                    refs[-1][:, place] = refs[i][...]
                else:
                    refs[-1][place, :] = refs[i][...]

        shape = (size, STREAMS * size) if by_rows else (STREAMS * size, size)
        return chain(kernel, [(shape, BF)], self.parts, scalars=[self.devices], after=after)[0]


def ring_order(n):
    return list(range(0, n, 2)) + list(range(n - 1, 0, -2))


def ring_member(place, n):
    place = lax.rem(place + 2 * n, n)
    return jnp.where(place < n // 2, 2 * place, 2 * (n - place) - 1)


def ring_place(g, n):
    return jnp.where(g % 2 == 0, g // 2, n - (g + 1) // 2)


def ring_step(values, n, step):
    order = ring_order(n)
    pairs = [(order[i], order[(i + step) % n]) for i in range(n)]
    return lax.ppermute(values, "dp", pairs)


def ring_pieces(own, n):
    rows = own.shape[0]
    pieces = [(0, 0, own)]
    ahead = back = own
    for k in range(1, n // 2):
        ahead = ring_step(ahead, n, 1)
        back = ring_step(back, n, -1)
        pieces += [(k, 0, ahead), (n - k, 0, back)]
    half = halved(rows)
    top = ring_step(ahead[:half], n, 1)
    bottom = ring_step(back[half:], n, -1)
    pieces += [(n // 2, 0, top), (n // 2, half, bottom)]
    return pieces


def halved(rows):
    return rows // 32 * 16


def assemble(chain, pieces, index, regions, shapes, n, after=()):
    moves = []
    for number, (behind, first, piece) in enumerate(pieces):
        last = first + piece.shape[0]
        for r0, r1, c0, c1, which, to_row, to_col in regions:
            lo, hi = max(r0, first), min(r1, last)
            if lo < hi:
                moves.append((number, behind, lo - first, hi - first, c0, c1, which, to_row + lo - r0, to_col))

    def kernel(index_ref, *refs):
        sources = refs[: len(pieces)]
        outs = refs[len(pieces) : -1]
        copy_all(
            [
                (
                    sources[number].at[lo:hi, c0:c1],
                    outs[which].at[index_ref[behind], row : row + hi - lo, col : col + c1 - c0],
                )
                for number, behind, lo, hi, c0, c1, which, row, col in moves
            ],
            refs[-1],
        )

    return chain(
        kernel,
        [((n,) + shape, BF) for shape in shapes],
        [],
        scalars=[index],
        away=[piece for _, _, piece in pieces],
        scratch=[pltpu.SemaphoreType.DMA((len(moves),))],
        after=after,
    )


def unpack(chain, packed, regions, shapes, after=()):
    n = packed.shape[0]

    def kernel(packed_ref, *refs):
        copy_all(
            [
                (
                    packed_ref.at[:, r0:r1, c0:c1],
                    refs[which].at[:, row : row + r1 - r0, col : col + c1 - c0],
                )
                for r0, r1, c0, c1, which, row, col in regions
            ],
            refs[-1],
        )

    return chain(
        kernel,
        [((n,) + shape, BF) for shape in shapes],
        [],
        away=[packed],
        scratch=[pltpu.SemaphoreType.DMA((len(regions),))],
        after=after,
    )


class RingSum:
    def __init__(self, chain, arrays, regions, columns, n, index):
        self.chain, self.arrays, self.regions, self.n, self.index = chain, arrays, regions, n, index
        self.columns = columns
        self.rows = sum(r[3] for r in regions)
        self.half = halved(self.rows)
        self.up = self.down = None
        self.done = 0
        self.left = n // 2

    def fetch(self, index_ref, offsets, refs, buffers, sems):
        copies = []
        for slot, offset in enumerate(offsets):
            g = index_ref[offset]
            for i, (which, column, row, rows) in enumerate(self.regions):
                copies.append(
                    pltpu.make_async_copy(
                        refs[which].at[g, :, column : column + self.columns],
                        buffers.at[slot, row : row + rows, :],
                        sems.at[slot * len(self.regions) + i],
                    )
                )
                copies[-1].start()
        for copy in copies:
            copy.wait()

    def step(self, after=()):
        rows, half, columns, count = self.rows, self.half, self.columns, len(self.arrays)
        first = self.left == self.n // 2
        last = self.left == 0
        joined = self.left == self.n // 2 - 1
        offsets = [(self.n - self.left) % self.n] + ([] if first or last else [self.left])
        received = [] if first else [self.up, self.down]

        def kernel(index_ref, *refs):
            ups = refs[: len(received)]
            arrays = refs[len(received) : len(received) + count]
            outs = refs[len(received) + count : -2]
            buffers, sems = refs[-2:]
            self.fetch(index_ref, offsets, arrays, buffers, sems)
            if first:
                outs[0][...] = buffers[0, :half, :]
                outs[1][...] = buffers[0, half:, :]
            elif last:
                outs[0][...] = (
                    buffers[0].astype(F32) + ups[0][...].astype(F32) + ups[1][...].astype(F32)
                ).astype(BF)
            elif joined:
                outs[0][:half, :] = (buffers[0, :half, :].astype(F32) + ups[0][...].astype(F32)).astype(BF)
                outs[0][half:, :] = buffers[0, half:, :]
                outs[1][:half, :] = buffers[1, :half, :]
                outs[1][half:, :] = (buffers[1, half:, :].astype(F32) + ups[1][...].astype(F32)).astype(BF)
            else:
                outs[0][...] = (buffers[0].astype(F32) + ups[0][...].astype(F32)).astype(BF)
                outs[1][...] = (buffers[1].astype(F32) + ups[1][...].astype(F32)).astype(BF)

        if first:
            outs = [((half, columns), BF), ((rows - half, columns), BF)]
        else:
            outs = [((rows, columns), BF)] * (1 if last else 2)
        results = self.chain(
            kernel,
            outs,
            received,
            scalars=[self.index],
            away=self.arrays,
            scratch=[
                pltpu.VMEM((len(offsets), rows, columns), BF),
                pltpu.SemaphoreType.DMA((len(offsets) * len(self.regions),)),
            ],
            after=after,
        )
        self.left -= 1
        if last:
            return results[0]
        self.up = ring_step(results[0], self.n, 1)
        self.down = ring_step(results[1], self.n, -1)
        return None


def tile_width(t, causal, total):
    return TILE * (t + 1) if causal else total


def head_mask(e):
    lane = lax.broadcasted_iota(jnp.int32, (1, TILE), 1)
    return ((lane // HD) == e).astype(F32)


def rel_mask(h):
    lane = lax.broadcasted_iota(jnp.int32, (1, TILE), 1)
    return ((lane // NB) == h).astype(F32)


def allowed_keys(t, width, meta, causal, strict):
    bucket = meta[8]
    shape = (TILE, width)
    row = lax.broadcasted_iota(jnp.int32, shape, 0) + t * TILE
    col = lax.broadcasted_iota(jnp.int32, shape, 1)
    pos = col & (bucket - 1)
    first = col < bucket
    limit = bucket - jnp.where(first, meta[9], meta[10])
    allowed = (pos < limit) & ((row < bucket) == first)
    if causal:
        allowed = allowed & ((col < row) if strict else (col <= row))
    return allowed


def load_rows(meta, target, source, c0, c1):
    for chunk in range(8):
        start = pl.multiple_of(meta[chunk], 64)
        target[pl.ds(start, 64), :] = source[chunk * 64 : chunk * 64 + 64, c0:c1].astype(target.dtype)


def store_rows(meta, target, source, c0, c1):
    for chunk in range(8):
        start = pl.multiple_of(meta[chunk], 64)
        target[chunk * 64 : chunk * 64 + 64, c0:c1] = source[pl.ds(start, 64), :].astype(target.dtype)


def rel_bias(rel_rows, h, table):
    high = rel_rows.astype(BF)
    rest = (rel_rows - high.astype(F32)).astype(BF)
    mask = rel_mask(h)
    both = jnp.concatenate(
        [(high.astype(F32) * mask).astype(BF), (rest.astype(F32) * mask).astype(BF)], axis=1
    )
    spread = dot(both, table)
    return pltpu.roll(spread, 0, 1, stride=1, stride_axis=0)


def table_slice(t, width):
    first = sum(TILE * (u + 1) for u in range(t))
    return slice(first, first + width)


def attention_forward(chain, meta, qkv, main=None, rel=None, tables=None, w_out=None, after=()):
    total = qkv.shape[0]
    width_all = qkv.shape[1] // 3
    heads = width_all // HD
    causal = rel is not None
    own = main is not None
    project = w_out is not None
    block = total // STREAMS

    def kernel(meta_ref, *refs):
        refs = list(refs)
        qkv_ref = refs.pop(0)
        main_ref = refs.pop(0) if own else qkv_ref
        rel_ref, table_ref, hot_ref = (refs.pop(0), refs.pop(0), refs.pop(0)) if causal else (None,) * 3
        out_ref = refs.pop(0) if project else None
        ctx_ref, lse_ref = refs.pop(0), refs.pop(0)
        parts_refs = [refs.pop(0) for _ in range(3)] if project else None
        qs, ks, vs, cs, kt = refs[:5]
        refs = refs[5:]
        rs = refs.pop(0) if causal else None
        load_rows(meta_ref, qs, qkv_ref, 0, width_all)
        load_rows(meta_ref, ks, main_ref, width_all, 2 * width_all)
        load_rows(meta_ref, vs, main_ref, 2 * width_all, 3 * width_all)
        if causal:
            load_rows(meta_ref, rs, rel_ref, 0, rel.shape[1])
        if own:
            kn, vn = refs
            load_rows(meta_ref, kn, qkv_ref, width_all, 2 * width_all)
            load_rows(meta_ref, vn, qkv_ref, 2 * width_all, 3 * width_all)
        kt[...] = ks[...].T
        for t in range(total // TILE):
            rows = slice(TILE * t, TILE * (t + 1))
            width = tile_width(t, causal, total)
            allowed = allowed_keys(t, width, meta_ref, causal, own)
            lse_lane = lax.broadcasted_iota(jnp.int32, (TILE, TILE), 1)
            lse = jnp.zeros((TILE, TILE), F32)
            query = [(qs[rows, HD * h : HD * (h + 1)].astype(F32) * HD**-0.5).astype(BF) for h in range(heads)]
            scores = [dot(query[h], kt[HD * h : HD * (h + 1), 0:width]) for h in range(heads)]
            if causal:
                biases = [rel_bias(rs[rows, :], h, table_ref[:, table_slice(t, width)]) for h in range(heads)]
                scores = [a + b for a, b in zip(scores, biases)]
            scores = [jnp.where(allowed, a, MASKED) for a in scores]
            tops = [jnp.max(a, axis=1, keepdims=True) for a in scores]
            if own:
                own_scores = [
                    jnp.sum(
                        query[h].astype(F32) * kn[rows, HD * h : HD * (h + 1)].astype(F32), axis=1, keepdims=True
                    )
                    + jnp.sum(rs[rows, :] * (hot_ref[...] * rel_mask(h)), axis=1, keepdims=True)
                    for h in range(heads)
                ]
                tops = [jnp.maximum(a, b) for a, b in zip(tops, own_scores)]
            expos = [jnp.exp(a - b) for a, b in zip(scores, tops)]
            sums = [jnp.sum(a, axis=1, keepdims=True) for a in expos]
            if own:
                own_expos = [jnp.exp(a - b) for a, b in zip(own_scores, tops)]
                sums = [a + b for a, b in zip(sums, own_expos)]
            inverses = [1.0 / a for a in sums]
            parts = [
                dot((expos[h] * inverses[h]).astype(BF), vs[0:width, HD * h : HD * (h + 1)]) for h in range(heads)
            ]
            if own:
                own_probs = [own_expos[h] * inverses[h] for h in range(heads)]
                parts = [
                    parts[h] + own_probs[h] * vn[rows, HD * h : HD * (h + 1)].astype(F32) for h in range(heads)
                ]
            cs[rows, :] = jnp.concatenate(parts, axis=1).astype(BF)
            for h in range(heads):
                lse = jnp.where(lse_lane == h, tops[h] + jnp.log(sums[h]), lse)
                if own:
                    lse = jnp.where(lse_lane == heads + h, own_probs[h], lse)
            lse_ref[rows, :] = lse
        store_rows(meta_ref, ctx_ref, cs, 0, width_all)
        if project:
            for part in range(2):
                value = dot(ctx_ref[part * 2 * block : (part + 1) * 2 * block, :], out_ref[...])
                store_partials(part, value, *parts_refs)

    args = [qkv]
    scratch = [pltpu.VMEM((total, width_all), BF) for _ in range(4)] + [pltpu.VMEM((width_all, total), BF)]
    outs = [((total, width_all), BF), ((total, TILE), F32)]
    if own:
        args.append(main)
    if causal:
        args += [rel, tables[0], tables[2]]
        scratch.append(pltpu.VMEM((total, rel.shape[1]), F32))
    if own:
        scratch += [pltpu.VMEM((total, width_all), BF) for _ in range(2)]
    if project:
        args.append(w_out)
        outs += scatter_outs(block, w_out.shape[1])
    context, lse, *parts = chain(kernel, outs, args, scalars=[meta], scratch=scratch, after=after, room=8, cost=6)
    return context, lse, parts


def attention_backward(chain, meta, qkv, attended, w_out, lse, main=None, rel=None, tables=None, after=()):
    total = qkv.shape[0]
    width_all = qkv.shape[1] // 3
    heads = width_all // HD
    causal = rel is not None
    own = main is not None

    def kernel(meta_ref, *refs):
        refs = list(refs)
        qkv_ref = refs.pop(0)
        attended_refs = [refs.pop(0) for _ in range(STREAMS)]
        out_ref, lse_ref = refs.pop(0), refs.pop(0)
        main_ref = refs.pop(0) if own else qkv_ref
        rel_ref, table_ref, back_ref, hot_ref, flip_ref = (
            [refs.pop(0) for _ in range(5)] if causal else (None,) * 5
        )
        dq_ref, dk_ref, dv_ref, joined_ref = refs[:4]
        refs = refs[4:]
        drel_ref = refs.pop(0) if causal else None
        dkn_ref, dvn_ref = (refs.pop(0), refs.pop(0)) if own else (None, None)
        qs, ks, vs, gs, dqs, dks, kt, vt, qt, gt, dkt, dvt = refs[:12]
        refs = refs[12:]
        rs, drs = (refs.pop(0), refs.pop(0)) if causal else (None, None)
        join(joined_ref, attended_refs)
        dqs[...] = dot_nt(joined_ref[...], out_ref[...])
        load_rows(meta_ref, qs, qkv_ref, 0, width_all)
        load_rows(meta_ref, ks, main_ref, width_all, 2 * width_all)
        load_rows(meta_ref, vs, main_ref, 2 * width_all, 3 * width_all)
        load_rows(meta_ref, gs, dqs, 0, width_all)
        if causal:
            load_rows(meta_ref, rs, rel_ref, 0, rel.shape[1])
        if own:
            kn, vn, dkn, dvn = refs
            load_rows(meta_ref, kn, qkv_ref, width_all, 2 * width_all)
            load_rows(meta_ref, vn, qkv_ref, 2 * width_all, 3 * width_all)
        qs[...] = (qs[...].astype(F32) * HD**-0.5).astype(BF)
        kt[...] = ks[...].T
        vt[...] = vs[...].T
        qt[...] = qs[...].T
        gt[...] = gs[...].T
        dkt[...] = jnp.zeros_like(dkt)
        dvt[...] = jnp.zeros_like(dvt)
        each = range(heads)
        feat = [slice(HD * h, HD * (h + 1)) for h in each]
        for t in range(total // TILE):
            rows = slice(TILE * t, TILE * (t + 1))
            width = tile_width(t, causal, total)
            allowed = allowed_keys(t, width, meta_ref, causal, own)
            norms = [lse_ref[rows, h : h + 1] for h in each]
            query = [qs[rows, feat[h]] for h in each]
            grad = [gs[rows, feat[h]] for h in each]
            scores = [dot(query[h], kt[feat[h], 0:width]) for h in each]
            dprobs = [dot(grad[h], vt[feat[h], 0:width]) for h in each]
            if causal:
                biases = [rel_bias(rs[rows, :], h, table_ref[:, table_slice(t, width)]) for h in each]
                scores = [a + b for a, b in zip(scores, biases)]
            probs = [jnp.exp(jnp.where(allowed, scores[h], MASKED) - norms[h]) for h in each]
            rowdots = [jnp.sum(probs[h] * dprobs[h], axis=1, keepdims=True) for h in each]
            if own:
                own_probs = [lse_ref[rows, heads + h : heads + h + 1] for h in each]
                own_dprobs = [
                    jnp.sum(grad[h].astype(F32) * vn[rows, feat[h]].astype(F32), axis=1, keepdims=True) for h in each
                ]
                rowdots = [rowdots[h] + own_probs[h] * own_dprobs[h] for h in each]
                own_dscores = [
                    (own_probs[h] * (own_dprobs[h] - rowdots[h])).astype(BF).astype(F32) for h in each
                ]
            dscores = [(probs[h] * (dprobs[h] - rowdots[h])).astype(BF) for h in each]
            dqs_parts = [dot(dscores[h], ks[0:width, feat[h]]) for h in each]
            if own:
                dqs_parts = [dqs_parts[h] + own_dscores[h] * kn[rows, feat[h]].astype(F32) for h in each]
                dkn[rows, :] = jnp.concatenate([own_dscores[h] * query[h].astype(F32) for h in each], axis=1)
                dvn[rows, :] = jnp.concatenate([own_probs[h] * grad[h].astype(F32) for h in each], axis=1)
            dqs[rows, :] = jnp.concatenate(dqs_parts, axis=1) * HD**-0.5
            for h in each:
                dkt[feat[h], 0:width] += dot(qt[feat[h], rows], dscores[h])
                dvt[feat[h], 0:width] += dot(gt[feat[h], rows], probs[h].astype(BF))
            if causal:
                drel = jnp.zeros((TILE, TILE), F32)
                for h in each:
                    blocks = [
                        dot(dscores[h][:, TILE * b : TILE * (b + 1)], flip_ref[...])
                        for b in reversed(range(width // TILE))
                    ]
                    mirrored = jnp.concatenate(blocks, axis=1) if len(blocks) > 1 else blocks[0]
                    turned = pltpu.roll(mirrored, 0, 1, stride=1, stride_axis=0).astype(BF)
                    drel = drel + dot(turned, back_ref[table_slice(t, width), :]) * rel_mask(h)
                    if own:
                        drel = drel + own_dscores[h] * (hot_ref[...] * rel_mask(h))
                drs[rows, :] = drel
        store_rows(meta_ref, dq_ref, dqs, 0, width_all)
        dks[...] = dkt[...].T
        store_rows(meta_ref, dk_ref, dks, 0, width_all)
        dks[...] = dvt[...].T
        store_rows(meta_ref, dv_ref, dks, 0, width_all)
        if causal:
            store_rows(meta_ref, drel_ref, drs, 0, rel.shape[1])
        if own:
            store_rows(meta_ref, dkn_ref, dkn, 0, width_all)
            store_rows(meta_ref, dvn_ref, dvn, 0, width_all)

    args = [qkv, *attended, w_out, lse]
    shape = (total, width_all)
    turned = (width_all, total)
    outs = [(shape, BF), (shape, F32), (shape, F32), ((total, w_out.shape[1]), BF)]
    scratch = [pltpu.VMEM(shape, BF) for _ in range(4)] + [pltpu.VMEM(shape, F32) for _ in range(2)]
    scratch += [pltpu.VMEM(turned, BF) for _ in range(4)] + [pltpu.VMEM(turned, F32) for _ in range(2)]
    if own:
        args.append(main)
    if causal:
        args += [rel, *tables]
        outs.append(((total, rel.shape[1]), BF))
        scratch += [pltpu.VMEM((total, rel.shape[1]), F32) for _ in range(2)]
    if own:
        outs += [(shape, BF), (shape, BF)]
        scratch += [pltpu.VMEM(shape, BF) for _ in range(2)] + [pltpu.VMEM(shape, F32) for _ in range(2)]
    return chain(kernel, outs, args, scalars=[meta], scratch=scratch, after=after, room=12, cost=10 if causal else 6)


def rel_tables(rel_table, total):
    ahead, back = [], []
    for t in range(total // TILE):
        width = TILE * (t + 1)
        here = rel_table[:width]
        ahead += [jnp.flip(here[: TILE * t + 1]), jnp.flip(here[TILE * t + 1 :])]
        back += [here[width - TILE + 1 :], here[: width - TILE + 1]]
    ahead, back = jnp.concatenate(ahead), jnp.concatenate(back)
    rows = jnp.arange(2 * TILE, dtype=jnp.int32) % NB
    forward = (rows[:, None] == ahead[None, :]).astype(BF)
    backward = (back[:, None] == rows[None, :TILE]).astype(BF)
    hot = (rows[None, :TILE] == rel_table[0]).astype(F32)
    ids = jnp.arange(TILE, dtype=jnp.int32)
    flip = (ids[:, None] + ids[None, :] == TILE - 1).astype(BF)
    return forward, backward, hot, flip


def unit_of(values):
    center = values - jnp.mean(values, axis=-1, keepdims=True)
    spread = jnp.mean(center * center, axis=-1, keepdims=True)
    inverse = lax.rsqrt(spread + EPSILON)
    return center * inverse, inverse


def unit_back(grad, unit, inverse, gain):
    inner = grad * gain
    mean = jnp.mean(inner, axis=-1, keepdims=True)
    along = jnp.mean(inner * unit, axis=-1, keepdims=True)
    return inverse * (inner - mean - unit * along)


def column(values):
    return jnp.sum(values, axis=0, keepdims=True)


def tiny_sums(low, grad, unit):
    return jnp.concatenate([column(low.astype(F32)), column(grad * unit), column(grad)], axis=0)


def norm_first(chain, inputs, parts, w, after=()):
    rows, dim = inputs.shape

    def kernel(in_ref, own_ref, near_ref, far_ref, small_ref, unit_ref, inverse_ref, low_ref):
        values = in_ref[...].astype(F32) + scattered(own_ref, near_ref, far_ref) + small_ref[2:3, :]
        unit, inverse = unit_of(values)
        unit_ref[...] = unit
        inverse_ref[...] = inverse
        low_ref[...] = (unit * small_ref[4:5, :] + small_ref[6:7, :]).astype(BF)

    outs = [((rows, dim), F32), ((rows, 1), F32), ((rows, dim), BF)]
    return chain(kernel, outs, [inputs, *parts, w.small], after=after)


def norm_second(chain, unit0, parts, w, after=()):
    rows, dim = unit0.shape

    def kernel(unit_ref, own_ref, near_ref, far_ref, small_ref, unit1_ref, inverse_ref, out_ref, low_ref):
        hidden = unit_ref[...] * small_ref[4:5, :] + small_ref[6:7, :]
        unit, inverse = unit_of(hidden + scattered(own_ref, near_ref, far_ref) + small_ref[3:4, :])
        out = unit * small_ref[5:6, :] + small_ref[7:8, :]
        unit1_ref[...] = unit
        inverse_ref[...] = inverse
        out_ref[...] = out
        low_ref[...] = out.astype(BF)

    outs = [((rows, dim), F32), ((rows, 1), F32), ((rows, dim), F32), ((rows, dim), BF)]
    return chain(kernel, outs, [unit0, *parts, w.small], after=after)


def norm_second_back(chain, residual, parts, unit1, inverse, w, after=()):
    rows, dim = residual.shape

    def kernel(res_ref, own_ref, near_ref, far_ref, unit_ref, inverse_ref, small_ref, sum_ref, low_ref, tiny_ref):
        grad = res_ref[...] + scattered(own_ref, near_ref, far_ref)
        unit = unit_ref[...]
        back = unit_back(grad, unit, inverse_ref[...], small_ref[5:6, :])
        low = back.astype(BF)
        sum_ref[...] = back
        low_ref[...] = low
        tiny_ref[...] = tiny_sums(low, grad, unit)

    outs = [((rows, dim), F32), ((rows, dim), BF), ((3, dim), F32)]
    return chain(kernel, outs, [residual, *parts, unit1, inverse, w.small], after=after)


def norm_second_both(chain, unit0, parts, cotangent, w, after=()):
    rows, dim = unit0.shape

    def kernel(unit_ref, own_ref, near_ref, far_ref, cot_ref, small_ref, out_ref, sum_ref, low_ref, tiny_ref):
        hidden = unit_ref[...] * small_ref[4:5, :] + small_ref[6:7, :]
        unit, inverse = unit_of(hidden + scattered(own_ref, near_ref, far_ref) + small_ref[3:4, :])
        out_ref[...] = unit * small_ref[5:6, :] + small_ref[7:8, :]
        grad = cot_ref[...].astype(F32)
        back = unit_back(grad, unit, inverse, small_ref[5:6, :])
        low = back.astype(BF)
        sum_ref[...] = back
        low_ref[...] = low
        tiny_ref[...] = tiny_sums(low, grad, unit)

    outs = [((rows, dim), F32), ((rows, dim), F32), ((rows, dim), BF), ((3, dim), F32)]
    return chain(kernel, outs, [unit0, *parts, cotangent, w.small], after=after)


def norm_first_back(chain, sum_grad, parts, unit0, inverse, w, after=()):
    rows, dim = sum_grad.shape

    def kernel(sum_ref, own_ref, near_ref, far_ref, unit_ref, inverse_ref, small_ref, out_ref, low_ref, tiny_ref):
        grad = sum_ref[...] + scattered(own_ref, near_ref, far_ref)
        unit = unit_ref[...]
        back = unit_back(grad, unit, inverse_ref[...], small_ref[4:5, :])
        low = back.astype(BF)
        out_ref[...] = back
        low_ref[...] = low
        tiny_ref[...] = tiny_sums(low, grad, unit)

    outs = [((rows, dim), F32), ((rows, dim), BF), ((3, dim), F32)]
    return chain(kernel, outs, [sum_grad, *parts, unit0, inverse, w.small], after=after)


def input_gradient(chain, residual, parts, after=()):
    rows, dim = residual.shape

    def kernel(res_ref, own_ref, near_ref, far_ref, out_ref):
        out_ref[...] = res_ref[...] + scattered(own_ref, near_ref, far_ref)

    return chain(kernel, [((rows, dim), F32)], [residual, *parts], after=after)[0]


def project(chain, quads, w, with_rel, after=()):
    rows, dim = quads[0].shape
    width = w.qkv.shape[1]

    def kernel(*refs):
        refs = list(refs)
        quad_refs = [refs.pop(0) for _ in range(STREAMS)]
        qkv_ref, bias_ref = refs.pop(0), refs.pop(0)
        rel_ref, rel_bias_ref = (refs.pop(0), refs.pop(0)) if with_rel else (None, None)
        joined_ref, heads_ref = refs.pop(0), refs.pop(0)
        join(joined_ref, quad_refs)
        heads_ref[...] = (dot(joined_ref[...], qkv_ref[...]) + bias_ref[...]).astype(BF)
        if with_rel:
            refs[0][...] = dot(joined_ref[...], rel_ref[...]) + rel_bias_ref[...]

    args = [*quads, w.qkv, w.qkv_bias]
    outs = [((STREAMS * rows, dim), BF), ((STREAMS * rows, width), BF)]
    if with_rel:
        args += [w.rel, w.rel_bias]
        outs.append(((STREAMS * rows, w.rel.shape[1]), F32))
    return chain(kernel, outs, args, after=after)


def out_project(chain, context, w, after=()):
    total, _ = context.shape
    block = total // STREAMS

    def kernel(context_ref, out_ref, *parts_refs):
        for part in range(2):
            value = dot(context_ref[part * 2 * block : (part + 1) * 2 * block, :], out_ref[...])
            store_partials(part, value, *parts_refs)

    return chain(kernel, scatter_outs(block, w.out.shape[1]), [context, w.out], after=after)


def project_back(chain, dq, dk, dv, drel, w, after=()):
    total, width = dq.shape
    block = total // STREAMS
    dim = w.qkv.shape[0]
    with_rel = drel is not None
    keys, vals = len(dk), len(dv)

    def kernel(*refs):
        refs = list(refs)
        dq_ref = refs.pop(0)
        dk_refs = [refs.pop(0) for _ in range(keys)]
        dv_refs = [refs.pop(0) for _ in range(vals)]
        drel_ref = refs.pop(0) if with_rel else None
        qkv_ref = refs.pop(0)
        rel_ref = refs.pop(0) if with_rel else None
        parts_refs = [refs.pop(0) for _ in range(3)]
        heads_ref, sums_ref = refs.pop(0), refs.pop(0)
        heads_ref[:, :width] = dq_ref[...]
        heads_ref[:, width : 2 * width] = sum(r[...] for r in dk_refs).astype(BF)
        heads_ref[:, 2 * width :] = sum(r[...] for r in dv_refs).astype(BF)
        sums_ref[...] = column(heads_ref[...].astype(F32))
        if with_rel:
            refs[0][...] = column(drel_ref[...].astype(F32))
        for part in range(2):
            rows = slice(part * 2 * block, (part + 1) * 2 * block)
            value = dot_nt(heads_ref[rows, :], qkv_ref[...])
            if with_rel:
                value = value + dot_nt(drel_ref[rows, :], rel_ref[...])
            store_partials(part, value, *parts_refs)

    args = [dq, *dk, *dv]
    outs = scatter_outs(block, dim) + [((total, 3 * width), BF), ((1, 3 * width), F32)]
    if with_rel:
        args += [drel, w.qkv, w.rel]
        outs.append(((1, w.rel.shape[1]), F32))
    else:
        args.append(w.qkv)
    return chain(kernel, outs, args, after=after)


def gelu_and_slope(x):
    bell = jnp.exp(-0.5 * x * x)
    under = 1.0 + (0.3275911 * 0.5**0.5) * jnp.abs(x)
    t = pl.reciprocal(under, approx=True)
    t = t * (2.0 - under * t)
    series = ((((1.061405429 * t - 1.453152027) * t + 1.421413741) * t - 0.284496736) * t + 0.254829592) * t
    tail = (0.5 * series) * bell
    below = jnp.where(x >= 0.0, 1.0 - tail, tail)
    return x * below, below + x * bell * 0.3989422804014327


FFN_TILE = 256


def ffn_in_tile(ref, share, first):
    tile = ref[:, :share, first : first + FFN_TILE]
    return tile.reshape(tile.shape[0] * share, FFN_TILE)


def ffn_out_rows(ref, share, first, last):
    part = ref.shape[1] - share
    tile = ref[first // part : last // part, share:, :]
    return tile.reshape(last - first, ref.shape[2])


def ffn_forward(chain, quads, w, after=()):
    rows, dim = quads[0].shape
    n, both, units = w.ffn.shape
    share = dim // n
    half = 2 * rows

    def kernel(a_ref, b_ref, c_ref, d_ref, w_ref, bias_ref, own_ref, across_ref, near_ref, joined_ref, act_ref, slope_ref):
        join(joined_ref, (a_ref, b_ref, c_ref, d_ref))
        for part in range(2):
            block = slice(part * half, (part + 1) * half)
            for u in range(0, units, FFN_TILE):
                tile = slice(u, u + FFN_TILE)
                inner = dot(joined_ref[block, :], ffn_in_tile(w_ref, share, u)) + bias_ref[:, tile]
                active, slope = gelu_and_slope(inner)
                act_ref[block, tile] = active.astype(BF)
                slope_ref[block, tile] = slope.astype(BF)
            branch = dot(act_ref[block, :], ffn_out_rows(w_ref, share, 0, units))
            store_partials(part, branch, own_ref, across_ref, near_ref)

    wide = ((4 * rows, units), BF)
    outs = scatter_outs(rows, dim) + [((4 * rows, dim), BF), wide, wide]
    return chain(kernel, outs, [*quads, w.ffn, w.ffn_bias], after=after, cost=5)


def ffn_backward(chain, quads, slope, w, after=()):
    rows, dim = quads[0].shape
    n, both, units = w.ffn.shape
    share = dim // n
    half = 2 * rows

    def kernel(a_ref, b_ref, c_ref, d_ref, w_ref, slope_ref, own_ref, across_ref, near_ref, joined_ref, inner_ref, sums_ref):
        join(joined_ref, (a_ref, b_ref, c_ref, d_ref))
        for part in range(2):
            block = slice(part * half, (part + 1) * half)
            for u in range(0, units, FFN_TILE):
                tile = slice(u, u + FFN_TILE)
                back = dot_nt(joined_ref[block, :], ffn_out_rows(w_ref, share, u, u + FFN_TILE))
                inner = (back * slope_ref[block, tile].astype(F32)).astype(BF)
                inner_ref[block, tile] = inner
                if part == 0:
                    sums_ref[:, tile] = column(inner.astype(F32))
                else:
                    sums_ref[:, tile] += column(inner.astype(F32))
            hidden = sum(
                dot_nt(inner_ref[block, u : u + FFN_TILE], ffn_in_tile(w_ref, share, u))
                for u in range(0, units, FFN_TILE)
            )
            store_partials(part, hidden, own_ref, across_ref, near_ref)

    outs = scatter_outs(rows, dim) + [((4 * rows, dim), BF), ((4 * rows, units), BF), ((1, units), F32)]
    return chain(kernel, outs, [*quads, w.ffn, slope], after=after, cost=4)


def copy_all(moves, sems):
    copies = [pltpu.make_async_copy(source, target, sems.at[i]) for i, (source, target) in enumerate(moves)]
    for copy in copies:
        copy.start()
    for copy in copies:
        copy.wait()


def pack_attention(chain, devices, qkv, out, smalls=None, rel=None, after=()):
    share, dim = out.shape
    quarter = dim // STREAMS
    fixed = 4 * share
    half = share // 2
    more = 16 if rel is None else half
    extra = list(smalls) if rel is None else [rel]

    def kernel(devices_ref, qkv_ref, out_ref, *refs):
        sources, packed_ref, targets, sems = refs[: len(extra)], refs[len(extra)], refs[len(extra) + 1 : -1], refs[-1]
        columns = pl.ds(pl.multiple_of(devices_ref[0] * quarter, quarter), quarter)
        moves = [(qkv_ref.at[i, :, columns], packed_ref.at[i * share : (i + 1) * share, :]) for i in range(3)]
        moves.append((out_ref.at[:, columns], packed_ref.at[3 * share : fixed, :]))
        if rel is None:
            moves += list(zip(sources, targets))
        else:
            part = rel.shape[1] // STREAMS
            columns = pl.ds(pl.multiple_of(devices_ref[0] * part, part), part)
            for i in range(2):
                moves.append(
                    (
                        sources[0].at[i * half : (i + 1) * half, columns],
                        packed_ref.at[fixed:, i * part : (i + 1) * part],
                    )
                )
        copy_all(moves, sems)
        if rel is None:
            lines = []
            ffn_share = STREAMS * share
            last = targets[0][:, 2 * ffn_share :].astype(F32)
            last = jnp.concatenate([last, jnp.zeros((1, share - last.shape[1]), F32)], axis=1)
            for layer in range(2):
                bias_ref, gain_ref, shift_ref = targets[3 * layer + 1 : 3 * layer + 4]
                left = jnp.concatenate([r[...].astype(F32) for r in (bias_ref, gain_ref, shift_ref)], axis=0)
                first = layer * ffn_share
                right = [
                    targets[0][:, first + i * share : first + (i + 1) * share].astype(F32) for i in range(STREAMS)
                ]
                right += [last, jnp.zeros((3, share), F32)]
                lines.append(jnp.concatenate([left, jnp.concatenate(right, axis=0)], axis=1))
            lines = jnp.concatenate(lines, axis=0)
            packed_ref[fixed:, : 2 * share] = lines.astype(BF)
            if 2 * share < quarter:
                packed_ref[fixed:, 2 * share :] = jnp.zeros((more, quarter - 2 * share), BF)

    scratch = [pltpu.VMEM(a.shape, BF) for a in extra] if rel is None else []
    scratch.append(pltpu.SemaphoreType.DMA((4 + (len(extra) if rel is None else 2),)))
    outs = [((fixed + more, quarter), BF)]
    return chain(kernel, outs, [], scalars=[devices], stored=[qkv, out] + extra, scratch=scratch, after=after)[0]


def pack_ffn(chain, devices, here, matrix_in, matrix_out, n, after=()):
    share, ffn = matrix_in.shape
    ffn_share, dim = matrix_out.shape
    part = ffn_share // STREAMS
    if part % TILE:
        blocks = lax.dynamic_slice_in_dim(matrix_in.reshape(share, n, ffn_share), here * part, part, axis=2)
        rows = lax.dynamic_slice_in_dim(matrix_out, here * part, part, axis=0)
        return jnp.concatenate([blocks.reshape(share, n * part), rows], axis=0)

    def kernel(devices_ref, in_ref, out_ref, packed_ref, sems):
        first = devices_ref[0] * part
        moves = [(out_ref.at[pl.ds(pl.multiple_of(first, TILE), part), :], packed_ref.at[share:, :])]
        for g in range(n):
            columns = pl.ds(pl.multiple_of(g * ffn_share + first, TILE), part)
            moves.append((in_ref.at[:, columns], packed_ref.at[:share, g * part : (g + 1) * part]))
        copy_all(moves, sems)

    return chain(
        kernel,
        [((share + part, n * part), BF)],
        [],
        scalars=[devices],
        stored=[matrix_in, matrix_out],
        scratch=[pltpu.SemaphoreType.DMA((n + 1,))],
        after=after,
    )[0]


def place_ffn(chain, devices, here, blocks, share, n, after=()):
    rows, dim = blocks[0].shape
    part = rows - share
    ffn = n * part * STREAMS
    if part % TILE:
        stacked = jnp.stack([blocks[XOR.index(j)] for j in range(STREAMS)])
        ordered = [lax.dynamic_index_in_dim(stacked, here ^ a, 0, keepdims=False) for a in range(STREAMS)]
        grad_in = jnp.stack([b[:share].reshape(share, n, part) for b in ordered], axis=2)
        grad_out = jnp.concatenate([b[share:] for b in ordered], axis=0)
        return grad_in.reshape(share, ffn).astype(F32), grad_out.astype(F32)

    def kernel(devices_ref, *refs):
        in_ref, out_ref = refs[STREAMS:]
        for i in range(STREAMS):
            first = devices_ref[i] * part
            for g in range(n):
                columns = pl.ds(pl.multiple_of(g * part * STREAMS + first, TILE), part)
                in_ref[:, columns] = refs[i][:share, g * part : (g + 1) * part].astype(F32)
            out_ref[pl.ds(pl.multiple_of(first, TILE), part), :] = refs[i][share:, :].astype(F32)

    outs = [((share, ffn), F32), ((STREAMS * part, dim), F32)]
    return chain(kernel, outs, blocks, scalars=[devices], after=after, room=6)


def place_attention(chain, devices, blocks, share, ffn_part, rel_part, after=()):
    quarter = blocks[0].shape[1]
    dim = quarter * STREAMS
    fixed = 4 * share
    half = share // 2
    tiny = fixed + (half if rel_part else 0)
    tiny_rows = blocks[0].shape[0] - tiny

    def kernel(devices_ref, *refs):
        refs = list(refs)
        block_refs = [refs.pop(0) for _ in range(STREAMS)]
        qkv_ref, out_ref, tiny_ref, inner_ref = refs[:4]
        total = jnp.zeros((tiny_rows, quarter), F32)
        for i, ref in enumerate(block_refs):
            columns = pl.ds(pl.multiple_of(devices_ref[i] * quarter, quarter), quarter)
            for k in range(3):
                qkv_ref[k, :, columns] = ref[k * share : (k + 1) * share, :].astype(F32)
            out_ref[:, columns] = ref[3 * share : fixed, :].astype(F32)
            if rel_part:
                columns = pl.ds(pl.multiple_of(devices_ref[i] * rel_part, rel_part), rel_part)
                refs[4][:half, columns] = ref[fixed : fixed + half, :rel_part].astype(F32)
                refs[4][half:, columns] = ref[fixed : fixed + half, rel_part:].astype(F32)
            mine = ref[tiny:, :].astype(F32)
            total = total + mine
            inner_ref[pl.ds(devices_ref[i], 1), :] = mine[0:1, share : share + ffn_part]
        tiny_ref[...] = total

    outs = [
        ((3, share, dim), F32),
        ((share, dim), F32),
        ((tiny_rows, quarter), F32),
        ((STREAMS, ffn_part), F32),
    ]
    if rel_part:
        outs.append(((share, rel_part * STREAMS), F32))
    return chain(kernel, outs, blocks, scalars=[devices], after=after, room=6)


class Layer:
    pass


def own_columns(matrix, here):
    width = matrix.shape[-1] // STREAMS
    return lax.dynamic_slice_in_dim(matrix, here * width, width, axis=matrix.ndim - 1)


def per_device(
    enc_input, pred_input, cotangent, bucket_len, pad_len, rel_table,
    enc_qkv, enc_out, enc_ffn_in, enc_ffn_out, enc_ffn_bias, enc_bias, enc_gain, enc_shift,
    dec_qkv, dec_out, dec_rel, dec_rel_bias, dec_ffn_in, dec_ffn_out, dec_ffn_bias, dec_bias, dec_gain, dec_shift,
):
    chain = Chain()
    here = lax.axis_index("stream")
    n = lax.axis_size("dp")
    group = lax.axis_index("dp")
    place = ring_place(group, n)
    rows = enc_input.shape[0]
    total = STREAMS * rows
    dim = enc_input.shape[1]
    share = enc_out.shape[0]
    quarter = dim // STREAMS
    ffn_share = enc_ffn_out.shape[0]
    ffn_part = ffn_share // STREAMS
    rel_all = dec_rel.shape[1]
    rel_part = rel_all // STREAMS
    fixed = 4 * share
    half = share // 2

    bucket = bucket_len[0]
    starts = []
    for j in XOR:
        holder = here ^ j
        for chunk in range(2):
            starts.append(jnp.where(bucket == total, holder * rows + chunk * 64, chunk * bucket + holder * 64))
    meta = jnp.stack([v.astype(jnp.int32) for v in starts + [bucket, pad_len[0, 0], pad_len[0, 1]]])
    devices = jnp.stack([here ^ j for j in XOR]).astype(jnp.int32)
    ring_index = jnp.stack([ring_member(place - o, n) for o in range(n)]).astype(jnp.int32)
    tables = rel_tables(rel_table, total)

    vectors = jnp.concatenate([enc_ffn_bias, dec_ffn_bias, dec_rel_bias])[None]
    smalls = (vectors, enc_bias, enc_gain, enc_shift, dec_bias, dec_gain, dec_shift)
    small_rows = 16

    def attention_regions(extra):
        regions = [(i * share, (i + 1) * share, 0, quarter, 0, 0, i * quarter) for i in range(3)]
        regions.append((fixed - share, fixed, 0, quarter, 1, 0, 0))
        return regions + extra

    shapes = [(share, 3 * quarter), (share, quarter)]

    def gather_shares(packed):
        return lax.all_gather(packed, "dp", axis=0, tiled=False)

    enc_ffn = gather_shares(pack_ffn(chain, devices, here, enc_ffn_in, enc_ffn_out, n))
    enc_pieces = ring_pieces(pack_attention(chain, devices, enc_qkv, enc_out, smalls=smalls), n)
    enc_quads = gather_rows(enc_input)
    pred_quads = [gather_rows(pred_input[i]) for i in range(2)]
    dec_packed = gather_shares(pack_attention(chain, devices, dec_qkv, dec_out, rel=dec_rel))
    dec_ffn = gather_shares(pack_ffn(chain, devices, here, dec_ffn_in, dec_ffn_out, n))

    def turn_out_back(grad):
        sent = [lax.dynamic_slice_in_dim(grad, (here ^ j) * quarter, quarter, axis=1) for j in XOR]
        return jnp.concatenate(by_absolute(turn_blocks(sent), here), axis=0).reshape(n, share, quarter)

    enc_wqkv, enc_wout, small_all = assemble(
        chain,
        enc_pieces,
        ring_index,
        attention_regions([(fixed, fixed + small_rows, 0, quarter, 2, 0, 0)]),
        shapes + [(small_rows, quarter)],
        n,
        after=[quads[1] for quads in pred_quads],
    )

    small_all = small_all.astype(F32)

    def attention_layer(number, wqkv, wout):
        w = Layer()
        w.qkv = wqkv.reshape(dim, 3 * quarter)
        w.turn = Turn(chain, devices, wout.reshape(dim, quarter), True)
        block = small_all[:, 8 * number : 8 * number + 8]
        w.ffn_bias = lax.dynamic_slice_in_dim(block, here, 1, axis=1)[:, 0, share : 2 * share].reshape(1, -1)
        w.small = jnp.transpose(block[:, :, :share], (1, 0, 2)).reshape(8, dim)
        mine = own_columns(w.small, here)
        w.qkv_bias = jnp.concatenate([mine[0:1], jnp.zeros_like(mine[0:1]), mine[1:2]], axis=1)
        return w

    enc = attention_layer(0, enc_wqkv, enc_wout)
    enc_all, enc_heads = project(chain, enc_quads, enc, False)
    enc_context, enc_lse, _ = attention_forward(chain, meta, enc_heads)
    enc.out = enc.turn.join(chain)
    scatter = Scatter(out_project(chain, enc_context, enc))
    scatter.middle(chain)
    enc_unit0, enc_inverse0, low = norm_first(chain, enc_input, scatter.parts(), enc)
    quads = gather_rows(low)
    enc.ffn = enc_ffn
    *parts, enc_hidden, enc_active, enc_slope = ffn_forward(chain, quads, enc)
    scatter = Scatter(parts)
    scatter.middle(chain)
    enc_unit1, enc_inverse1, main_rows, main_low = norm_second(chain, enc_unit0, scatter.parts(), enc)
    main_quads = gather_rows(main_low)

    dec_wqkv, dec_wout, dec_wrel = unpack(
        chain,
        dec_packed,
        attention_regions(
            [
                (fixed, fixed + half, 0, rel_part, 2, 0, 0),
                (fixed, fixed + half, rel_part, 2 * rel_part, 2, half, 0),
            ]
        ),
        shapes + [(share, rel_part)],
    )
    dec = attention_layer(1, dec_wqkv, dec_wout)
    dec.rel = dec_wrel.reshape(dim, rel_part)
    dec.rel_bias = own_columns(small_all[:, 12, share : share + rel_all // n].reshape(1, -1), here)
    alls, heads, rels = [None] * 3, [None] * 3, [None] * 3
    stream_inputs = (main_rows, pred_input[0], pred_input[1])
    for i, quads in ((0, main_quads), (1, pred_quads[0]), (2, pred_quads[1])):
        alls[i], heads[i], rels[i] = project(chain, quads, dec, True)
    contexts, lses = [None] * 3, [None] * 3

    def attend(i, after=()):
        contexts[i], lses[i], parts = attention_forward(
            chain, meta, heads[i], heads[0] if i else None, rels[i], tables, dec.out if i else None, after
        )
        if i == 0:
            dec.out = dec.turn.join(chain)
            parts = out_project(chain, contexts[i], dec)
        return Scatter(parts)

    def staged(work, finish):
        scatters = []
        for i in range(3):
            scatters.append(work(i))
            if i:
                scatters[i - 1].middle(chain)
        results = [finish(0, scatters[0])]
        scatters[2].middle(chain)
        results += [finish(1, scatters[1]), finish(2, scatters[2])]
        return results

    firsts = staged(
        lambda i: attend(i),
        lambda i, scatter: norm_first(chain, stream_inputs[i], scatter.parts(), dec),
    )
    hidden_quads = [gather_rows(first[2]) for first in firsts]
    dec.ffn = dec_ffn
    kept = [None] * 3

    def feed(i):
        *parts, hidden, active, slope = ffn_forward(chain, hidden_quads[i], dec)
        kept[i] = (hidden, active, slope)
        return Scatter(parts)

    seconds = staged(
        feed, lambda i, scatter: norm_second_both(chain, firsts[i][0], scatter.parts(), cotangent[i], dec)
    )
    outputs = [second[0] for second in seconds]

    branch_quads = [gather_rows(second[2]) for second in seconds]
    branches = [None] * 3

    def feed_back(i):
        *parts, branch, inner, inner_sum = ffn_backward(chain, branch_quads[i], kept[i][2], dec)
        branches[i] = (branch, inner, inner_sum)
        return Scatter(parts)

    backs = staged(
        feed_back,
        lambda i, scatter: norm_first_back(
            chain, seconds[i][1], scatter.parts(), firsts[i][0], firsts[i][1], dec
        ),
    )
    attended_quads = [gather_rows(back[1]) for back in backs]

    def ffn_grads(pairs):
        grad_in = sum(dot_tn(hidden, inner) for hidden, _, inner, _ in pairs).astype(BF)
        grad_out = sum(dot_tn(active, branch) for _, active, _, branch in pairs).astype(BF)
        return grad_in.reshape(n, share, dim), grad_out.reshape(n, ffn_part, dim)

    def ffn_sum(pairs):
        regions = [(0, 0, 0, share), (1, 0, share, ffn_part)]
        return RingSum(chain, list(ffn_grads(pairs)), regions, dim, n, ring_index)

    def advance(ring, stage):
        result = None
        while ring.done < stage * (n // 2 + 1) // 5:
            result = ring.step()
            ring.done += 1
        return result

    dec_ffn_total = lax.psum_scatter(
        jnp.concatenate(
            ffn_grads([(kept[i][0], kept[i][1], branches[i][1], branches[i][0]) for i in range(3)]), axis=1
        ),
        "dp",
        scatter_dimension=0,
        tiled=False,
    )
    results = [None] * 3
    for i in (1, 2, 0):
        results[i] = attention_backward(
            chain, meta, heads[i], attended_quads[i], dec.out, lses[i], None if i == 0 else heads[0], rels[i], tables
        )
    dheads, head_sums, rel_sums = [None] * 3, [None] * 3, [None] * 3

    def back_project(i):
        dq, dk, dv, _, drel = results[i][:5]
        keys = [r[1] for r in results] if i == 0 else [results[i][5]]
        vals = [r[2] for r in results] if i == 0 else [results[i][6]]
        *parts, dheads[i], head_sums[i], rel_sums[i] = project_back(chain, dq, keys, vals, drel, dec)
        return Scatter(parts)

    main_scatter = back_project(0)
    pred_scatters = [back_project(1)]
    main_scatter.middle(chain)
    pred_scatters.append(back_project(2))
    pred_scatters[0].middle(chain)

    def widen(part, size):
        return lax.dynamic_update_slice(jnp.zeros((1, size), F32), part, (0, here * part.shape[1]))

    def small_pack(inner_sum, tiny0, tiny1, heads_sum, rel_sum=None):
        wide = jnp.concatenate(
            [
                widen(heads_sum[:, :quarter], dim),
                widen(heads_sum[:, 2 * quarter :], dim),
                tiny0[0:1],
                tiny1[0:1],
                tiny0[1:2],
                tiny1[1:2],
                tiny0[2:3],
                tiny1[2:3],
            ],
            axis=0,
        )
        left = jnp.transpose(wide.reshape(8, n, share), (1, 0, 2))
        spare = quarter - share
        lines = [jnp.pad(inner_sum.reshape(n, 1, ffn_part), ((0, 0), (0, 0), (0, spare - ffn_part)))]
        if rel_sum is not None:
            line = widen(rel_sum, rel_all).reshape(n, 1, rel_all // n)
            lines.append(jnp.pad(line, ((0, 0), (0, 0), (0, spare - rel_all // n))))
        lines.append(jnp.zeros((n, 8 - len(lines), spare), F32))
        packed = jnp.concatenate([left, jnp.concatenate(lines, axis=1)], axis=2)
        return jnp.pad(packed, ((0, 0), (0, 8), (0, 0))).astype(BF)

    def attention_grads(qkv_grad, out_grad, more):
        return [qkv_grad.astype(BF).reshape(n, share, 3 * quarter), turn_out_back(out_grad.astype(BF))] + more

    def attention_ring(*grads):
        arrays = attention_grads(*grads)
        regions = [(0, i * quarter, i * share, share) for i in range(3)] + [(1, 0, 3 * share, share)]
        at = fixed
        for which, array in enumerate(arrays[2:]):
            regions.append((2 + which, 0, at, array.shape[1]))
            at += array.shape[1]
        return RingSum(chain, arrays, regions, quarter, n, ring_index)

    dec_out_part = sum(dot_tn(contexts[i], results[i][3]) for i in range(3))
    dec_qkv_part = sum(dot_tn(alls[i], dheads[i]) for i in range(3))
    rel_blocks = sum(dot_tn(alls[i], results[i][4]) for i in range(3)).astype(BF).reshape(n, share, rel_part)
    dec_small = small_pack(
        sum(branches[i][2] for i in range(3)),
        sum(backs[i][2] for i in range(3)),
        sum(seconds[i][3] for i in range(3)),
        sum(head_sums),
        sum(rel_sums),
    )
    wide, *others = attention_grads(
        dec_qkv_part,
        dec_out_part,
        [jnp.concatenate([rel_blocks[:, :half], rel_blocks[:, half:]], axis=2), dec_small],
    )
    thirds = [wide[:, :, i * quarter : (i + 1) * quarter] for i in range(3)]
    dec_total = lax.psum_scatter(
        jnp.concatenate(thirds + others, axis=1), "dp", scatter_dimension=0, tiled=False
    )

    enc_sum_grad, low, enc_tiny1 = norm_second_back(
        chain, backs[0][0], main_scatter.parts(), enc_unit1, enc_inverse1, enc
    )
    quads = gather_rows(low)
    pred_scatters[1].middle(chain)
    *parts, enc_branch, enc_inner, enc_inner_sum = ffn_backward(chain, quads, enc_slope, enc)
    scatter = Scatter(parts)
    pred_grads = [input_gradient(chain, backs[1][0], pred_scatters[0].parts())]
    scatter.middle(chain)
    enc_ffn_ring = ffn_sum([(enc_hidden, enc_active, enc_inner, enc_branch)])
    advance(enc_ffn_ring, 1)
    pred_grads.append(input_gradient(chain, backs[2][0], pred_scatters[1].parts()))
    residual, attended_low, enc_tiny0 = norm_first_back(
        chain, enc_sum_grad, scatter.parts(), enc_unit0, enc_inverse0, enc
    )
    quads = gather_rows(attended_low)
    dec_ffn_blocks = gather_rows(dec_ffn_total)
    advance(enc_ffn_ring, 2)
    enc_out_part = dot_tn(enc_context, jnp.concatenate(quads, axis=0))
    dq, dk, dv, _ = attention_backward(chain, meta, enc_heads, quads, enc.out, enc_lse)
    *parts, enc_dheads, enc_head_sum = project_back(chain, dq, [dk], [dv], None, enc)
    scatter = Scatter(parts)
    enc_ring = attention_ring(
        dot_tn(enc_all, enc_dheads),
        enc_out_part,
        [small_pack(enc_inner_sum, enc_tiny0, enc_tiny1, enc_head_sum)],
    )
    advance(enc_ring, 1)
    scatter.middle(chain)
    advance(enc_ffn_ring, 3)
    advance(enc_ring, 2)
    dec_in_grad, dec_back_grad = place_ffn(chain, devices, here, dec_ffn_blocks, share, n)
    enc_input_grad = input_gradient(chain, residual, scatter.parts())
    advance(enc_ffn_ring, 4)
    advance(enc_ring, 3)
    dec_blocks = gather_rows(dec_total)
    enc_ffn_blocks = gather_rows(advance(enc_ffn_ring, 5))
    advance(enc_ring, 4)
    dec_results = place_attention(chain, devices, dec_blocks, share, ffn_part, rel_part)
    enc_blocks = gather_rows(advance(enc_ring, 5))
    enc_in_grad, enc_back_grad = place_ffn(chain, devices, here, enc_ffn_blocks, share, n)
    enc_results = place_attention(chain, devices, enc_blocks, share, ffn_part, 0)

    def tiny_out(results):
        tiny, inner = results[2], results[3]
        return inner.reshape(-1), tiny[0:4, :share], tiny[4:6, :share], tiny[6:8, :share]

    return (
        jnp.stack(outputs),
        enc_input_grad,
        jnp.stack(pred_grads),
        enc_results[0],
        enc_results[1],
        enc_in_grad,
        enc_back_grad,
        *tiny_out(enc_results),
        dec_results[0],
        dec_results[1],
        dec_results[4],
        dec_results[2][1, share : share + rel_all // n],
        dec_in_grad,
        dec_back_grad,
        *tiny_out(dec_results),
    )


def solution(mesh):
    tokens = P(("stream", "dp"), None)
    streams = P(None, ("stream", "dp"), None)
    first, second, cube = P("dp", None), P(None, "dp"), P(None, "dp", None)
    flat = P("dp")
    return jax.shard_map(
        per_device,
        mesh=mesh,
        in_specs=(
            tokens, streams, streams, flat, first, P(),
            cube, first, first, first, flat, second, second, second,
            cube, first, first, flat, first, first, flat, second, second, second,
        ),
        out_specs=(
            streams, tokens, streams,
            cube, first, first, first, flat, second, second, second,
            cube, first, first, flat, first, first, flat, second, second, second,
        ),
        check_vma=False,
    )
```

```python
from functools import partial

import jax
import jax.numpy as jnp
from jax import lax
from jax.experimental import pallas as pl
from jax.experimental.pallas import tpu as pltpu
from jax.sharding import PartitionSpec as P

H = 16
NB = 32
HD = 64
EPSILON = 1e-05
MASKED = -1000000000.0
BF = jnp.bfloat16
F32 = jnp.float32
TILE = 128
STREAMS = 4
XOR = (0, 2, 1, 3)
MIB = 1024 * 1024


def dot(a, b):
    return jnp.dot(a, b, preferred_element_type=F32)


def dot_nt(a, b):
    return lax.dot_general(a, b, (((1,), (1,)), ((), ())), preferred_element_type=F32)


def dot_tn(a, b):
    return lax.dot_general(a, b, (((0,), (0,)), ((), ())), preferred_element_type=F32)


def swap(values, bit):
    return lax.ppermute(values, "stream", [(i, i ^ bit) for i in range(STREAMS)])


class Chain:
    def __init__(self):
        self.last = None

    def __call__(self, kernel, outs, args, scalars=(), away=(), stored=(), scratch=(), after=(), room=3, cost=1):
        ties = list(after)
        if self.last is not None:
            ties.append(self.last)
        reads = len(scalars) + len(args) + len(away) + len(stored)

        def body(*refs):
            kernel(*refs[:reads], *refs[reads + len(ties) :])

        vmem = pl.BlockSpec(memory_space=pltpu.VMEM)
        anywhere = pl.BlockSpec(memory_space=pl.ANY)
        results = pl.pallas_call(
            body,
            out_shape=[jax.ShapeDtypeStruct(shape, kind) for shape, kind in outs],
            in_specs=[pl.BlockSpec(memory_space=pltpu.SMEM)] * len(scalars)
            + [vmem] * len(args)
            + [anywhere] * len(away)
            + [pl.BlockSpec(memory_space=pltpu.HBM)] * len(stored)
            + [anywhere] * len(ties),
            out_specs=[vmem] * len(outs),
            scratch_shapes=list(scratch),
            compiler_params=pltpu.CompilerParams(vmem_limit_bytes=room * MIB),
            cost_estimate=pl.CostEstimate(flops=10**10, bytes_accessed=10**7, transcendentals=0),
        )(*scalars, *args, *away, *[pltpu.with_memory_space_constraint(a, pltpu.HBM) for a in stored], *ties)
        self.last = results[0]
        return results


def gather_rows(rows):
    far = swap(rows, 2)
    return rows, far, swap(rows, 1), swap(far, 1)


class Scatter:
    def __init__(self, parts):
        self.own, self.across, near = parts
        self.near = swap(near, 1)

    def middle(self, chain, after=()):
        rows, dim = self.own.shape

        def kernel(across_ref, near_ref, out_ref):
            out_ref[...] = (across_ref[...] + near_ref[rows:, :].astype(F32)).astype(BF)

        (low,) = chain(kernel, [((rows, dim), BF)], [self.across, self.near], after=after, cost=0.1)
        self.far = swap(low, 2)

    def parts(self):
        return [self.own, self.near, self.far]


def scattered(own_ref, near_ref, far_ref):
    rows = own_ref.shape[0]
    return own_ref[...] + near_ref[:rows, :].astype(F32) + far_ref[...].astype(F32)


def scatter_outs(rows, dim):
    return [((rows, dim), F32), ((rows, dim), F32), ((2 * rows, dim), BF)]


def store_partials(part, value, own_ref, across_ref, near_ref):
    rows = own_ref.shape[0]
    if part == 0:
        own_ref[...] = value[:rows, :]
        across_ref[...] = value[rows:, :]
    else:
        near_ref[...] = value.astype(BF)


def join(target, refs):
    rows = refs[0].shape[0]
    for i, ref in enumerate(refs):
        target[i * rows : (i + 1) * rows, :] = ref[...]


def turn_blocks(blocks):
    far = swap(jnp.stack([blocks[1], blocks[3]]), 2)
    near = swap(jnp.stack([blocks[2], far[1]]), 1)
    return [blocks[0], far[0], near[0], near[1]]


def by_absolute(blocks, here):
    stacked = jnp.stack([blocks[XOR.index(j)] for j in range(4)])
    return [lax.dynamic_index_in_dim(stacked, here ^ a, 0, keepdims=False) for a in range(4)]


class Turn:
    def __init__(self, chain, devices, array, by_rows):
        self.devices, self.by_rows = devices, by_rows
        size = array.shape[0 if by_rows else 1] // STREAMS
        self.size = size

        def kernel(devices_ref, array_ref, *part_refs):
            for i in range(STREAMS):
                place = pl.ds(pl.multiple_of(devices_ref[i] * size, size), size)
                part_refs[i][...] = (array_ref[place, :] if by_rows else array_ref[:, place]).astype(BF)

        own, *others = chain(kernel, [((size, size), BF)] * STREAMS, [array], scalars=[devices])
        self.parts = [own] + [swap(part, bit) for part, bit in zip(others, XOR[1:])]

    def join(self, chain, after=()):
        size, by_rows = self.size, self.by_rows

        def kernel(devices_ref, *refs):
            for i in range(STREAMS):
                place = pl.ds(pl.multiple_of(devices_ref[i] * size, size), size)
                if by_rows:
                    refs[-1][:, place] = refs[i][...]
                else:
                    refs[-1][place, :] = refs[i][...]

        shape = (size, STREAMS * size) if by_rows else (STREAMS * size, size)
        return chain(kernel, [(shape, BF)], self.parts, scalars=[self.devices], after=after)[0]


def ring_order(n):
    return list(range(0, n, 2)) + list(range(n - 1, 0, -2))


def ring_member(place, n):
    place = lax.rem(place + 2 * n, n)
    return jnp.where(place < n // 2, 2 * place, 2 * (n - place) - 1)


def ring_place(g, n):
    return jnp.where(g % 2 == 0, g // 2, n - (g + 1) // 2)


def ring_step(values, n, step):
    order = ring_order(n)
    pairs = [(order[i], order[(i + step) % n]) for i in range(n)]
    return lax.ppermute(values, "dp", pairs)


def ring_pieces(own, n):
    rows = own.shape[0]
    pieces = [(0, 0, own)]
    ahead = back = own
    for k in range(1, n // 2):
        ahead = ring_step(ahead, n, 1)
        back = ring_step(back, n, -1)
        pieces += [(k, 0, ahead), (n - k, 0, back)]
    half = halved(rows)
    top = ring_step(ahead[:half], n, 1)
    bottom = ring_step(back[half:], n, -1)
    pieces += [(n // 2, 0, top), (n // 2, half, bottom)]
    return pieces


def halved(rows):
    return rows // 32 * 16


def assemble(chain, pieces, index, regions, shapes, n, after=()):
    moves = []
    for number, (behind, first, piece) in enumerate(pieces):
        last = first + piece.shape[0]
        for r0, r1, c0, c1, which, to_row, to_col in regions:
            lo, hi = max(r0, first), min(r1, last)
            if lo < hi:
                moves.append((number, behind, lo - first, hi - first, c0, c1, which, to_row + lo - r0, to_col))

    def kernel(index_ref, *refs):
        sources = refs[: len(pieces)]
        outs = refs[len(pieces) : -1]
        copy_all(
            [
                (
                    sources[number].at[lo:hi, c0:c1],
                    outs[which].at[index_ref[behind], row : row + hi - lo, col : col + c1 - c0],
                )
                for number, behind, lo, hi, c0, c1, which, row, col in moves
            ],
            refs[-1],
        )

    return chain(
        kernel,
        [((n,) + shape, BF) for shape in shapes],
        [],
        scalars=[index],
        away=[piece for _, _, piece in pieces],
        scratch=[pltpu.SemaphoreType.DMA((len(moves),))],
        after=after,
    )


def unpack(chain, packed, regions, shapes, after=()):
    n = packed.shape[0]

    def kernel(packed_ref, *refs):
        copy_all(
            [
                (
                    packed_ref.at[:, r0:r1, c0:c1],
                    refs[which].at[:, row : row + r1 - r0, col : col + c1 - c0],
                )
                for r0, r1, c0, c1, which, row, col in regions
            ],
            refs[-1],
        )

    return chain(
        kernel,
        [((n,) + shape, BF) for shape in shapes],
        [],
        away=[packed],
        scratch=[pltpu.SemaphoreType.DMA((len(regions),))],
        after=after,
    )


class RingSum:
    def __init__(self, chain, arrays, regions, columns, n, index):
        self.chain, self.arrays, self.regions, self.n, self.index = chain, arrays, regions, n, index
        self.columns = columns
        self.rows = sum(r[3] for r in regions)
        self.half = halved(self.rows)
        self.up = self.down = None
        self.done = 0
        self.left = n // 2

    def fetch(self, index_ref, offsets, refs, buffers, sems):
        copies = []
        for slot, offset in enumerate(offsets):
            g = index_ref[offset]
            for i, (which, column, row, rows) in enumerate(self.regions):
                copies.append(
                    pltpu.make_async_copy(
                        refs[which].at[g, :, column : column + self.columns],
                        buffers.at[slot, row : row + rows, :],
                        sems.at[slot * len(self.regions) + i],
                    )
                )
                copies[-1].start()
        for copy in copies:
            copy.wait()

    def step(self, after=()):
        rows, half, columns, count = self.rows, self.half, self.columns, len(self.arrays)
        first = self.left == self.n // 2
        last = self.left == 0
        joined = self.left == self.n // 2 - 1
        offsets = [(self.n - self.left) % self.n] + ([] if first or last else [self.left])
        received = [] if first else [self.up, self.down]

        def kernel(index_ref, *refs):
            ups = refs[: len(received)]
            arrays = refs[len(received) : len(received) + count]
            outs = refs[len(received) + count : -2]
            buffers, sems = refs[-2:]
            self.fetch(index_ref, offsets, arrays, buffers, sems)
            if first:
                outs[0][...] = buffers[0, :half, :]
                outs[1][...] = buffers[0, half:, :]
            elif last:
                outs[0][...] = (
                    buffers[0].astype(F32) + ups[0][...].astype(F32) + ups[1][...].astype(F32)
                ).astype(BF)
            elif joined:
                outs[0][:half, :] = (buffers[0, :half, :].astype(F32) + ups[0][...].astype(F32)).astype(BF)
                outs[0][half:, :] = buffers[0, half:, :]
                outs[1][:half, :] = buffers[1, :half, :]
                outs[1][half:, :] = (buffers[1, half:, :].astype(F32) + ups[1][...].astype(F32)).astype(BF)
            else:
                outs[0][...] = (buffers[0].astype(F32) + ups[0][...].astype(F32)).astype(BF)
                outs[1][...] = (buffers[1].astype(F32) + ups[1][...].astype(F32)).astype(BF)

        if first:
            outs = [((half, columns), BF), ((rows - half, columns), BF)]
        else:
            outs = [((rows, columns), BF)] * (1 if last else 2)
        results = self.chain(
            kernel,
            outs,
            received,
            scalars=[self.index],
            away=self.arrays,
            scratch=[
                pltpu.VMEM((len(offsets), rows, columns), BF),
                pltpu.SemaphoreType.DMA((len(offsets) * len(self.regions),)),
            ],
            after=after,
        )
        self.left -= 1
        if last:
            return results[0]
        self.up = ring_step(results[0], self.n, 1)
        self.down = ring_step(results[1], self.n, -1)
        return None


def tile_width(t, causal, total):
    return TILE * (t + 1) if causal else total


def head_mask(e):
    lane = lax.broadcasted_iota(jnp.int32, (1, TILE), 1)
    return ((lane // HD) == e).astype(F32)


def rel_mask(h):
    lane = lax.broadcasted_iota(jnp.int32, (1, TILE), 1)
    return ((lane // NB) == h).astype(F32)


def allowed_keys(t, width, meta, causal, strict):
    bucket = meta[8]
    shape = (TILE, width)
    row = lax.broadcasted_iota(jnp.int32, shape, 0) + t * TILE
    col = lax.broadcasted_iota(jnp.int32, shape, 1)
    pos = col & (bucket - 1)
    first = col < bucket
    limit = bucket - jnp.where(first, meta[9], meta[10])
    allowed = (pos < limit) & ((row < bucket) == first)
    if causal:
        allowed = allowed & ((col < row) if strict else (col <= row))
    return allowed


def load_rows(meta, target, source, c0, c1):
    for chunk in range(8):
        start = pl.multiple_of(meta[chunk], 64)
        target[pl.ds(start, 64), :] = source[chunk * 64 : chunk * 64 + 64, c0:c1].astype(target.dtype)


def store_rows(meta, target, source, c0, c1):
    for chunk in range(8):
        start = pl.multiple_of(meta[chunk], 64)
        target[chunk * 64 : chunk * 64 + 64, c0:c1] = source[pl.ds(start, 64), :].astype(target.dtype)


def rel_bias(rel_rows, h, table):
    high = rel_rows.astype(BF)
    rest = (rel_rows - high.astype(F32)).astype(BF)
    mask = rel_mask(h)
    both = jnp.concatenate(
        [(high.astype(F32) * mask).astype(BF), (rest.astype(F32) * mask).astype(BF)], axis=1
    )
    spread = dot(both, table)
    return pltpu.roll(spread, 0, 1, stride=1, stride_axis=0)


def table_slice(t, width):
    first = sum(TILE * (u + 1) for u in range(t))
    return slice(first, first + width)


def attention_forward(chain, meta, qkv, main=None, rel=None, tables=None, w_out=None, after=()):
    total = qkv.shape[0]
    width_all = qkv.shape[1] // 3
    heads = width_all // HD
    causal = rel is not None
    own = main is not None
    project = w_out is not None
    block = total // STREAMS

    def kernel(meta_ref, *refs):
        refs = list(refs)
        qkv_ref = refs.pop(0)
        main_ref = refs.pop(0) if own else qkv_ref
        rel_ref, table_ref, hot_ref = (refs.pop(0), refs.pop(0), refs.pop(0)) if causal else (None,) * 3
        out_ref = refs.pop(0) if project else None
        ctx_ref, lse_ref = refs.pop(0), refs.pop(0)
        parts_refs = [refs.pop(0) for _ in range(3)] if project else None
        qs, ks, vs, cs, kt = refs[:5]
        refs = refs[5:]
        rs = refs.pop(0) if causal else None
        load_rows(meta_ref, qs, qkv_ref, 0, width_all)
        load_rows(meta_ref, ks, main_ref, width_all, 2 * width_all)
        load_rows(meta_ref, vs, main_ref, 2 * width_all, 3 * width_all)
        if causal:
            load_rows(meta_ref, rs, rel_ref, 0, rel.shape[1])
        if own:
            kn, vn = refs
            load_rows(meta_ref, kn, qkv_ref, width_all, 2 * width_all)
            load_rows(meta_ref, vn, qkv_ref, 2 * width_all, 3 * width_all)
        kt[...] = ks[...].T
        for t in range(total // TILE):
            rows = slice(TILE * t, TILE * (t + 1))
            width = tile_width(t, causal, total)
            allowed = allowed_keys(t, width, meta_ref, causal, own)
            lse_lane = lax.broadcasted_iota(jnp.int32, (TILE, TILE), 1)
            lse = jnp.zeros((TILE, TILE), F32)
            query = [(qs[rows, HD * h : HD * (h + 1)].astype(F32) * HD**-0.5).astype(BF) for h in range(heads)]
            scores = [dot(query[h], kt[HD * h : HD * (h + 1), 0:width]) for h in range(heads)]
            if causal:
                biases = [rel_bias(rs[rows, :], h, table_ref[:, table_slice(t, width)]) for h in range(heads)]
                scores = [a + b for a, b in zip(scores, biases)]
            scores = [jnp.where(allowed, a, MASKED) for a in scores]
            tops = [jnp.max(a, axis=1, keepdims=True) for a in scores]
            if own:
                own_scores = [
                    jnp.sum(
                        query[h].astype(F32) * kn[rows, HD * h : HD * (h + 1)].astype(F32), axis=1, keepdims=True
                    )
                    + jnp.sum(rs[rows, :] * (hot_ref[...] * rel_mask(h)), axis=1, keepdims=True)
                    for h in range(heads)
                ]
                tops = [jnp.maximum(a, b) for a, b in zip(tops, own_scores)]
            expos = [jnp.exp(a - b) for a, b in zip(scores, tops)]
            sums = [jnp.sum(a, axis=1, keepdims=True) for a in expos]
            if own:
                own_expos = [jnp.exp(a - b) for a, b in zip(own_scores, tops)]
                sums = [a + b for a, b in zip(sums, own_expos)]
            inverses = [1.0 / a for a in sums]
            parts = [
                dot((expos[h] * inverses[h]).astype(BF), vs[0:width, HD * h : HD * (h + 1)]) for h in range(heads)
            ]
            if own:
                own_probs = [own_expos[h] * inverses[h] for h in range(heads)]
                parts = [
                    parts[h] + own_probs[h] * vn[rows, HD * h : HD * (h + 1)].astype(F32) for h in range(heads)
                ]
            cs[rows, :] = jnp.concatenate(parts, axis=1).astype(BF)
            for h in range(heads):
                lse = jnp.where(lse_lane == h, tops[h] + jnp.log(sums[h]), lse)
                if own:
                    lse = jnp.where(lse_lane == heads + h, own_probs[h], lse)
            lse_ref[rows, :] = lse
        store_rows(meta_ref, ctx_ref, cs, 0, width_all)
        if project:
            for part in range(2):
                value = dot(ctx_ref[part * 2 * block : (part + 1) * 2 * block, :], out_ref[...])
                store_partials(part, value, *parts_refs)

    args = [qkv]
    scratch = [pltpu.VMEM((total, width_all), BF) for _ in range(4)] + [pltpu.VMEM((width_all, total), BF)]
    outs = [((total, width_all), BF), ((total, TILE), F32)]
    if own:
        args.append(main)
    if causal:
        args += [rel, tables[0], tables[2]]
        scratch.append(pltpu.VMEM((total, rel.shape[1]), F32))
    if own:
        scratch += [pltpu.VMEM((total, width_all), BF) for _ in range(2)]
    if project:
        args.append(w_out)
        outs += scatter_outs(block, w_out.shape[1])
    context, lse, *parts = chain(kernel, outs, args, scalars=[meta], scratch=scratch, after=after, room=8, cost=6)
    return context, lse, parts


def attention_backward(chain, meta, qkv, attended, w_out, lse, main=None, rel=None, tables=None, after=()):
    total = qkv.shape[0]
    width_all = qkv.shape[1] // 3
    heads = width_all // HD
    causal = rel is not None
    own = main is not None

    def kernel(meta_ref, *refs):
        refs = list(refs)
        qkv_ref = refs.pop(0)
        attended_refs = [refs.pop(0) for _ in range(STREAMS)]
        out_ref, lse_ref = refs.pop(0), refs.pop(0)
        main_ref = refs.pop(0) if own else qkv_ref
        rel_ref, table_ref, back_ref, hot_ref, flip_ref = (
            [refs.pop(0) for _ in range(5)] if causal else (None,) * 5
        )
        dq_ref, dk_ref, dv_ref, joined_ref = refs[:4]
        refs = refs[4:]
        drel_ref = refs.pop(0) if causal else None
        dkn_ref, dvn_ref = (refs.pop(0), refs.pop(0)) if own else (None, None)
        qs, ks, vs, gs, dqs, dks, kt, vt, qt, gt, dkt, dvt = refs[:12]
        refs = refs[12:]
        rs, drs = (refs.pop(0), refs.pop(0)) if causal else (None, None)
        join(joined_ref, attended_refs)
        dqs[...] = dot_nt(joined_ref[...], out_ref[...])
        load_rows(meta_ref, qs, qkv_ref, 0, width_all)
        load_rows(meta_ref, ks, main_ref, width_all, 2 * width_all)
        load_rows(meta_ref, vs, main_ref, 2 * width_all, 3 * width_all)
        load_rows(meta_ref, gs, dqs, 0, width_all)
        if causal:
            load_rows(meta_ref, rs, rel_ref, 0, rel.shape[1])
        if own:
            kn, vn, dkn, dvn = refs
            load_rows(meta_ref, kn, qkv_ref, width_all, 2 * width_all)
            load_rows(meta_ref, vn, qkv_ref, 2 * width_all, 3 * width_all)
        qs[...] = (qs[...].astype(F32) * HD**-0.5).astype(BF)
        kt[...] = ks[...].T
        vt[...] = vs[...].T
        qt[...] = qs[...].T
        gt[...] = gs[...].T
        dkt[...] = jnp.zeros_like(dkt)
        dvt[...] = jnp.zeros_like(dvt)
        each = range(heads)
        feat = [slice(HD * h, HD * (h + 1)) for h in each]
        for t in range(total // TILE):
            rows = slice(TILE * t, TILE * (t + 1))
            width = tile_width(t, causal, total)
            allowed = allowed_keys(t, width, meta_ref, causal, own)
            norms = [lse_ref[rows, h : h + 1] for h in each]
            query = [qs[rows, feat[h]] for h in each]
            grad = [gs[rows, feat[h]] for h in each]
            scores = [dot(query[h], kt[feat[h], 0:width]) for h in each]
            dprobs = [dot(grad[h], vt[feat[h], 0:width]) for h in each]
            if causal:
                biases = [rel_bias(rs[rows, :], h, table_ref[:, table_slice(t, width)]) for h in each]
                scores = [a + b for a, b in zip(scores, biases)]
            probs = [jnp.exp(jnp.where(allowed, scores[h], MASKED) - norms[h]) for h in each]
            rowdots = [jnp.sum(probs[h] * dprobs[h], axis=1, keepdims=True) for h in each]
            if own:
                own_probs = [lse_ref[rows, heads + h : heads + h + 1] for h in each]
                own_dprobs = [
                    jnp.sum(grad[h].astype(F32) * vn[rows, feat[h]].astype(F32), axis=1, keepdims=True) for h in each
                ]
                rowdots = [rowdots[h] + own_probs[h] * own_dprobs[h] for h in each]
                own_dscores = [
                    (own_probs[h] * (own_dprobs[h] - rowdots[h])).astype(BF).astype(F32) for h in each
                ]
            dscores = [(probs[h] * (dprobs[h] - rowdots[h])).astype(BF) for h in each]
            dqs_parts = [dot(dscores[h], ks[0:width, feat[h]]) for h in each]
            if own:
                dqs_parts = [dqs_parts[h] + own_dscores[h] * kn[rows, feat[h]].astype(F32) for h in each]
                dkn[rows, :] = jnp.concatenate([own_dscores[h] * query[h].astype(F32) for h in each], axis=1)
                dvn[rows, :] = jnp.concatenate([own_probs[h] * grad[h].astype(F32) for h in each], axis=1)
            dqs[rows, :] = jnp.concatenate(dqs_parts, axis=1) * HD**-0.5
            for h in each:
                dkt[feat[h], 0:width] += dot(qt[feat[h], rows], dscores[h])
                dvt[feat[h], 0:width] += dot(gt[feat[h], rows], probs[h].astype(BF))
            if causal:
                drel = jnp.zeros((TILE, TILE), F32)
                for h in each:
                    blocks = [
                        dot(dscores[h][:, TILE * b : TILE * (b + 1)], flip_ref[...])
                        for b in reversed(range(width // TILE))
                    ]
                    mirrored = jnp.concatenate(blocks, axis=1) if len(blocks) > 1 else blocks[0]
                    turned = pltpu.roll(mirrored, 0, 1, stride=1, stride_axis=0).astype(BF)
                    drel = drel + dot(turned, back_ref[table_slice(t, width), :]) * rel_mask(h)
                    if own:
                        drel = drel + own_dscores[h] * (hot_ref[...] * rel_mask(h))
                drs[rows, :] = drel
        store_rows(meta_ref, dq_ref, dqs, 0, width_all)
        dks[...] = dkt[...].T
        store_rows(meta_ref, dk_ref, dks, 0, width_all)
        dks[...] = dvt[...].T
        store_rows(meta_ref, dv_ref, dks, 0, width_all)
        if causal:
            store_rows(meta_ref, drel_ref, drs, 0, rel.shape[1])
        if own:
            store_rows(meta_ref, dkn_ref, dkn, 0, width_all)
            store_rows(meta_ref, dvn_ref, dvn, 0, width_all)

    args = [qkv, *attended, w_out, lse]
    shape = (total, width_all)
    turned = (width_all, total)
    outs = [(shape, BF), (shape, F32), (shape, F32), ((total, w_out.shape[1]), BF)]
    scratch = [pltpu.VMEM(shape, BF) for _ in range(4)] + [pltpu.VMEM(shape, F32) for _ in range(2)]
    scratch += [pltpu.VMEM(turned, BF) for _ in range(4)] + [pltpu.VMEM(turned, F32) for _ in range(2)]
    if own:
        args.append(main)
    if causal:
        args += [rel, *tables]
        outs.append(((total, rel.shape[1]), BF))
        scratch += [pltpu.VMEM((total, rel.shape[1]), F32) for _ in range(2)]
    if own:
        outs += [(shape, BF), (shape, BF)]
        scratch += [pltpu.VMEM(shape, BF) for _ in range(2)] + [pltpu.VMEM(shape, F32) for _ in range(2)]
    return chain(kernel, outs, args, scalars=[meta], scratch=scratch, after=after, room=12, cost=10 if causal else 6)


def rel_tables(rel_table, total):
    ahead, back = [], []
    for t in range(total // TILE):
        width = TILE * (t + 1)
        here = rel_table[:width]
        ahead += [jnp.flip(here[: TILE * t + 1]), jnp.flip(here[TILE * t + 1 :])]
        back += [here[width - TILE + 1 :], here[: width - TILE + 1]]
    ahead, back = jnp.concatenate(ahead), jnp.concatenate(back)
    rows = jnp.arange(2 * TILE, dtype=jnp.int32) % NB
    forward = (rows[:, None] == ahead[None, :]).astype(BF)
    backward = (back[:, None] == rows[None, :TILE]).astype(BF)
    hot = (rows[None, :TILE] == rel_table[0]).astype(F32)
    ids = jnp.arange(TILE, dtype=jnp.int32)
    flip = (ids[:, None] + ids[None, :] == TILE - 1).astype(BF)
    return forward, backward, hot, flip


def unit_of(values):
    center = values - jnp.mean(values, axis=-1, keepdims=True)
    spread = jnp.mean(center * center, axis=-1, keepdims=True)
    inverse = lax.rsqrt(spread + EPSILON)
    return center * inverse, inverse


def unit_back(grad, unit, inverse, gain):
    inner = grad * gain
    mean = jnp.mean(inner, axis=-1, keepdims=True)
    along = jnp.mean(inner * unit, axis=-1, keepdims=True)
    return inverse * (inner - mean - unit * along)


def column(values):
    return jnp.sum(values, axis=0, keepdims=True)


def tiny_sums(low, grad, unit):
    return jnp.concatenate([column(low.astype(F32)), column(grad * unit), column(grad)], axis=0)


def norm_first(chain, inputs, parts, w, after=()):
    rows, dim = inputs.shape

    def kernel(in_ref, own_ref, near_ref, far_ref, small_ref, unit_ref, inverse_ref, low_ref):
        values = in_ref[...].astype(F32) + scattered(own_ref, near_ref, far_ref) + small_ref[2:3, :]
        unit, inverse = unit_of(values)
        unit_ref[...] = unit
        inverse_ref[...] = inverse
        low_ref[...] = (unit * small_ref[4:5, :] + small_ref[6:7, :]).astype(BF)

    outs = [((rows, dim), F32), ((rows, 1), F32), ((rows, dim), BF)]
    return chain(kernel, outs, [inputs, *parts, w.small], after=after)


def norm_second(chain, unit0, parts, w, after=()):
    rows, dim = unit0.shape

    def kernel(unit_ref, own_ref, near_ref, far_ref, small_ref, unit1_ref, inverse_ref, out_ref, low_ref):
        hidden = unit_ref[...] * small_ref[4:5, :] + small_ref[6:7, :]
        unit, inverse = unit_of(hidden + scattered(own_ref, near_ref, far_ref) + small_ref[3:4, :])
        out = unit * small_ref[5:6, :] + small_ref[7:8, :]
        unit1_ref[...] = unit
        inverse_ref[...] = inverse
        out_ref[...] = out
        low_ref[...] = out.astype(BF)

    outs = [((rows, dim), F32), ((rows, 1), F32), ((rows, dim), F32), ((rows, dim), BF)]
    return chain(kernel, outs, [unit0, *parts, w.small], after=after)


def norm_second_back(chain, residual, parts, unit1, inverse, w, after=()):
    rows, dim = residual.shape

    def kernel(res_ref, own_ref, near_ref, far_ref, unit_ref, inverse_ref, small_ref, sum_ref, low_ref, tiny_ref):
        grad = res_ref[...] + scattered(own_ref, near_ref, far_ref)
        unit = unit_ref[...]
        back = unit_back(grad, unit, inverse_ref[...], small_ref[5:6, :])
        low = back.astype(BF)
        sum_ref[...] = back
        low_ref[...] = low
        tiny_ref[...] = tiny_sums(low, grad, unit)

    outs = [((rows, dim), F32), ((rows, dim), BF), ((3, dim), F32)]
    return chain(kernel, outs, [residual, *parts, unit1, inverse, w.small], after=after)


def norm_second_both(chain, unit0, parts, cotangent, w, after=()):
    rows, dim = unit0.shape

    def kernel(unit_ref, own_ref, near_ref, far_ref, cot_ref, small_ref, out_ref, sum_ref, low_ref, tiny_ref):
        hidden = unit_ref[...] * small_ref[4:5, :] + small_ref[6:7, :]
        unit, inverse = unit_of(hidden + scattered(own_ref, near_ref, far_ref) + small_ref[3:4, :])
        out_ref[...] = unit * small_ref[5:6, :] + small_ref[7:8, :]
        grad = cot_ref[...].astype(F32)
        back = unit_back(grad, unit, inverse, small_ref[5:6, :])
        low = back.astype(BF)
        sum_ref[...] = back
        low_ref[...] = low
        tiny_ref[...] = tiny_sums(low, grad, unit)

    outs = [((rows, dim), F32), ((rows, dim), F32), ((rows, dim), BF), ((3, dim), F32)]
    return chain(kernel, outs, [unit0, *parts, cotangent, w.small], after=after)


def norm_first_back(chain, sum_grad, parts, unit0, inverse, w, after=()):
    rows, dim = sum_grad.shape

    def kernel(sum_ref, own_ref, near_ref, far_ref, unit_ref, inverse_ref, small_ref, out_ref, low_ref, tiny_ref):
        grad = sum_ref[...] + scattered(own_ref, near_ref, far_ref)
        unit = unit_ref[...]
        back = unit_back(grad, unit, inverse_ref[...], small_ref[4:5, :])
        low = back.astype(BF)
        out_ref[...] = back
        low_ref[...] = low
        tiny_ref[...] = tiny_sums(low, grad, unit)

    outs = [((rows, dim), F32), ((rows, dim), BF), ((3, dim), F32)]
    return chain(kernel, outs, [sum_grad, *parts, unit0, inverse, w.small], after=after)


def input_gradient(chain, residual, parts, after=()):
    rows, dim = residual.shape

    def kernel(res_ref, own_ref, near_ref, far_ref, out_ref):
        out_ref[...] = res_ref[...] + scattered(own_ref, near_ref, far_ref)

    return chain(kernel, [((rows, dim), F32)], [residual, *parts], after=after)[0]


def project(chain, quads, w, with_rel, after=()):
    rows, dim = quads[0].shape
    width = w.qkv.shape[1]

    def kernel(*refs):
        refs = list(refs)
        quad_refs = [refs.pop(0) for _ in range(STREAMS)]
        qkv_ref, bias_ref = refs.pop(0), refs.pop(0)
        rel_ref, rel_bias_ref = (refs.pop(0), refs.pop(0)) if with_rel else (None, None)
        joined_ref, heads_ref = refs.pop(0), refs.pop(0)
        join(joined_ref, quad_refs)
        heads_ref[...] = (dot(joined_ref[...], qkv_ref[...]) + bias_ref[...]).astype(BF)
        if with_rel:
            refs[0][...] = dot(joined_ref[...], rel_ref[...]) + rel_bias_ref[...]

    args = [*quads, w.qkv, w.qkv_bias]
    outs = [((STREAMS * rows, dim), BF), ((STREAMS * rows, width), BF)]
    if with_rel:
        args += [w.rel, w.rel_bias]
        outs.append(((STREAMS * rows, w.rel.shape[1]), F32))
    return chain(kernel, outs, args, after=after)


def out_project(chain, context, w, after=()):
    total, _ = context.shape
    block = total // STREAMS

    def kernel(context_ref, out_ref, *parts_refs):
        for part in range(2):
            value = dot(context_ref[part * 2 * block : (part + 1) * 2 * block, :], out_ref[...])
            store_partials(part, value, *parts_refs)

    return chain(kernel, scatter_outs(block, w.out.shape[1]), [context, w.out], after=after)


def project_back(chain, dq, dk, dv, drel, w, after=()):
    total, width = dq.shape
    block = total // STREAMS
    dim = w.qkv.shape[0]
    with_rel = drel is not None
    keys, vals = len(dk), len(dv)

    def kernel(*refs):
        refs = list(refs)
        dq_ref = refs.pop(0)
        dk_refs = [refs.pop(0) for _ in range(keys)]
        dv_refs = [refs.pop(0) for _ in range(vals)]
        drel_ref = refs.pop(0) if with_rel else None
        qkv_ref = refs.pop(0)
        rel_ref = refs.pop(0) if with_rel else None
        parts_refs = [refs.pop(0) for _ in range(3)]
        heads_ref, sums_ref = refs.pop(0), refs.pop(0)
        heads_ref[:, :width] = dq_ref[...]
        heads_ref[:, width : 2 * width] = sum(r[...] for r in dk_refs).astype(BF)
        heads_ref[:, 2 * width :] = sum(r[...] for r in dv_refs).astype(BF)
        sums_ref[...] = column(heads_ref[...].astype(F32))
        if with_rel:
            refs[0][...] = column(drel_ref[...].astype(F32))
        for part in range(2):
            rows = slice(part * 2 * block, (part + 1) * 2 * block)
            value = dot_nt(heads_ref[rows, :], qkv_ref[...])
            if with_rel:
                value = value + dot_nt(drel_ref[rows, :], rel_ref[...])
            store_partials(part, value, *parts_refs)

    args = [dq, *dk, *dv]
    outs = scatter_outs(block, dim) + [((total, 3 * width), BF), ((1, 3 * width), F32)]
    if with_rel:
        args += [drel, w.qkv, w.rel]
        outs.append(((1, w.rel.shape[1]), F32))
    else:
        args.append(w.qkv)
    return chain(kernel, outs, args, after=after)


def gelu_and_slope(x):
    bell = jnp.exp(-0.5 * x * x)
    under = 1.0 + (0.3275911 * 0.5**0.5) * jnp.abs(x)
    t = pl.reciprocal(under, approx=True)
    t = t * (2.0 - under * t)
    series = ((((1.061405429 * t - 1.453152027) * t + 1.421413741) * t - 0.284496736) * t + 0.254829592) * t
    tail = (0.5 * series) * bell
    below = jnp.where(x >= 0.0, 1.0 - tail, tail)
    return x * below, below + x * bell * 0.3989422804014327


FFN_TILE = 256


def ffn_in_tile(ref, share, first):
    tile = ref[:, :share, first : first + FFN_TILE]
    return tile.reshape(tile.shape[0] * share, FFN_TILE)


def ffn_out_rows(ref, share, first, last):
    part = ref.shape[1] - share
    tile = ref[first // part : last // part, share:, :]
    return tile.reshape(last - first, ref.shape[2])


def ffn_forward(chain, quads, w, after=()):
    rows, dim = quads[0].shape
    n, both, units = w.ffn.shape
    share = dim // n
    half = 2 * rows

    def kernel(a_ref, b_ref, c_ref, d_ref, w_ref, bias_ref, own_ref, across_ref, near_ref, joined_ref, act_ref, slope_ref):
        join(joined_ref, (a_ref, b_ref, c_ref, d_ref))
        for part in range(2):
            block = slice(part * half, (part + 1) * half)
            for u in range(0, units, FFN_TILE):
                tile = slice(u, u + FFN_TILE)
                inner = dot(joined_ref[block, :], ffn_in_tile(w_ref, share, u)) + bias_ref[:, tile]
                active, slope = gelu_and_slope(inner)
                act_ref[block, tile] = active.astype(BF)
                slope_ref[block, tile] = slope.astype(BF)
            branch = dot(act_ref[block, :], ffn_out_rows(w_ref, share, 0, units))
            store_partials(part, branch, own_ref, across_ref, near_ref)

    wide = ((4 * rows, units), BF)
    outs = scatter_outs(rows, dim) + [((4 * rows, dim), BF), wide, wide]
    return chain(kernel, outs, [*quads, w.ffn, w.ffn_bias], after=after, cost=5)


def ffn_backward(chain, quads, slope, w, after=()):
    rows, dim = quads[0].shape
    n, both, units = w.ffn.shape
    share = dim // n
    half = 2 * rows

    def kernel(a_ref, b_ref, c_ref, d_ref, w_ref, slope_ref, own_ref, across_ref, near_ref, joined_ref, inner_ref, sums_ref):
        join(joined_ref, (a_ref, b_ref, c_ref, d_ref))
        for part in range(2):
            block = slice(part * half, (part + 1) * half)
            for u in range(0, units, FFN_TILE):
                tile = slice(u, u + FFN_TILE)
                back = dot_nt(joined_ref[block, :], ffn_out_rows(w_ref, share, u, u + FFN_TILE))
                inner = (back * slope_ref[block, tile].astype(F32)).astype(BF)
                inner_ref[block, tile] = inner
                if part == 0:
                    sums_ref[:, tile] = column(inner.astype(F32))
                else:
                    sums_ref[:, tile] += column(inner.astype(F32))
            hidden = sum(
                dot_nt(inner_ref[block, u : u + FFN_TILE], ffn_in_tile(w_ref, share, u))
                for u in range(0, units, FFN_TILE)
            )
            store_partials(part, hidden, own_ref, across_ref, near_ref)

    outs = scatter_outs(rows, dim) + [((4 * rows, dim), BF), ((4 * rows, units), BF), ((1, units), F32)]
    return chain(kernel, outs, [*quads, w.ffn, slope], after=after, cost=4)


def copy_all(moves, sems):
    copies = [pltpu.make_async_copy(source, target, sems.at[i]) for i, (source, target) in enumerate(moves)]
    for copy in copies:
        copy.start()
    for copy in copies:
        copy.wait()


def pack_attention(chain, devices, qkv, out, smalls=None, rel=None, after=()):
    share, dim = out.shape
    quarter = dim // STREAMS
    fixed = 4 * share
    half = share // 2
    more = 16 if rel is None else half
    extra = list(smalls) if rel is None else [rel]

    def kernel(devices_ref, qkv_ref, out_ref, *refs):
        sources, packed_ref, targets, sems = refs[: len(extra)], refs[len(extra)], refs[len(extra) + 1 : -1], refs[-1]
        columns = pl.ds(pl.multiple_of(devices_ref[0] * quarter, quarter), quarter)
        moves = [(qkv_ref.at[i, :, columns], packed_ref.at[i * share : (i + 1) * share, :]) for i in range(3)]
        moves.append((out_ref.at[:, columns], packed_ref.at[3 * share : fixed, :]))
        if rel is None:
            moves += list(zip(sources, targets))
        else:
            part = rel.shape[1] // STREAMS
            columns = pl.ds(pl.multiple_of(devices_ref[0] * part, part), part)
            for i in range(2):
                moves.append(
                    (
                        sources[0].at[i * half : (i + 1) * half, columns],
                        packed_ref.at[fixed:, i * part : (i + 1) * part],
                    )
                )
        copy_all(moves, sems)
        if rel is None:
            lines = []
            ffn_share = STREAMS * share
            last = targets[0][:, 2 * ffn_share :].astype(F32)
            last = jnp.concatenate([last, jnp.zeros((1, share - last.shape[1]), F32)], axis=1)
            for layer in range(2):
                bias_ref, gain_ref, shift_ref = targets[3 * layer + 1 : 3 * layer + 4]
                left = jnp.concatenate([r[...].astype(F32) for r in (bias_ref, gain_ref, shift_ref)], axis=0)
                first = layer * ffn_share
                right = [
                    targets[0][:, first + i * share : first + (i + 1) * share].astype(F32) for i in range(STREAMS)
                ]
                right += [last, jnp.zeros((3, share), F32)]
                lines.append(jnp.concatenate([left, jnp.concatenate(right, axis=0)], axis=1))
            lines = jnp.concatenate(lines, axis=0)
            packed_ref[fixed:, : 2 * share] = lines.astype(BF)
            if 2 * share < quarter:
                packed_ref[fixed:, 2 * share :] = jnp.zeros((more, quarter - 2 * share), BF)

    scratch = [pltpu.VMEM(a.shape, BF) for a in extra] if rel is None else []
    scratch.append(pltpu.SemaphoreType.DMA((4 + (len(extra) if rel is None else 2),)))
    outs = [((fixed + more, quarter), BF)]
    return chain(kernel, outs, [], scalars=[devices], stored=[qkv, out] + extra, scratch=scratch, after=after)[0]


def pack_ffn(chain, devices, here, matrix_in, matrix_out, n, after=()):
    share, ffn = matrix_in.shape
    ffn_share, dim = matrix_out.shape
    part = ffn_share // STREAMS
    if part % TILE:
        blocks = lax.dynamic_slice_in_dim(matrix_in.reshape(share, n, ffn_share), here * part, part, axis=2)
        rows = lax.dynamic_slice_in_dim(matrix_out, here * part, part, axis=0)
        return jnp.concatenate([blocks.reshape(share, n * part), rows], axis=0)

    def kernel(devices_ref, in_ref, out_ref, packed_ref, sems):
        first = devices_ref[0] * part
        moves = [(out_ref.at[pl.ds(pl.multiple_of(first, TILE), part), :], packed_ref.at[share:, :])]
        for g in range(n):
            columns = pl.ds(pl.multiple_of(g * ffn_share + first, TILE), part)
            moves.append((in_ref.at[:, columns], packed_ref.at[:share, g * part : (g + 1) * part]))
        copy_all(moves, sems)

    return chain(
        kernel,
        [((share + part, n * part), BF)],
        [],
        scalars=[devices],
        stored=[matrix_in, matrix_out],
        scratch=[pltpu.SemaphoreType.DMA((n + 1,))],
        after=after,
    )[0]


def place_ffn(chain, devices, here, blocks, share, n, after=()):
    rows, dim = blocks[0].shape
    part = rows - share
    ffn = n * part * STREAMS
    if part % TILE:
        stacked = jnp.stack([blocks[XOR.index(j)] for j in range(STREAMS)])
        ordered = [lax.dynamic_index_in_dim(stacked, here ^ a, 0, keepdims=False) for a in range(STREAMS)]
        grad_in = jnp.stack([b[:share].reshape(share, n, part) for b in ordered], axis=2)
        grad_out = jnp.concatenate([b[share:] for b in ordered], axis=0)
        return grad_in.reshape(share, ffn).astype(F32), grad_out.astype(F32)

    def kernel(devices_ref, *refs):
        in_ref, out_ref = refs[STREAMS:]
        for i in range(STREAMS):
            first = devices_ref[i] * part
            for g in range(n):
                columns = pl.ds(pl.multiple_of(g * part * STREAMS + first, TILE), part)
                in_ref[:, columns] = refs[i][:share, g * part : (g + 1) * part].astype(F32)
            out_ref[pl.ds(pl.multiple_of(first, TILE), part), :] = refs[i][share:, :].astype(F32)

    outs = [((share, ffn), F32), ((STREAMS * part, dim), F32)]
    return chain(kernel, outs, blocks, scalars=[devices], after=after, room=6)


def place_attention(chain, devices, blocks, share, ffn_part, rel_part, after=()):
    quarter = blocks[0].shape[1]
    dim = quarter * STREAMS
    fixed = 4 * share
    half = share // 2
    tiny = fixed + (half if rel_part else 0)
    tiny_rows = blocks[0].shape[0] - tiny

    def kernel(devices_ref, *refs):
        refs = list(refs)
        block_refs = [refs.pop(0) for _ in range(STREAMS)]
        qkv_ref, out_ref, bias_ref, gain_ref, shift_ref, inner_ref = refs[:6]
        total = jnp.zeros((tiny_rows, quarter), F32)
        for i, ref in enumerate(block_refs):
            columns = pl.ds(pl.multiple_of(devices_ref[i] * quarter, quarter), quarter)
            for k in range(3):
                qkv_ref[k, :, columns] = ref[k * share : (k + 1) * share, :].astype(F32)
            out_ref[:, columns] = ref[3 * share : fixed, :].astype(F32)
            if rel_part:
                columns = pl.ds(pl.multiple_of(devices_ref[i] * rel_part, rel_part), rel_part)
                refs[6][:half, columns] = ref[fixed : fixed + half, :rel_part].astype(F32)
                refs[6][half:, columns] = ref[fixed : fixed + half, rel_part:].astype(F32)
            mine = ref[tiny:, :].astype(F32)
            total = total + mine
            inner_ref[pl.ds(devices_ref[i], 1), :] = mine[0:1, share : share + ffn_part]
        bias_ref[...] = total[0:4, :share]
        gain_ref[...] = total[4:6, :share]
        shift_ref[...] = total[6:8, :share]
        if rel_part:
            refs[7][...] = total[1:2, share : 2 * share]

    outs = [
        ((3, share, dim), F32),
        ((share, dim), F32),
        ((4, share), F32),
        ((2, share), F32),
        ((2, share), F32),
        ((STREAMS, ffn_part), F32),
    ]
    if rel_part:
        outs += [((share, rel_part * STREAMS), F32), ((1, share), F32)]
    return chain(kernel, outs, blocks, scalars=[devices], after=after, room=6)


class Layer:
    pass


def own_columns(matrix, here):
    width = matrix.shape[-1] // STREAMS
    return lax.dynamic_slice_in_dim(matrix, here * width, width, axis=matrix.ndim - 1)


def per_device(
    enc_input, pred_input, cotangent, bucket_len, pad_len, rel_table,
    enc_qkv, enc_out, enc_ffn_in, enc_ffn_out, enc_ffn_bias, enc_bias, enc_gain, enc_shift,
    dec_qkv, dec_out, dec_rel, dec_rel_bias, dec_ffn_in, dec_ffn_out, dec_ffn_bias, dec_bias, dec_gain, dec_shift,
):
    chain = Chain()
    here = lax.axis_index("stream")
    n = lax.axis_size("dp")
    group = lax.axis_index("dp")
    place = ring_place(group, n)
    rows = enc_input.shape[0]
    total = STREAMS * rows
    dim = enc_input.shape[1]
    share = enc_out.shape[0]
    quarter = dim // STREAMS
    ffn_share = enc_ffn_out.shape[0]
    ffn_part = ffn_share // STREAMS
    rel_all = dec_rel.shape[1]
    rel_part = rel_all // STREAMS
    fixed = 4 * share
    half = share // 2

    bucket = bucket_len[0]
    starts = []
    for j in XOR:
        holder = here ^ j
        for chunk in range(2):
            starts.append(jnp.where(bucket == total, holder * rows + chunk * 64, chunk * bucket + holder * 64))
    meta = jnp.stack([v.astype(jnp.int32) for v in starts + [bucket, pad_len[0, 0], pad_len[0, 1]]])
    devices = jnp.stack([here ^ j for j in XOR]).astype(jnp.int32)
    ring_index = jnp.stack([ring_member(place - o, n) for o in range(n)]).astype(jnp.int32)
    tables = rel_tables(rel_table, total)

    vectors = jnp.concatenate([enc_ffn_bias, dec_ffn_bias, dec_rel_bias])[None]
    smalls = (vectors, enc_bias, enc_gain, enc_shift, dec_bias, dec_gain, dec_shift)
    small_rows = 16

    def attention_regions(extra):
        regions = [(i * share, (i + 1) * share, 0, quarter, 0, 0, i * quarter) for i in range(3)]
        regions.append((fixed - share, fixed, 0, quarter, 1, 0, 0))
        return regions + extra

    shapes = [(share, 3 * quarter), (share, quarter)]

    def gather_shares(packed):
        return lax.all_gather(packed, "dp", axis=0, tiled=False)

    enc_ffn = gather_shares(pack_ffn(chain, devices, here, enc_ffn_in, enc_ffn_out, n))
    enc_pieces = ring_pieces(pack_attention(chain, devices, enc_qkv, enc_out, smalls=smalls), n)
    enc_quads = gather_rows(enc_input)
    pred_quads = [gather_rows(pred_input[i]) for i in range(2)]
    dec_packed = gather_shares(pack_attention(chain, devices, dec_qkv, dec_out, rel=dec_rel))
    dec_ffn = gather_shares(pack_ffn(chain, devices, here, dec_ffn_in, dec_ffn_out, n))

    def turn_out_back(grad):
        sent = [lax.dynamic_slice_in_dim(grad, (here ^ j) * quarter, quarter, axis=1) for j in XOR]
        return jnp.concatenate(by_absolute(turn_blocks(sent), here), axis=0).reshape(n, share, quarter)

    enc_wqkv, enc_wout, small_all = assemble(
        chain,
        enc_pieces,
        ring_index,
        attention_regions([(fixed, fixed + small_rows, 0, quarter, 2, 0, 0)]),
        shapes + [(small_rows, quarter)],
        n,
        after=[quads[1] for quads in pred_quads],
    )

    small_all = small_all.astype(F32)

    def attention_layer(number, wqkv, wout):
        w = Layer()
        w.qkv = wqkv.reshape(dim, 3 * quarter)
        w.turn = Turn(chain, devices, wout.reshape(dim, quarter), True)
        block = small_all[:, 8 * number : 8 * number + 8]
        w.ffn_bias = lax.dynamic_slice_in_dim(block, here, 1, axis=1)[:, 0, share : 2 * share].reshape(1, -1)
        w.small = jnp.transpose(block[:, :, :share], (1, 0, 2)).reshape(8, dim)
        mine = own_columns(w.small, here)
        w.qkv_bias = jnp.concatenate([mine[0:1], jnp.zeros_like(mine[0:1]), mine[1:2]], axis=1)
        return w

    enc = attention_layer(0, enc_wqkv, enc_wout)
    enc_all, enc_heads = project(chain, enc_quads, enc, False)
    enc_context, enc_lse, _ = attention_forward(chain, meta, enc_heads)
    enc.out = enc.turn.join(chain)
    scatter = Scatter(out_project(chain, enc_context, enc))
    scatter.middle(chain)
    enc_unit0, enc_inverse0, low = norm_first(chain, enc_input, scatter.parts(), enc)
    quads = gather_rows(low)
    enc.ffn = enc_ffn
    *parts, enc_hidden, enc_active, enc_slope = ffn_forward(chain, quads, enc)
    scatter = Scatter(parts)
    scatter.middle(chain)
    enc_unit1, enc_inverse1, main_rows, main_low = norm_second(chain, enc_unit0, scatter.parts(), enc)
    main_quads = gather_rows(main_low)

    dec_wqkv, dec_wout, dec_wrel = unpack(
        chain,
        dec_packed,
        attention_regions(
            [
                (fixed, fixed + half, 0, rel_part, 2, 0, 0),
                (fixed, fixed + half, rel_part, 2 * rel_part, 2, half, 0),
            ]
        ),
        shapes + [(share, rel_part)],
    )
    dec = attention_layer(1, dec_wqkv, dec_wout)
    dec.rel = dec_wrel.reshape(dim, rel_part)
    dec.rel_bias = own_columns(small_all[:, 12, share : share + rel_all // n].reshape(1, -1), here)
    alls, heads, rels = [None] * 3, [None] * 3, [None] * 3
    stream_inputs = (main_rows, pred_input[0], pred_input[1])
    for i, quads in ((0, main_quads), (1, pred_quads[0]), (2, pred_quads[1])):
        alls[i], heads[i], rels[i] = project(chain, quads, dec, True)
    contexts, lses = [None] * 3, [None] * 3

    def attend(i, after=()):
        contexts[i], lses[i], parts = attention_forward(
            chain, meta, heads[i], heads[0] if i else None, rels[i], tables, dec.out if i else None, after
        )
        if i == 0:
            dec.out = dec.turn.join(chain)
            parts = out_project(chain, contexts[i], dec)
        return Scatter(parts)

    def staged(work, finish):
        scatters = []
        for i in range(3):
            scatters.append(work(i))
            if i:
                scatters[i - 1].middle(chain)
        results = [finish(0, scatters[0])]
        scatters[2].middle(chain)
        results += [finish(1, scatters[1]), finish(2, scatters[2])]
        return results

    firsts = staged(
        lambda i: attend(i),
        lambda i, scatter: norm_first(chain, stream_inputs[i], scatter.parts(), dec),
    )
    hidden_quads = [gather_rows(first[2]) for first in firsts]
    dec.ffn = dec_ffn
    kept = [None] * 3

    def feed(i):
        *parts, hidden, active, slope = ffn_forward(chain, hidden_quads[i], dec)
        kept[i] = (hidden, active, slope)
        return Scatter(parts)

    seconds = staged(
        feed, lambda i, scatter: norm_second_both(chain, firsts[i][0], scatter.parts(), cotangent[i], dec)
    )
    outputs = [second[0] for second in seconds]

    branch_quads = [gather_rows(second[2]) for second in seconds]
    branches = [None] * 3

    def feed_back(i):
        *parts, branch, inner, inner_sum = ffn_backward(chain, branch_quads[i], kept[i][2], dec)
        branches[i] = (branch, inner, inner_sum)
        return Scatter(parts)

    backs = staged(
        feed_back,
        lambda i, scatter: norm_first_back(
            chain, seconds[i][1], scatter.parts(), firsts[i][0], firsts[i][1], dec
        ),
    )
    attended_quads = [gather_rows(back[1]) for back in backs]

    def ffn_grads(pairs):
        grad_in = sum(dot_tn(hidden, inner) for hidden, _, inner, _ in pairs).astype(BF)
        grad_out = sum(dot_tn(active, branch) for _, active, _, branch in pairs).astype(BF)
        return grad_in.reshape(n, share, dim), grad_out.reshape(n, ffn_part, dim)

    def ffn_sum(pairs):
        regions = [(0, 0, 0, share), (1, 0, share, ffn_part)]
        return RingSum(chain, list(ffn_grads(pairs)), regions, dim, n, ring_index)

    def advance(ring, stage):
        result = None
        while ring.done < stage * (n // 2 + 1) // 5:
            result = ring.step()
            ring.done += 1
        return result

    dec_ffn_total = lax.psum_scatter(
        jnp.concatenate(
            ffn_grads([(kept[i][0], kept[i][1], branches[i][1], branches[i][0]) for i in range(3)]), axis=1
        ),
        "dp",
        scatter_dimension=0,
        tiled=False,
    )
    results = [None] * 3
    for i in (1, 2, 0):
        results[i] = attention_backward(
            chain, meta, heads[i], attended_quads[i], dec.out, lses[i], None if i == 0 else heads[0], rels[i], tables
        )
    dheads, head_sums, rel_sums = [None] * 3, [None] * 3, [None] * 3

    def back_project(i):
        dq, dk, dv, _, drel = results[i][:5]
        keys = [r[1] for r in results] if i == 0 else [results[i][5]]
        vals = [r[2] for r in results] if i == 0 else [results[i][6]]
        *parts, dheads[i], head_sums[i], rel_sums[i] = project_back(chain, dq, keys, vals, drel, dec)
        return Scatter(parts)

    main_scatter = back_project(0)
    pred_scatters = [back_project(1)]
    main_scatter.middle(chain)
    pred_scatters.append(back_project(2))
    pred_scatters[0].middle(chain)

    def widen(part, size):
        return lax.dynamic_update_slice(jnp.zeros((1, size), F32), part, (0, here * part.shape[1]))

    def small_pack(inner_sum, tiny0, tiny1, heads_sum, rel_sum=None):
        wide = jnp.concatenate(
            [
                widen(heads_sum[:, :quarter], dim),
                widen(heads_sum[:, 2 * quarter :], dim),
                tiny0[0:1],
                tiny1[0:1],
                tiny0[1:2],
                tiny1[1:2],
                tiny0[2:3],
                tiny1[2:3],
            ],
            axis=0,
        )
        left = jnp.transpose(wide.reshape(8, n, share), (1, 0, 2))
        spare = quarter - share
        lines = [jnp.pad(inner_sum.reshape(n, 1, ffn_part), ((0, 0), (0, 0), (0, spare - ffn_part)))]
        if rel_sum is not None:
            line = widen(rel_sum, rel_all).reshape(n, 1, rel_all // n)
            lines.append(jnp.pad(line, ((0, 0), (0, 0), (0, spare - rel_all // n))))
        lines.append(jnp.zeros((n, 8 - len(lines), spare), F32))
        packed = jnp.concatenate([left, jnp.concatenate(lines, axis=1)], axis=2)
        return jnp.pad(packed, ((0, 0), (0, 8), (0, 0))).astype(BF)

    def attention_grads(qkv_grad, out_grad, more):
        return [qkv_grad.astype(BF).reshape(n, share, 3 * quarter), turn_out_back(out_grad.astype(BF))] + more

    def attention_ring(*grads):
        arrays = attention_grads(*grads)
        regions = [(0, i * quarter, i * share, share) for i in range(3)] + [(1, 0, 3 * share, share)]
        at = fixed
        for which, array in enumerate(arrays[2:]):
            regions.append((2 + which, 0, at, array.shape[1]))
            at += array.shape[1]
        return RingSum(chain, arrays, regions, quarter, n, ring_index)

    dec_out_part = sum(dot_tn(contexts[i], results[i][3]) for i in range(3))
    dec_qkv_part = sum(dot_tn(alls[i], dheads[i]) for i in range(3))
    rel_blocks = sum(dot_tn(alls[i], results[i][4]) for i in range(3)).astype(BF).reshape(n, share, rel_part)
    dec_small = small_pack(
        sum(branches[i][2] for i in range(3)),
        sum(backs[i][2] for i in range(3)),
        sum(seconds[i][3] for i in range(3)),
        sum(head_sums),
        sum(rel_sums),
    )
    wide, *others = attention_grads(
        dec_qkv_part,
        dec_out_part,
        [jnp.concatenate([rel_blocks[:, :half], rel_blocks[:, half:]], axis=2), dec_small],
    )
    thirds = [wide[:, :, i * quarter : (i + 1) * quarter] for i in range(3)]
    dec_total = lax.psum_scatter(
        jnp.concatenate(thirds + others, axis=1), "dp", scatter_dimension=0, tiled=False
    )

    enc_sum_grad, low, enc_tiny1 = norm_second_back(
        chain, backs[0][0], main_scatter.parts(), enc_unit1, enc_inverse1, enc
    )
    quads = gather_rows(low)
    pred_scatters[1].middle(chain)
    *parts, enc_branch, enc_inner, enc_inner_sum = ffn_backward(chain, quads, enc_slope, enc)
    scatter = Scatter(parts)
    pred_grads = [input_gradient(chain, backs[1][0], pred_scatters[0].parts())]
    scatter.middle(chain)
    enc_ffn_ring = ffn_sum([(enc_hidden, enc_active, enc_inner, enc_branch)])
    advance(enc_ffn_ring, 1)
    pred_grads.append(input_gradient(chain, backs[2][0], pred_scatters[1].parts()))
    residual, attended_low, enc_tiny0 = norm_first_back(
        chain, enc_sum_grad, scatter.parts(), enc_unit0, enc_inverse0, enc
    )
    quads = gather_rows(attended_low)
    dec_ffn_blocks = gather_rows(dec_ffn_total)
    advance(enc_ffn_ring, 2)
    enc_out_part = dot_tn(enc_context, jnp.concatenate(quads, axis=0))
    dq, dk, dv, _ = attention_backward(chain, meta, enc_heads, quads, enc.out, enc_lse)
    *parts, enc_dheads, enc_head_sum = project_back(chain, dq, [dk], [dv], None, enc)
    scatter = Scatter(parts)
    enc_ring = attention_ring(
        dot_tn(enc_all, enc_dheads),
        enc_out_part,
        [small_pack(enc_inner_sum, enc_tiny0, enc_tiny1, enc_head_sum)],
    )
    advance(enc_ring, 1)
    scatter.middle(chain)
    advance(enc_ffn_ring, 3)
    advance(enc_ring, 2)
    dec_in_grad, dec_back_grad = place_ffn(chain, devices, here, dec_ffn_blocks, share, n)
    enc_input_grad = input_gradient(chain, residual, scatter.parts())
    advance(enc_ffn_ring, 4)
    advance(enc_ring, 3)
    dec_blocks = gather_rows(dec_total)
    enc_ffn_blocks = gather_rows(advance(enc_ffn_ring, 5))
    advance(enc_ring, 4)
    dec_results = place_attention(chain, devices, dec_blocks, share, ffn_part, rel_part)
    enc_blocks = gather_rows(advance(enc_ring, 5))
    enc_in_grad, enc_back_grad = place_ffn(chain, devices, here, enc_ffn_blocks, share, n)
    enc_results = place_attention(chain, devices, enc_blocks, share, ffn_part, 0)

    def tiny_out(results):
        return results[5].reshape(-1), *results[2:5]

    return (
        jnp.stack(outputs),
        enc_input_grad,
        jnp.stack(pred_grads),
        enc_results[0],
        enc_results[1],
        enc_in_grad,
        enc_back_grad,
        *tiny_out(enc_results),
        dec_results[0],
        dec_results[1],
        dec_results[6],
        dec_results[7][0, : rel_all // n],
        dec_in_grad,
        dec_back_grad,
        *tiny_out(dec_results),
    )


def solution(mesh):
    tokens = P(("stream", "dp"), None)
    streams = P(None, ("stream", "dp"), None)
    first, second, cube = P("dp", None), P(None, "dp"), P(None, "dp", None)
    flat = P("dp")
    return jax.shard_map(
        per_device,
        mesh=mesh,
        in_specs=(
            tokens, streams, streams, flat, first, P(),
            cube, first, first, first, flat, second, second, second,
            cube, first, first, flat, first, first, flat, second, second, second,
        ),
        out_specs=(
            streams, tokens, streams,
            cube, first, first, first, flat, second, second, second,
            cube, first, first, flat, first, first, flat, second, second, second,
        ),
        check_vma=False,
    )
```
